32 devices in a mesh: fsdp: 4 (over y, core), ctx: 8 (over z, x).
Axes of the slice: x: 2, y: 2, z: 4, core: 2. Of those that a mesh axis runs over, the one named last changes fastest.
Arguments:
- hidden: bfloat16 [4, 1024, 2048], P('fsdp', 'ctx'), may hold values from -6 to 6
- queries: bfloat16 [4, 1024, 1024], P('fsdp', 'ctx'), may hold values from -6 to 6
- attn_out: bfloat16 [4, 1024, 1024], P('fsdp', 'ctx'), may hold values from -6 to 6
- grad_out: bfloat16 [4, 1024, 1024], P('fsdp', 'ctx'), may hold values from -6 to 6
- log_sums: float32 [4, 16, 1024], P('fsdp', None, 'ctx'), may hold values from 6 to 9
- block_order: int32 [4, 8], P('fsdp'), may hold values from 0 to 7, each once within a row
- w_kv: bfloat16 [2048, 512], P('fsdp'), may hold values from -0.125 to 0.125
Outputs:
- query_grads: bfloat16 [4, 1024, 1024], P('fsdp', 'ctx')
- input_grads: bfloat16 [4, 1024, 2048], P('fsdp', 'ctx')
- weight_grads: float32 [2048, 512], P(('fsdp', 'ctx'))
The draws below stay inside these ranges and needn't reach their ends.
Inputs may be any that keep to these rules, and one draw needn't show every extreme that they name: Each row of block_order is a permutation of the 8 block numbers.
All inputs are finite; a program needn't handle non-finite values.
Results may differ from the reference program's by a relative error of at most 0.013.
The reference program's roundings to bfloat16 on the way (of `key_vals`, `probs_low`, `score_grad` and `kv_grad`) count: a program that leaves them out, or rounds other values in their place, can miss the bound.
Values may be sent and summed in bfloat16 or wider, within the bound.
No kernel may reach another device: no remote copies, remote signals or barrier semaphores. Data moves between devices by JAX's collectives and lax.ppermute only.
A program may use at most 128 MiB of HBM per device.

```python
import jax
import jax.numpy as jnp
from jax import lax

D = 2048
Q_HEADS = 16
KV_HEADS = 4
HEAD_DIM = 64
TOK_DEV = 128
SEQS = 4
LENGTH = 1024
N_CTX = 8


def steps_of(own_key, extent, shards, least, largest):
    factor_of, own = 1.0, jax.random.fold_in(own_key, 6)
    for position, shards_of in shards:
        draws = jnp.exp(jax.random.uniform(jax.random.fold_in(own, position), (shards_of,), jnp.float32, least / len(shards), largest / len(shards)))
        factor_of = factor_of * jnp.repeat(draws, extent[position] // shards_of).reshape([-1 if axis == position else 1 for axis in range(len(extent))])
    return factor_of


def normal_values(key, dims, width, reach, pieces=(), kind=jnp.bfloat16):
    entries = jax.random.normal(key, dims, jnp.float32) * width
    if len(pieces) > 0:
        entries = steps_of(key, dims, pieces, -0.22, 0.18) * entries
    return jnp.clip(entries, min=-reach, max=reach).astype(kind)


def setup_inputs(seed: int = 0) -> dict:
    key_of = jax.random.split(jax.random.key(seed), 8)
    return {
        "hidden": normal_values(key_of[0], (SEQS, LENGTH, D), 1.0, 6.0, ((0, 4), (1, 8))),
        "queries": normal_values(key_of[1], (SEQS, LENGTH, Q_HEADS * HEAD_DIM), 1.0, 6.0, ((0, 4), (1, 8))),
        "attn_out": normal_values(key_of[2], (SEQS, LENGTH, Q_HEADS * HEAD_DIM), 1.0, 6.0, ((0, 4), (1, 8))),
        "grad_out": normal_values(key_of[3], (SEQS, LENGTH, Q_HEADS * HEAD_DIM), 1.0, 6.0, ((0, 4), (1, 8))),
        "log_sums": jnp.clip(6.0 + 3.0 * jax.random.uniform(key_of[4], (SEQS, Q_HEADS, LENGTH), jnp.float32) ** steps_of(key_of[4], (SEQS, Q_HEADS, LENGTH), ((0, 4), (2, 8)), -0.2, 0.2), 6.0, 9.0),
        "block_order": jax.vmap(lambda own: jax.random.permutation(own, N_CTX))(jax.random.split(key_of[5], SEQS)).reshape((SEQS, N_CTX)).astype(jnp.int32),
        "w_kv": normal_values(key_of[6], (D, 2 * KV_HEADS * HEAD_DIM), D ** -0.5, 0.125, ((0, 4),)),
    }


def reference(hidden, queries, attn_out, grad_out, log_sums, block_order, w_kv):
    groups = Q_HEADS // KV_HEADS
    score_scale = HEAD_DIM ** -0.5
    key_width = KV_HEADS * HEAD_DIM
    query_list = []
    input_list = []
    total_weight = jnp.zeros(w_kv.shape, jnp.float32)
    for seq_index in range(SEQS):
        positions = (block_order[seq_index][:, None].astype(jnp.int32) * TOK_DEV
                     + jnp.arange(TOK_DEV, dtype=jnp.int32)[None, :]).reshape(LENGTH)
        causal_mask = positions[None, :] <= positions[:, None]
        key_vals = jnp.dot(hidden[seq_index], w_kv, preferred_element_type=jnp.float32).astype(jnp.bfloat16)
        keys_all = key_vals[:, :key_width].astype(jnp.float32).reshape(LENGTH, KV_HEADS, HEAD_DIM)
        values_all = key_vals[:, key_width:].astype(jnp.float32).reshape(LENGTH, KV_HEADS, HEAD_DIM)
        keys_head = jnp.repeat(keys_all.transpose(1, 0, 2), groups, axis=0)
        values_head = jnp.repeat(values_all.transpose(1, 0, 2), groups, axis=0)
        query_head = queries[seq_index].astype(jnp.float32).reshape(LENGTH, Q_HEADS, HEAD_DIM).transpose(1, 0, 2)
        grad_head = grad_out[seq_index].astype(jnp.float32).reshape(LENGTH, Q_HEADS, HEAD_DIM).transpose(1, 0, 2)
        output_head = attn_out[seq_index].astype(jnp.float32).reshape(LENGTH, Q_HEADS, HEAD_DIM).transpose(1, 0, 2)

        def one_head(packed):
            query, key_mat, value, grad, output, lse_row = packed
            scores = jnp.dot(query, key_mat.T) * score_scale
            probs = jnp.where(causal_mask, jnp.exp(scores - lse_row[:, None]), jnp.float32(0.0))
            probs_low = lax.optimization_barrier(probs.astype(jnp.bfloat16)).astype(jnp.float32)
            value_grad = jnp.dot(probs_low.T, grad)
            prob_grad = jnp.dot(grad, value.T)
            row_delta = jnp.sum(grad * output, axis=1)
            score_grad = lax.optimization_barrier((probs * (prob_grad - row_delta[:, None])).astype(jnp.bfloat16)).astype(jnp.float32)
            return jnp.dot(score_grad, key_mat) * score_scale, jnp.dot(score_grad.T, query) * score_scale, value_grad

        dq_head, dk_head, dv_head = lax.map(one_head, (query_head, keys_head, values_head, grad_head,
                                                       output_head, log_sums[seq_index]))
        query_list.append(dq_head.transpose(1, 0, 2).reshape(LENGTH, Q_HEADS * HEAD_DIM).astype(jnp.bfloat16))
        key_grad = dk_head.reshape(KV_HEADS, groups, LENGTH, HEAD_DIM).sum(axis=1).transpose(1, 0, 2).reshape(LENGTH, key_width)
        value_grad = dv_head.reshape(KV_HEADS, groups, LENGTH, HEAD_DIM).sum(axis=1).transpose(1, 0, 2).reshape(LENGTH, key_width)
        kv_grad = jnp.concatenate([key_grad, value_grad], axis=1).astype(jnp.bfloat16)
        input_list.append(jnp.dot(kv_grad, w_kv.T, preferred_element_type=jnp.float32).astype(jnp.bfloat16))
        total_weight = total_weight + jnp.dot(hidden[seq_index].T, kv_grad, preferred_element_type=jnp.float32)
    return jnp.stack(query_list), jnp.stack(input_list), total_weight
```

```python
import functools

import jax
import jax.numpy as jnp
from jax import lax
from jax.experimental import pallas as pl
from jax.experimental.pallas import tpu as pltpu
from jax.sharding import PartitionSpec as P

Q_HEADS = 16
KV_HEADS = 4
HEAD_DIM = 64
GROUPS = Q_HEADS // KV_HEADS
KEY_WIDTH = KV_HEADS * HEAD_DIM
PAIR = 2 * HEAD_DIM
TEAM = Q_HEADS // 2
SCALE = HEAD_DIM ** -0.5
LOWER = HEAD_DIM

NT = (((1,), (1,)), ((), ()))
TN = (((0,), (0,)), ((), ()))
VMEM = pl.BlockSpec(memory_space=pltpu.VMEM)
SMEM = pl.BlockSpec(memory_space=pltpu.SMEM)
PARAMS = pltpu.CompilerParams(vmem_limit_bytes=40 * 1024 * 1024)


def matmul(left, right, dims=(((1,), (0,)), ((), ()))):
    return lax.dot_general(left, right, dims, preferred_element_type=jnp.float32)


def swapped(array, axis, bits):
    size = lax.axis_size(axis)
    return lax.ppermute(array, axis, [(i, i ^ bits) for i in range(size)])


def member():
    return lax.rem(lax.axis_index("ctx"), TEAM)


def call(kernel, out_shape, scratch, args, smem=0):
    return pl.pallas_call(
        kernel,
        out_shape=out_shape,
        in_specs=[SMEM] * smem + [VMEM] * (len(args) - smem),
        out_specs=[VMEM] * len(out_shape),
        scratch_shapes=scratch,
        compiler_params=PARAMS,
    )(*args)


def sds(shape, dtype=jnp.bfloat16):
    return jax.ShapeDtypeStruct(shape, dtype)


def pieces_kernel(fsdp, q_ref, go_ref, ao_ref, hid_ref, lse_ref, *rest):
    qd_refs, hid_refs, (stat, hid_parts) = rest[:TEAM], rest[TEAM:2 * TEAM], rest[2 * TEAM:]
    me = member()
    rows, width = q_ref.shape
    product = go_ref[...].astype(jnp.float32) * ao_ref[...].astype(jnp.float32)
    high = product.astype(jnp.bfloat16)
    low = (product - high.astype(jnp.float32)).astype(jnp.bfloat16)
    head_of = lax.broadcasted_iota(jnp.int32, (Q_HEADS, width), 1) // HEAD_DIM
    ones = (head_of == lax.broadcasted_iota(jnp.int32, (Q_HEADS, width), 0)).astype(jnp.bfloat16)
    delta = matmul(ones, high, NT) + matmul(ones, low, NT)
    for team in range(TEAM):
        stat[team, 0:2, :] = lse_ref[2 * team:2 * team + 2, :]
        stat[team, 2:4, :] = delta[2 * team:2 * team + 2, :]
        stat[team, 4:8, :] = jnp.zeros((4, rows), jnp.float32)
    model = hid_ref.shape[1]
    span, piece = model // fsdp, model // fsdp // TEAM
    for team in range(TEAM):
        parts = [hid_ref[:, f * span + team * piece:f * span + (team + 1) * piece] for f in range(fsdp)]
        hid_parts[team] = jnp.concatenate(parts, axis=1)
    for k in range(TEAM):
        to = jnp.bitwise_xor(me, k)
        columns = pl.ds(pl.multiple_of(to * PAIR, PAIR), PAIR)
        qd_refs[k][0:rows, 0:PAIR] = q_ref[:, columns]
        qd_refs[k][0:rows, PAIR:] = go_ref[:, columns]
        exact = stat[to]
        first = exact.astype(jnp.bfloat16).astype(jnp.float32)
        second = (exact - first).astype(jnp.bfloat16).astype(jnp.float32)
        third = exact - first - second
        qd_refs[k][rows:, 0:PAIR] = jnp.concatenate([first, third], axis=0).astype(jnp.bfloat16)
        qd_refs[k][rows:, PAIR:] = jnp.concatenate([second, jnp.zeros_like(second)], axis=0).astype(jnp.bfloat16)
        hid_refs[k][...] = hid_parts[to]


def project_kernel(fsdp, hid_ref, *rest):
    w_refs, out_refs, (parts,) = rest[:fsdp], rest[fsdp:fsdp + KV_HEADS], rest[fsdp + KV_HEADS:]
    mine = lax.axis_index("fsdp")
    span = w_refs[0].shape[0]
    total = None
    for m in range(fsdp):
        start = pl.multiple_of(jnp.bitwise_xor(mine, m) * span, span)
        term = matmul(hid_ref[:, pl.ds(start, span)], w_refs[m][...])
        total = term if total is None else total + term
    low = total.astype(jnp.bfloat16)
    for g in range(KV_HEADS):
        key = low[:, g * HEAD_DIM:(g + 1) * HEAD_DIM]
        value = low[:, KEY_WIDTH + g * HEAD_DIM:KEY_WIDTH + (g + 1) * HEAD_DIM]
        parts[g] = jnp.concatenate([key, value], axis=1)
    own = member() // 2
    for m in range(KV_HEADS):
        out_refs[m][...] = parts[jnp.bitwise_xor(own, m)]


def lower_half(shape):
    return lax.broadcasted_iota(jnp.int32, shape, len(shape) - 1) < LOWER


def stacked(key_value):
    wide = key_value.astype(jnp.float32)
    turned = pltpu.roll(wide, LOWER, 1)
    lower = lower_half(wide.shape)
    zero = jnp.zeros_like(wide)
    keys = jnp.concatenate([jnp.where(lower, wide, zero), jnp.where(lower, zero, turned)], axis=0) * SCALE
    values = jnp.concatenate([jnp.where(lower, turned, zero), jnp.where(lower, zero, wide)], axis=0)
    return keys.astype(jnp.bfloat16), values.astype(jnp.bfloat16)


def both_heads(stats, first):
    lines = [jnp.concatenate([one[first + head:first + head + 1, :] for one in stats], axis=1) for head in range(2)]
    return lines


def tile(keys, values, query, grad, stats, mask):
    size = keys.shape[0] // 2
    lse, delta = both_heads(stats, 0), both_heads(stats, 2)
    scores = matmul(keys, query, NT)
    prob_grad = matmul(values, grad, NT)
    lows, grads = [], []
    for head in range(2):
        part = slice(head * size, (head + 1) * size)
        probs = jnp.exp(scores[part] - lse[head])
        if mask is not None:
            probs = jnp.where(mask, probs, 0.0)
        lows.append(probs.astype(jnp.bfloat16))
        grads.append((probs * (prob_grad[part] - delta[head])).astype(jnp.bfloat16))
    low, score_grad = jnp.concatenate(lows, axis=0), jnp.concatenate(grads, axis=0)
    return matmul(score_grad, query), matmul(low, grad), matmul(score_grad, keys, TN)


def folded(key_sum, value_sum):
    size = key_sum.shape[0] // 2
    lower = lower_half((size, PAIR))
    straight = jnp.where(lower, key_sum[:size], value_sum[size:])
    crossed = jnp.where(lower, value_sum[:size], key_sum[size:])
    return (straight + pltpu.roll(crossed, LOWER, 1)) * jnp.where(lower, SCALE, 1.0)


def unpacked(qd_ref, rows):
    exact = qd_ref[rows:, :].astype(jnp.float32)
    return exact[0:8, 0:PAIR] + exact[0:8, PAIR:] + exact[8:16, 0:PAIR]


def sequence_kernel(order_ref, *rest):
    qd_refs, kv_refs, rest = rest[:TEAM], rest[TEAM:2 * TEAM], rest[2 * TEAM:]
    dq_refs, keep_ref, send_ref, rest = rest[:TEAM], rest[TEAM], rest[TEAM + 1], rest[TEAM + 2:]
    q_all, go_all, stat_all, key_all, value_all, dq_all, dkv_all = rest
    me = member()
    rows = kv_refs[0].shape[0]
    for k in range(TEAM):
        place = order_ref[0, jnp.bitwise_xor(me, k)]
        q_all[place] = qd_refs[k][0:rows, 0:PAIR]
        go_all[place] = qd_refs[k][0:rows, PAIR:]
        stat_all[place] = unpacked(qd_refs[k], rows)
        key_all[place], value_all[place] = stacked(kv_refs[k][...])
    written = [False] * TEAM
    for block in range(TEAM):
        key_sum = value_sum = None
        first = block
        while first < TEAM:
            count = 2 - first % 2
            query = q_all[first:first + count].reshape(count * rows, PAIR)
            grad = go_all[first:first + count].reshape(count * rows, PAIR)
            mask = None
            if first == block:
                shape = (rows, count * rows)
                mask = lax.broadcasted_iota(jnp.int32, shape, 0) <= lax.broadcasted_iota(jnp.int32, shape, 1)
            key_part, value_part, query_part = tile(
                key_all[block], value_all[block], query, grad, [stat_all[first + i] for i in range(count)], mask)
            key_sum = key_part if key_sum is None else key_sum + key_part
            value_sum = value_part if value_sum is None else value_sum + value_part
            for i in range(count):
                piece = query_part[i * rows:(i + 1) * rows]
                at = first + i
                dq_all[at] = dq_all[at] + piece if written[at] else piece
                written[at] = True
            first += count
        dkv_all[block] = folded(key_sum, value_sum)
    for k in range(TEAM):
        dq_refs[k][...] = dq_all[order_ref[0, jnp.bitwise_xor(me, k)]].astype(jnp.bfloat16)
    half = TEAM // 2
    side = lax.rem(me, 2)
    for i in range(half):
        keep_ref[i] = dkv_all[side * half + i]
        send_ref[i] = dkv_all[(1 - side) * half + i]


def teams_kernel(order_ref, qd_ref, kv_ref, dq_ref, dkv_ref, dq_all):
    me = member()
    rows = kv_ref.shape[1]
    base = lax.axis_index("ctx") - me
    dq_all[...] = jnp.zeros_like(dq_all)

    @pl.loop(0, kv_ref.shape[0])
    def _(block):
        keys, values = stacked(kv_ref[block])
        dkv_ref[block] = jnp.zeros((rows, PAIR), jnp.float32)
        place = order_ref[0, (block // TEAM) * TEAM + jnp.bitwise_xor(me, lax.rem(block, TEAM))]

        @pl.loop(0, TEAM)
        def _(at):
            own = order_ref[0, base + jnp.bitwise_xor(me, at)]

            @pl.when(place <= own)
            def _():
                shape = (rows, rows)
                mask = (place * rows + lax.broadcasted_iota(jnp.int32, shape, 0)
                        <= own * rows + lax.broadcasted_iota(jnp.int32, shape, 1))
                one = qd_ref.at[at]
                key_part, value_part, query_part = tile(
                    keys, values, one[0:rows, 0:PAIR], one[0:rows, PAIR:], [unpacked(one, rows)], mask)
                dq_all[at] += query_part
                dkv_ref[block] += folded(key_part, value_part)

    dq_ref[...] = dq_all[...].astype(jnp.bfloat16)


def sum_kernel(keep_ref, got_ref, out_ref):
    out_ref[...] = (keep_ref[...] + got_ref[...]).astype(jnp.bfloat16)


def weight_kernel(fsdp, slot_ref, *rest):
    hid_refs, grad_refs, rest = rest[:TEAM], rest[TEAM:2 * TEAM], rest[2 * TEAM:]
    out_refs, own_ref, (hid_all, grad_all, sums) = rest[:fsdp], rest[fsdp], rest[fsdp + 1:]
    me = member()
    mine = lax.axis_index("fsdp")
    rows = hid_refs[0].shape[0]
    half = TEAM // 2 * rows
    for k in range(TEAM):
        source = jnp.bitwise_xor(me, k)
        place = slot_ref[0, source]
        hid_all[pl.ds(pl.multiple_of(place * rows, rows), rows), :] = hid_refs[k][...]
        at = pl.ds(pl.multiple_of(lax.rem(source, 2) * half, half), half)
        columns = pl.ds(pl.multiple_of(source // 2 * PAIR, PAIR), PAIR)
        grad_all[at, columns] = grad_refs[k][...].reshape(half, PAIR)
    sums[...] = matmul(hid_all[...], grad_all[...], TN)
    part = out_refs[0].shape[0]
    for m in range(fsdp):
        start = pl.multiple_of(jnp.bitwise_xor(mine, m) * part, part)
        out_refs[m][...] = sums[pl.ds(start, part), :]
    own = grad_all[pl.ds(pl.multiple_of(slot_ref[0, me] * rows, rows), rows), :]
    own_ref[...] = standard(own)


def standard(columns):
    keys = [columns[:, g * PAIR:g * PAIR + HEAD_DIM] for g in range(KV_HEADS)]
    values = [columns[:, g * PAIR + HEAD_DIM:(g + 1) * PAIR] for g in range(KV_HEADS)]
    return jnp.concatenate(keys + values, axis=1)


def input_kernel(fsdp, grad_ref, *rest):
    w_refs, out_ref = rest[:fsdp], rest[fsdp]
    mine = lax.axis_index("fsdp")
    span = w_refs[0].shape[0]
    for m in range(fsdp):
        start = pl.multiple_of(jnp.bitwise_xor(mine, m) * span, span)
        out_ref[:, pl.ds(start, span)] = matmul(grad_ref[...], w_refs[m][...], NT).astype(jnp.bfloat16)


def query_kernel(*rest):
    dq_refs, out_ref = rest[:TEAM], rest[TEAM]
    me = member()
    for k in range(TEAM):
        columns = pl.ds(pl.multiple_of(jnp.bitwise_xor(me, k) * PAIR, PAIR), PAIR)
        out_ref[:, columns] = dq_refs[k][...]


def total_kernel(*rest):
    part_refs, out_ref = rest[:-1], rest[-1]
    total = part_refs[0][...]
    for ref in part_refs[1:]:
        total = total + ref[...]
    out_ref[...] = standard(total)


def shards(hidden, queries, attn_out, grad_out, log_sums, block_order, w_kv):
    rows, model = hidden.shape[1:]
    fsdp, devices = lax.axis_size("fsdp"), lax.axis_size("ctx")
    teams = devices // TEAM
    half = TEAM // 2
    f32 = jnp.float32
    span = model // fsdp
    width = span // TEAM * fsdp
    inputs = hidden[0]

    across = fsdp // 2
    w_parts = [w_kv] * fsdp
    w_parts[across] = swapped(w_kv, "fsdp", across)
    bits = 1
    while bits < across:
        for m in range(bits):
            for base in (0, across):
                w_parts[base + bits + m] = swapped(w_parts[base + m], "fsdp", bits)
        bits *= 2

    sent = call(
        functools.partial(pieces_kernel, fsdp),
        [sds((rows + 16, 2 * PAIR))] * TEAM + [sds((rows, width))] * TEAM,
        [pltpu.VMEM((TEAM, 8, rows), f32), pltpu.VMEM((TEAM, rows, width), jnp.bfloat16)],
        (queries[0], grad_out[0], attn_out[0], inputs, log_sums[0]))
    qd = [sent[0]] + [swapped(sent[k], "ctx", k) for k in range(1, TEAM)]

    kv_sent = call(
        functools.partial(project_kernel, fsdp),
        [sds((rows, PAIR))] * KV_HEADS,
        [pltpu.VMEM((KV_HEADS, rows, PAIR), jnp.bfloat16)],
        (inputs, *w_parts))
    kv = [kv_sent[0]] + [swapped(kv_sent[k // 2], "ctx", k) for k in range(1, TEAM)]
    hid = [sent[TEAM]] + [swapped(sent[TEAM + k], "ctx", k) for k in range(1, TEAM)]

    block = (rows, PAIR)
    if teams == 1:
        *dq, keep, give = call(
            sequence_kernel,
            [sds(block)] * TEAM + [sds((half,) + block, f32)] * 2,
            [pltpu.VMEM((TEAM,) + block, jnp.bfloat16)] * 2 + [pltpu.VMEM((TEAM, 8, rows), f32)]
            + [pltpu.VMEM((TEAM, 2 * rows, PAIR), jnp.bfloat16)] * 2 + [pltpu.VMEM((TEAM,) + block, f32)] * 2,
            (block_order, *qd, *kv), smem=1)
        slots = block_order
    else:
        me = member()
        alike = [[team * TEAM + one for team in range(teams)] for one in range(TEAM)]
        kv_all = lax.all_gather(jnp.stack(kv), "ctx", axis_index_groups=alike, axis=0, tiled=True)
        dq, dkv = call(
            teams_kernel,
            [sds((TEAM,) + block), sds((devices,) + block, f32)],
            [pltpu.VMEM((TEAM,) + block, f32)],
            (block_order, jnp.stack(qd), kv_all), smem=1)
        dkv = lax.psum_scatter(dkv, "ctx", axis_index_groups=alike, scatter_dimension=0, tiled=True)
        dkv = jnp.take(dkv, jnp.bitwise_xor(jnp.arange(TEAM, dtype=jnp.int32), me), axis=0)
        keep = lax.dynamic_slice_in_dim(dkv, me % 2 * half, half)
        give = lax.dynamic_slice_in_dim(dkv, (1 - me % 2) * half, half)
        dq = [dq[k] for k in range(TEAM)]
        slots = jnp.arange(TEAM, dtype=jnp.int32)[None]

    (kv_grad,) = call(sum_kernel, [sds((half,) + block)], [], (keep, swapped(give, "ctx", 1)))
    grads = [kv_grad] * TEAM
    for m in range(1, half):
        grads[2 * m] = swapped(kv_grad, "ctx", 2 * m)
    for m in range(half):
        grads[2 * m + 1] = swapped(grads[2 * m], "ctx", 1)

    *parts, own = call(
        functools.partial(weight_kernel, fsdp),
        [sds((width // fsdp, 2 * KEY_WIDTH), f32)] * fsdp + [sds((rows, 2 * KEY_WIDTH))],
        [pltpu.VMEM((TEAM * rows, width), jnp.bfloat16), pltpu.VMEM((TEAM * rows, 2 * KEY_WIDTH), jnp.bfloat16),
         pltpu.VMEM((width, 2 * KEY_WIDTH), f32)],
        (slots, *hid, *grads), smem=1)
    got = [parts[0]] + [swapped(parts[m], "fsdp", m) for m in range(1, fsdp)]
    dq = [dq[0]] + [swapped(dq[k], "ctx", k) for k in range(1, TEAM)]
    (input_grads,) = call(functools.partial(input_kernel, fsdp), [sds((rows, model))], [], (own, *w_parts))
    (query_grads,) = call(query_kernel, [sds((rows, Q_HEADS * HEAD_DIM))], [], dq)
    (weight_grads,) = call(total_kernel, [sds((width // fsdp, 2 * KEY_WIDTH), f32)], [], got)
    if teams > 1:
        weight_grads = lax.psum_scatter(
            weight_grads, "ctx", axis_index_groups=alike, scatter_dimension=0, tiled=True)
        weight_grads = lax.ppermute(
            weight_grads, "ctx", [(i, i % TEAM * teams + i // TEAM) for i in range(devices)])
    return query_grads[None], input_grads[None], weight_grads


def solution(mesh):
    return jax.shard_map(
        shards,
        mesh=mesh,
        in_specs=(
            P("fsdp", "ctx", None),
            P("fsdp", "ctx", None),
            P("fsdp", "ctx", None),
            P("fsdp", "ctx", None),
            P("fsdp", None, "ctx"),
            P("fsdp", None),
            P("fsdp", None),
        ),
        out_specs=(P("fsdp", "ctx", None), P("fsdp", "ctx", None), P(("fsdp", "ctx"), None)),
        check_vma=False,
    )
```

```python
import functools

import jax
import jax.numpy as jnp
from jax import lax
from jax.experimental import pallas as pl
from jax.experimental.pallas import tpu as pltpu
from jax.sharding import PartitionSpec as P

Q_HEADS = 16
KV_HEADS = 4
HEAD_DIM = 64
GROUPS = Q_HEADS // KV_HEADS
KEY_WIDTH = KV_HEADS * HEAD_DIM
PAIR = 2 * HEAD_DIM
TEAM = Q_HEADS // 2
SCALE = HEAD_DIM ** -0.5
LOWER = HEAD_DIM

NT = (((1,), (1,)), ((), ()))
TN = (((0,), (0,)), ((), ()))
VMEM = pl.BlockSpec(memory_space=pltpu.VMEM)
SMEM = pl.BlockSpec(memory_space=pltpu.SMEM)
PARAMS = pltpu.CompilerParams(vmem_limit_bytes=40 * 1024 * 1024)


def matmul(left, right, dims=(((1,), (0,)), ((), ()))):
    return lax.dot_general(left, right, dims, preferred_element_type=jnp.float32)


def swapped(array, axis, bits):
    size = lax.axis_size(axis)
    return lax.ppermute(array, axis, [(i, i ^ bits) for i in range(size)])


def call(kernel, out_shape, scratch, args, smem=0):
    return pl.pallas_call(
        kernel,
        out_shape=out_shape,
        in_specs=[SMEM] * smem + [VMEM] * (len(args) - smem),
        out_specs=[VMEM] * len(out_shape),
        scratch_shapes=scratch,
        compiler_params=PARAMS,
    )(*args)


def sds(shape, dtype=jnp.bfloat16):
    return jax.ShapeDtypeStruct(shape, dtype)


def pieces_kernel(q_ref, go_ref, ao_ref, hid_ref, lse_ref, qd_ref, hid_out_ref):
    rows, width = q_ref.shape
    product = go_ref[...].astype(jnp.float32) * ao_ref[...].astype(jnp.float32)
    high = product.astype(jnp.bfloat16)
    low = (product - high.astype(jnp.float32)).astype(jnp.bfloat16)
    head_of = lax.broadcasted_iota(jnp.int32, (Q_HEADS, width), 1) // HEAD_DIM
    ones = (head_of == lax.broadcasted_iota(jnp.int32, (Q_HEADS, width), 0)).astype(jnp.bfloat16)
    delta = matmul(ones, high, NT) + matmul(ones, low, NT)
    zero = jnp.zeros((4, rows), jnp.float32)
    for to in range(TEAM):
        columns = slice(to * PAIR, (to + 1) * PAIR)
        qd_ref[to, 0:rows, 0:PAIR] = q_ref[:, columns]
        qd_ref[to, 0:rows, PAIR:] = go_ref[:, columns]
        exact = jnp.concatenate([lse_ref[2 * to:2 * to + 2, :], delta[2 * to:2 * to + 2, :], zero], axis=0)
        first = exact.astype(jnp.bfloat16).astype(jnp.float32)
        second = (exact - first).astype(jnp.bfloat16).astype(jnp.float32)
        third = exact - first - second
        qd_ref[to, rows:, 0:PAIR] = jnp.concatenate([first, third], axis=0).astype(jnp.bfloat16)
        qd_ref[to, rows:, PAIR:] = jnp.concatenate([second, jnp.zeros_like(second)], axis=0).astype(jnp.bfloat16)
    span = hid_out_ref.shape[2]
    for to in range(hid_out_ref.shape[0]):
        hid_out_ref[to] = hid_ref[:, to * span:(to + 1) * span]


def project_kernel(fsdp, hid_ref, *rest):
    w_refs, out_ref = rest[:fsdp], rest[fsdp]
    mine = lax.axis_index("fsdp")
    span = w_refs[0].shape[0]
    total = None
    for m in range(fsdp):
        start = pl.multiple_of(jnp.bitwise_xor(mine, m) * span, span)
        term = matmul(hid_ref[:, pl.ds(start, span)], w_refs[m][...])
        total = term if total is None else total + term
    low = total.astype(jnp.bfloat16)
    for g in range(KV_HEADS):
        key = low[:, g * HEAD_DIM:(g + 1) * HEAD_DIM]
        value = low[:, KEY_WIDTH + g * HEAD_DIM:KEY_WIDTH + (g + 1) * HEAD_DIM]
        both = jnp.concatenate([key, value], axis=1)
        out_ref[2 * g] = both
        out_ref[2 * g + 1] = both


def lower_half(shape):
    return lax.broadcasted_iota(jnp.int32, shape, len(shape) - 1) < LOWER


def stacked(key_value):
    wide = key_value.astype(jnp.float32)
    turned = pltpu.roll(wide, LOWER, 1)
    lower = lower_half(wide.shape)
    zero = jnp.zeros_like(wide)
    keys = jnp.concatenate([jnp.where(lower, wide, zero), jnp.where(lower, zero, turned)], axis=0) * SCALE
    values = jnp.concatenate([jnp.where(lower, turned, zero), jnp.where(lower, zero, wide)], axis=0)
    return keys.astype(jnp.bfloat16), values.astype(jnp.bfloat16)


def both_heads(stats, first):
    lines = [jnp.concatenate([one[first + head:first + head + 1, :] for one in stats], axis=1) for head in range(2)]
    return lines


def tile(keys, values, query, grad, stats, mask):
    size = keys.shape[0] // 2
    lse, delta = both_heads(stats, 0), both_heads(stats, 2)
    scores = matmul(keys, query, NT)
    prob_grad = matmul(values, grad, NT)
    lows, grads = [], []
    for head in range(2):
        part = slice(head * size, (head + 1) * size)
        probs = jnp.exp(scores[part] - lse[head])
        if mask is not None:
            probs = jnp.where(mask, probs, 0.0)
        lows.append(probs.astype(jnp.bfloat16))
        grads.append((probs * (prob_grad[part] - delta[head])).astype(jnp.bfloat16))
    low, score_grad = jnp.concatenate(lows, axis=0), jnp.concatenate(grads, axis=0)
    return matmul(score_grad, query), matmul(low, grad), matmul(score_grad, keys, TN)


def folded(key_sum, value_sum):
    size = key_sum.shape[0] // 2
    lower = lower_half((size, PAIR))
    straight = jnp.where(lower, key_sum[:size], value_sum[size:])
    crossed = jnp.where(lower, value_sum[:size], key_sum[size:])
    return (straight + pltpu.roll(crossed, LOWER, 1)) * jnp.where(lower, SCALE, 1.0)


def unpacked(part, rows):
    exact = part[rows:, :].astype(jnp.float32)
    return exact[0:8, 0:PAIR] + exact[0:8, PAIR:] + exact[8:16, 0:PAIR]


def sequence_kernel(order_ref, qd_ref, kv_ref, dq_ref, dkv_ref, q_all, go_all, stat_all, key_all, value_all, dq_all, dkv_all):
    rows = kv_ref.shape[1]
    for stored in range(TEAM):
        place = order_ref[0, stored]
        q_all[place] = qd_ref[stored, 0:rows, 0:PAIR]
        go_all[place] = qd_ref[stored, 0:rows, PAIR:]
        stat_all[place] = unpacked(qd_ref.at[stored], rows)
        key_all[place], value_all[place] = stacked(kv_ref[stored])
    written = [False] * TEAM
    for block in range(TEAM):
        key_sum = value_sum = None
        first = block
        while first < TEAM:
            count = 2 - first % 2
            query = q_all[first:first + count].reshape(count * rows, PAIR)
            grad = go_all[first:first + count].reshape(count * rows, PAIR)
            mask = None
            if first == block:
                shape = (rows, count * rows)
                mask = lax.broadcasted_iota(jnp.int32, shape, 0) <= lax.broadcasted_iota(jnp.int32, shape, 1)
            key_part, value_part, query_part = tile(
                key_all[block], value_all[block], query, grad, [stat_all[first + i] for i in range(count)], mask)
            key_sum = key_part if key_sum is None else key_sum + key_part
            value_sum = value_part if value_sum is None else value_sum + value_part
            for i in range(count):
                piece = query_part[i * rows:(i + 1) * rows]
                at = first + i
                dq_all[at] = dq_all[at] + piece if written[at] else piece
                written[at] = True
            first += count
        dkv_all[block] = folded(key_sum, value_sum)
    for stored in range(TEAM):
        dq_ref[stored] = dq_all[order_ref[0, stored]].astype(jnp.bfloat16)
        dkv_ref[stored] = dkv_all[order_ref[0, stored]].astype(jnp.bfloat16)


def teams_kernel(order_ref, qd_ref, kv_ref, dq_ref, dkv_ref, dq_all):
    rows = kv_ref.shape[1]
    base = lax.axis_index("ctx") // TEAM * TEAM
    dq_all[...] = jnp.zeros_like(dq_all)

    @pl.loop(0, kv_ref.shape[0])
    def _(block):
        keys, values = stacked(kv_ref[block])
        dkv_ref[block] = jnp.zeros((rows, PAIR), jnp.float32)
        place = order_ref[0, block]

        @pl.loop(0, TEAM)
        def _(at):
            own = order_ref[0, base + at]

            @pl.when(place <= own)
            def _():
                shape = (rows, rows)
                mask = (place * rows + lax.broadcasted_iota(jnp.int32, shape, 0)
                        <= own * rows + lax.broadcasted_iota(jnp.int32, shape, 1))
                one = qd_ref.at[at]
                key_part, value_part, query_part = tile(
                    keys, values, one[0:rows, 0:PAIR], one[0:rows, PAIR:], [unpacked(one, rows)], mask)
                dq_all[at] += query_part
                dkv_ref[block] += folded(key_part, value_part)

    dq_ref[...] = dq_all[...].astype(jnp.bfloat16)


def owner_kernel(dkv_ref, out_ref):
    parts = [dkv_ref[i].astype(jnp.float32) for i in range(TEAM)]
    heads = [(parts[2 * g] + parts[2 * g + 1]).astype(jnp.bfloat16) for g in range(KV_HEADS)]
    keys, values = [one[:, :HEAD_DIM] for one in heads], [one[:, HEAD_DIM:] for one in heads]
    grad = jnp.concatenate(keys + values, axis=1)
    for to in range(out_ref.shape[0]):
        out_ref[to] = grad


def input_kernel(fsdp, grad_ref, *rest):
    w_refs, out_ref = rest[:fsdp], rest[fsdp]
    mine = lax.axis_index("fsdp")
    span = w_refs[0].shape[0]
    for m in range(fsdp):
        start = pl.multiple_of(jnp.bitwise_xor(mine, m) * span, span)
        out_ref[:, pl.ds(start, span)] = matmul(grad_ref[0], w_refs[m][...], NT).astype(jnp.bfloat16)


def weight_kernel(hid_ref, grad_ref, out_ref):
    tokens = hid_ref.shape[0] * hid_ref.shape[1]
    hid, grad = hid_ref[...].reshape(tokens, hid_ref.shape[2]), grad_ref[...].reshape(tokens, grad_ref.shape[2])
    out_ref[...] = matmul(hid, grad, TN).astype(jnp.bfloat16)


def query_kernel(dq_ref, out_ref):
    for pair in range(TEAM):
        out_ref[:, pair * PAIR:(pair + 1) * PAIR] = dq_ref[pair]


def total_kernel(part_ref, out_ref):
    total = part_ref[0].astype(jnp.float32)
    for i in range(1, part_ref.shape[0]):
        total = total + part_ref[i].astype(jnp.float32)
    out_ref[...] = total


def shards(hidden, queries, attn_out, grad_out, log_sums, block_order, w_kv):
    rows, model = hidden.shape[1:]
    fsdp, devices = lax.axis_size("fsdp"), lax.axis_size("ctx")
    teams = devices // TEAM
    f32 = jnp.float32
    span = model // fsdp
    inputs = hidden[0]
    columns = 2 * KEY_WIDTH
    block = (rows, PAIR)

    def across(array, axis, groups=None):
        return lax.all_to_all(array, axis, 0, 0, axis_index_groups=groups, tiled=True)

    team = None if teams == 1 else [[t * TEAM + i for i in range(TEAM)] for t in range(teams)]

    far = fsdp // 2
    w_parts = [w_kv] * fsdp
    w_parts[far] = swapped(w_kv, "fsdp", far)
    bits = 1
    while bits < far:
        for m in range(bits):
            for base in (0, far):
                w_parts[base + bits + m] = swapped(w_parts[base + m], "fsdp", bits)
        bits *= 2

    qd, hid = call(
        pieces_kernel, [sds((TEAM, rows + 16, 2 * PAIR)), sds((fsdp, rows, span))], [],
        (queries[0], grad_out[0], attn_out[0], inputs, log_sums[0]))
    qd = across(qd, "ctx", team)
    (kv,) = call(functools.partial(project_kernel, fsdp), [sds((TEAM,) + block)], [], (inputs, *w_parts))
    kv = across(kv, "ctx", team)
    hid = across(hid, "fsdp")

    if teams == 1:
        dq, dkv = call(
            sequence_kernel, [sds((TEAM,) + block)] * 2,
            [pltpu.VMEM((TEAM,) + block, jnp.bfloat16)] * 2 + [pltpu.VMEM((TEAM, 8, rows), f32)]
            + [pltpu.VMEM((TEAM, 2 * rows, PAIR), jnp.bfloat16)] * 2 + [pltpu.VMEM((TEAM,) + block, f32)] * 2,
            (block_order, qd, kv), smem=1)
    else:
        alike = [[t * TEAM + i for t in range(teams)] for i in range(TEAM)]
        kv = lax.all_gather(kv, "ctx", axis_index_groups=alike, axis=0, tiled=True)
        dq, dkv = call(
            teams_kernel, [sds((TEAM,) + block), sds((devices,) + block, f32)],
            [pltpu.VMEM((TEAM,) + block, f32)], (block_order, qd, kv), smem=1)
        dkv = lax.psum_scatter(dkv, "ctx", axis_index_groups=alike, scatter_dimension=0, tiled=True)
        dkv = dkv.astype(jnp.bfloat16)

    dkv = across(dkv, "ctx", team)
    (kv_grad,) = call(owner_kernel, [sds((fsdp, rows, columns))], [], (dkv,))
    grads = across(kv_grad, "fsdp")
    (parts,) = call(weight_kernel, [sds((span, columns))], [], (hid, grads))
    parts = across(parts.reshape(devices, span // devices, columns), "ctx")
    dq = across(dq, "ctx", team)
    (input_grads,) = call(functools.partial(input_kernel, fsdp), [sds((rows, model))], [], (kv_grad, *w_parts))
    (query_grads,) = call(query_kernel, [sds((rows, Q_HEADS * HEAD_DIM))], [], (dq,))
    (weight_grads,) = call(total_kernel, [sds((span // devices, columns), f32)], [], (parts,))
    return query_grads[None], input_grads[None], weight_grads


def solution(mesh):
    return jax.shard_map(
        shards,
        mesh=mesh,
        in_specs=(
            P("fsdp", "ctx", None),
            P("fsdp", "ctx", None),
            P("fsdp", "ctx", None),
            P("fsdp", "ctx", None),
            P("fsdp", None, "ctx"),
            P("fsdp", None),
            P("fsdp", None),
        ),
        out_specs=(P("fsdp", "ctx", None), P("fsdp", "ctx", None), P(("fsdp", "ctx"), None)),
        check_vma=False,
    )
```

```python
import functools

import jax
import jax.numpy as jnp
from jax import lax
from jax.experimental import pallas as pl
from jax.experimental.pallas import tpu as pltpu
from jax.sharding import PartitionSpec as P

Q_HEADS = 16
KV_HEADS = 4
HEAD_DIM = 64
GROUPS = Q_HEADS // KV_HEADS
KEY_WIDTH = KV_HEADS * HEAD_DIM
PAIR = 2 * HEAD_DIM
TEAM = 2 * KV_HEADS
GROUP = GROUPS * HEAD_DIM
SCALE = HEAD_DIM ** -0.5
LOWER = HEAD_DIM

NT = (((1,), (1,)), ((), ()))
TN = (((0,), (0,)), ((), ()))
VMEM = pl.BlockSpec(memory_space=pltpu.VMEM)
SMEM = pl.BlockSpec(memory_space=pltpu.SMEM)
ANY = pl.BlockSpec(memory_space=pl.ANY)
PARAMS = pltpu.CompilerParams(vmem_limit_bytes=40 * 1024 * 1024)


def matmul(left, right, dims=(((1,), (0,)), ((), ()))):
    return lax.dot_general(left, right, dims, preferred_element_type=jnp.float32)


def swapped(array, axis, bits):
    size = lax.axis_size(axis)
    return lax.ppermute(array, axis, [(i, i ^ bits) for i in range(size)])


def call(kernel, out_shape, scratch, args, smem=0, anywhere=0):
    specs = [SMEM] * smem + [ANY] * anywhere + [VMEM] * (len(args) - smem - anywhere)
    return pl.pallas_call(
        kernel,
        out_shape=out_shape,
        in_specs=specs,
        out_specs=[VMEM] * len(out_shape),
        scratch_shapes=scratch,
        compiler_params=PARAMS,
    )(*args)


def sds(shape, dtype=jnp.bfloat16):
    return jax.ShapeDtypeStruct(shape, dtype)


def head_side():
    me = lax.rem(lax.axis_index("ctx"), TEAM)
    return me // 2, lax.rem(me, 2)


def split(exact):
    first = exact.astype(jnp.bfloat16).astype(jnp.float32)
    second = (exact - first).astype(jnp.bfloat16).astype(jnp.float32)
    return first, second, exact - first - second


def pieces_kernel(q_ref, go_ref, ao_ref, lse_ref, *rest):
    out_refs, (grad, output, stat, sems) = rest[:KV_HEADS], rest[KV_HEADS:]
    rows, width = q_ref.shape
    head, _ = head_side()
    loads = [pltpu.make_async_copy(go_ref, grad, sems.at[0]), pltpu.make_async_copy(ao_ref, output, sems.at[1])]
    moves = []
    for m in range(KV_HEADS):
        columns = pl.ds(pl.multiple_of(jnp.bitwise_xor(head, m) * GROUP, GROUP), GROUP)
        for i, ref in enumerate((q_ref, go_ref)):
            moves.append(pltpu.make_async_copy(
                ref.at[:, columns], out_refs[m].at[0:rows, i * GROUP:(i + 1) * GROUP], sems.at[2 + 2 * m + i]))
    for copy in loads + moves:
        copy.start()
    for copy in loads:
        copy.wait()
    product = grad[...].astype(jnp.float32) * output[...].astype(jnp.float32)
    high = product.astype(jnp.bfloat16)
    low = (product - high.astype(jnp.float32)).astype(jnp.bfloat16)
    head_of = lax.broadcasted_iota(jnp.int32, (Q_HEADS, width), 1) // HEAD_DIM
    ones = (head_of == lax.broadcasted_iota(jnp.int32, (Q_HEADS, width), 0)).astype(jnp.bfloat16)
    delta = matmul(ones, high, NT) + matmul(ones, low, NT)
    for g in range(KV_HEADS):
        part = slice(g * GROUPS, (g + 1) * GROUPS)
        stat[g] = jnp.concatenate([lse_ref[part, :], delta[part, :]], axis=0)
    zero = jnp.zeros((2 * GROUPS, rows), jnp.float32)
    for m in range(KV_HEADS):
        lines = [*split(stat[jnp.bitwise_xor(head, m)]), zero]
        for i, one in enumerate(lines):
            full = jnp.concatenate([one, zero], axis=0).astype(jnp.bfloat16)
            out_refs[m][rows:, i * rows:(i + 1) * rows] = full
    for copy in moves:
        copy.wait()


def hidden_kernel(fsdp, hid_ref, *rest):
    out_refs, sems = rest[:fsdp], rest[fsdp]
    mine = lax.axis_index("fsdp")
    span = out_refs[0].shape[1]
    copies = []
    for m in range(fsdp):
        columns = pl.ds(pl.multiple_of(jnp.bitwise_xor(mine, m) * span, span), span)
        copies.append(pltpu.make_async_copy(hid_ref.at[:, columns], out_refs[m], sems.at[m]))
    for copy in copies:
        copy.start()
    for copy in copies:
        copy.wait()


def project_kernel(fsdp, hid_ref, *rest):
    w_refs, out_refs, (parts,) = rest[:fsdp], rest[fsdp:fsdp + KV_HEADS], rest[fsdp + KV_HEADS:]
    mine = lax.axis_index("fsdp")
    head, _ = head_side()
    span = w_refs[0].shape[0]
    total = None
    for m in range(fsdp):
        start = pl.multiple_of(jnp.bitwise_xor(mine, m) * span, span)
        term = matmul(hid_ref[:, pl.ds(start, span)], w_refs[m][...])
        total = term if total is None else total + term
    low = total.astype(jnp.bfloat16)
    for g in range(KV_HEADS):
        key = low[:, g * HEAD_DIM:(g + 1) * HEAD_DIM]
        value = low[:, KEY_WIDTH + g * HEAD_DIM:KEY_WIDTH + (g + 1) * HEAD_DIM]
        parts[g] = jnp.concatenate([key, value], axis=1)
    for m in range(KV_HEADS):
        out_refs[m][...] = parts[jnp.bitwise_xor(head, m)]


def lower_half(shape):
    return lax.broadcasted_iota(jnp.int32, shape, len(shape) - 1) < LOWER


def stacked(key_value):
    wide = key_value.astype(jnp.float32)
    turned = pltpu.roll(wide, LOWER, 1)
    lower = lower_half(wide.shape)
    zero = jnp.zeros_like(wide)
    keys = jnp.concatenate([jnp.where(lower, wide, zero), jnp.where(lower, zero, turned)], axis=0) * SCALE
    values = jnp.concatenate([jnp.where(lower, turned, zero), jnp.where(lower, zero, wide)], axis=0)
    return keys.astype(jnp.bfloat16), values.astype(jnp.bfloat16)


def tile(keys, values, query, grad, stats, mask):
    size = keys.shape[0] // 2
    lse, delta = stats[:2], stats[2:]
    scores = matmul(keys, query, NT)
    prob_grad = matmul(values, grad, NT)
    lows, grads = [], []
    for head in range(2):
        part = slice(head * size, (head + 1) * size)
        probs = jnp.exp(scores[part] - lse[head])
        if mask is not None:
            probs = jnp.where(mask, probs, 0.0)
        lows.append(probs.astype(jnp.bfloat16))
        grads.append((probs * (prob_grad[part] - delta[head])).astype(jnp.bfloat16))
    low, score_grad = jnp.concatenate(lows, axis=0), jnp.concatenate(grads, axis=0)
    return matmul(score_grad, query), matmul(low, grad), matmul(score_grad, keys, TN)


def folded(key_sum, value_sum):
    size = key_sum.shape[0] // 2
    lower = lower_half((size, PAIR))
    straight = jnp.where(lower, key_sum[:size], value_sum[size:])
    crossed = jnp.where(lower, value_sum[:size], key_sum[size:])
    return (straight + pltpu.roll(crossed, LOWER, 1)) * jnp.where(lower, SCALE, 1.0)


def unpacked(part, rows):
    exact = part[rows:, 0:3 * rows].astype(jnp.float32)[0:2 * GROUPS]
    return exact[:, 0:rows] + exact[:, rows:2 * rows] + exact[:, 2 * rows:]


def pair_stats(stat, pair):
    first = 2 * pair
    return [stat[first:first + 1], stat[first + 1:first + 2],
            stat[GROUPS + first:GROUPS + first + 1], stat[GROUPS + first + 1:GROUPS + first + 2]]


def sequence_kernel(order_ref, *rest):
    qd_refs, kv_refs, rest = rest[:TEAM], rest[TEAM:TEAM + KV_HEADS], rest[TEAM + KV_HEADS:]
    dkv_refs, keep_ref, send_ref, rest = rest[:KV_HEADS], rest[KV_HEADS], rest[KV_HEADS + 1], rest[KV_HEADS + 2:]
    q_all, go_all, stat_all, key_all, value_all, dq_all, dkv_all = rest
    rows = kv_refs[0].shape[0]
    head, side = head_side()
    near = [order_ref[0, 2 * jnp.bitwise_xor(head, m) + side] for m in range(KV_HEADS)]
    far = [order_ref[0, 2 * jnp.bitwise_xor(head, m) + 1 - side] for m in range(KV_HEADS)]
    for place, ref in zip(near + far, qd_refs):
        q_all[place] = ref[0:rows, 0:GROUP]
        go_all[place] = ref[0:rows, GROUP:]
        stat_all[place] = unpacked(ref, rows)
    for place, ref in zip(near, kv_refs):
        key_all[place], value_all[place] = stacked(ref[...])
    dq_all[...] = jnp.zeros_like(dq_all)
    for block in range(TEAM):
        mine = functools.reduce(jnp.logical_or, [place == block for place in near])

        @pl.when(mine)
        def _():
            count = TEAM - block
            shape = (rows, count * rows)
            mask = lax.broadcasted_iota(jnp.int32, shape, 0) <= lax.broadcasted_iota(jnp.int32, shape, 1)
            stats = jnp.concatenate([stat_all[i] for i in range(block, TEAM)], axis=1)
            key_sum = value_sum = None
            for pair in range(GROUPS // 2):
                columns = slice(pair * PAIR, (pair + 1) * PAIR)
                query = q_all[block:, :, columns].reshape(count * rows, PAIR)
                grad = go_all[block:, :, columns].reshape(count * rows, PAIR)
                key_part, value_part, query_part = tile(
                    key_all[block], value_all[block], query, grad, pair_stats(stats, pair), mask)
                key_sum = key_part if key_sum is None else key_sum + key_part
                value_sum = value_part if value_sum is None else value_sum + value_part
                dq_all[block:, :, columns] += query_part.reshape(count, rows, PAIR)
            dkv_all[block] = folded(key_sum, value_sum)

    for m in range(KV_HEADS):
        dkv_refs[m][...] = dkv_all[near[m]].astype(jnp.bfloat16)
        keep_ref[m] = dq_all[near[m]]
        send_ref[m] = dq_all[far[m]].astype(jnp.bfloat16)


def teams_kernel(order_ref, qd_ref, kv_ref, dkv_ref, keep_ref, send_ref, dq_all):
    rows = kv_ref.shape[1]
    head, side = head_side()
    base = lax.axis_index("ctx") // TEAM * TEAM
    dq_all[...] = jnp.zeros_like(dq_all)

    @pl.loop(0, kv_ref.shape[0])
    def _(block):
        keys, values = stacked(kv_ref[block])
        dkv_ref[block] = jnp.zeros((rows, PAIR), jnp.float32)
        stored = block // KV_HEADS * TEAM + 2 * jnp.bitwise_xor(head, lax.rem(block, KV_HEADS)) + side
        place = order_ref[0, stored]

        @pl.loop(0, TEAM)
        def _(at):
            turned = jnp.where(at < KV_HEADS, side, 1 - side)
            own = order_ref[0, base + 2 * jnp.bitwise_xor(head, lax.rem(at, KV_HEADS)) + turned]

            @pl.when(place <= own)
            def _():
                shape = (rows, rows)
                mask = (place * rows + lax.broadcasted_iota(jnp.int32, shape, 0)
                        <= own * rows + lax.broadcasted_iota(jnp.int32, shape, 1))
                one = qd_ref.at[at]
                stats = unpacked(one, rows)
                for pair in range(GROUPS // 2):
                    first = pair * PAIR
                    key_part, value_part, query_part = tile(
                        keys, values, one[0:rows, first:first + PAIR], one[0:rows, GROUP + first:GROUP + first + PAIR],
                        pair_stats(stats, pair), mask)
                    dq_all[at, :, first:first + PAIR] += query_part
                    dkv_ref[block] += folded(key_part, value_part)

    keep_ref[...] = dq_all[0:KV_HEADS]
    send_ref[...] = dq_all[KV_HEADS:].astype(jnp.bfloat16)


def owner_kernel(*rest):
    dkv_refs, out_ref, parts = rest[:KV_HEADS], rest[KV_HEADS], rest[KV_HEADS + 1]
    head, _ = head_side()
    for m in range(KV_HEADS):
        parts[jnp.bitwise_xor(head, m)] = dkv_refs[m][...]
    keys = [parts[g, :, :HEAD_DIM] for g in range(KV_HEADS)]
    values = [parts[g, :, HEAD_DIM:] for g in range(KV_HEADS)]
    out_ref[...] = jnp.concatenate(keys + values, axis=1)


def pair_kernel(keep_ref, got_ref, *out_refs):
    for m in range(KV_HEADS):
        out_refs[m][...] = (keep_ref[m] + got_ref[m].astype(jnp.float32)).astype(jnp.bfloat16)


def query_kernel(*rest):
    dq_refs, out_ref = rest[:KV_HEADS], rest[KV_HEADS]
    head, _ = head_side()
    for m in range(KV_HEADS):
        columns = pl.ds(pl.multiple_of(jnp.bitwise_xor(head, m) * GROUP, GROUP), GROUP)
        out_ref[:, columns] = dq_refs[m][...]


def input_kernel(fsdp, grad_ref, *rest):
    w_refs, out_ref = rest[:fsdp], rest[fsdp]
    mine = lax.axis_index("fsdp")
    span = w_refs[0].shape[0]
    for m in range(fsdp):
        start = pl.multiple_of(jnp.bitwise_xor(mine, m) * span, span)
        out_ref[:, pl.ds(start, span)] = matmul(grad_ref[...], w_refs[m][...], NT).astype(jnp.bfloat16)


def weight_kernel(fsdp, *rest):
    hid_refs, grad_refs, out_ref = rest[:fsdp], rest[fsdp:2 * fsdp], rest[2 * fsdp]
    hid = jnp.concatenate([ref[...] for ref in hid_refs], axis=0)
    grad = jnp.concatenate([ref[...] for ref in grad_refs], axis=0)
    out_ref[...] = matmul(hid, grad, TN).astype(jnp.bfloat16)


def total_kernel(part_ref, out_ref):
    total = part_ref[0].astype(jnp.float32)
    for i in range(1, part_ref.shape[0]):
        total = total + part_ref[i].astype(jnp.float32)
    out_ref[...] = total


def over_fsdp(own, fsdp):
    got = list(own)
    bits = fsdp // 2
    while bits:
        for m in range(fsdp):
            if m & bits:
                got[m] = swapped(got[m], "fsdp", bits)
        bits //= 2
    return got


def shards(hidden, queries, attn_out, grad_out, log_sums, block_order, w_kv):
    rows, model = hidden.shape[1:]
    fsdp, devices = lax.axis_size("fsdp"), lax.axis_size("ctx")
    teams = devices // TEAM
    f32 = jnp.float32
    span = model // fsdp
    inputs = hidden[0]
    columns = 2 * KEY_WIDTH
    block, wide = (rows, PAIR), (rows, GROUP)

    def along_heads(arrays):
        return [arrays[0]] + [swapped(arrays[m], "ctx", 2 * m) for m in range(1, KV_HEADS)]

    w_parts = over_fsdp([w_kv] * fsdp, fsdp)

    qd = call(
        pieces_kernel, [sds((rows + 16, 2 * GROUP))] * KV_HEADS,
        [pltpu.VMEM((rows, Q_HEADS * HEAD_DIM), jnp.bfloat16)] * 2
        + [pltpu.VMEM((KV_HEADS, 2 * GROUPS, rows), f32), pltpu.SemaphoreType.DMA((2 + 2 * KV_HEADS,))],
        (queries[0], grad_out[0], attn_out[0], log_sums[0]), anywhere=3)
    qd = along_heads(qd)
    qd = qd + [swapped(one, "ctx", 1) for one in qd]

    kv = call(
        functools.partial(project_kernel, fsdp), [sds(block)] * KV_HEADS,
        [pltpu.VMEM((KV_HEADS,) + block, jnp.bfloat16)], (inputs, *w_parts))
    kv = along_heads(kv)

    hid = call(
        functools.partial(hidden_kernel, fsdp), [sds((rows, span))] * fsdp, [pltpu.SemaphoreType.DMA((fsdp,))],
        (inputs,), anywhere=1)
    hid = over_fsdp(hid, fsdp)

    half = (KV_HEADS,) + wide
    if teams == 1:
        *dkv, keep, give = call(
            sequence_kernel, [sds(block)] * KV_HEADS + [sds(half, f32), sds(half)],
            [pltpu.VMEM((TEAM,) + wide, jnp.bfloat16)] * 2 + [pltpu.VMEM((TEAM, 2 * GROUPS, rows), f32)]
            + [pltpu.VMEM((TEAM, 2 * rows, PAIR), jnp.bfloat16)] * 2
            + [pltpu.VMEM((TEAM,) + wide, f32), pltpu.VMEM((TEAM,) + block, f32)],
            (block_order, *qd, *kv), smem=1)
    else:
        alike = [[t * TEAM + i for t in range(teams)] for i in range(TEAM)]
        kv = lax.all_gather(jnp.stack(kv), "ctx", axis_index_groups=alike, axis=0, tiled=True)
        dkv, keep, give = call(
            teams_kernel, [sds((teams * KV_HEADS,) + block, f32), sds(half, f32), sds(half)],
            [pltpu.VMEM((TEAM,) + wide, f32)], (block_order, jnp.stack(qd), kv), smem=1)
        dkv = lax.psum_scatter(dkv, "ctx", axis_index_groups=alike, scatter_dimension=0, tiled=True)
        dkv = [dkv[m].astype(jnp.bfloat16) for m in range(KV_HEADS)]

    (kv_grad,) = call(
        owner_kernel, [sds((rows, columns))], [pltpu.VMEM((KV_HEADS,) + block, jnp.bfloat16)], along_heads(dkv))
    grads = over_fsdp([kv_grad] * fsdp, fsdp)
    (parts,) = call(functools.partial(weight_kernel, fsdp), [sds((span, columns))], [], (*hid, *grads))
    parts = lax.all_to_all(parts.reshape(devices, span // devices, columns), "ctx", 0, 0, tiled=True)

    dq = call(pair_kernel, [sds(wide)] * KV_HEADS, [], (keep, swapped(give, "ctx", 1)))
    (query_grads,) = call(query_kernel, [sds((rows, Q_HEADS * HEAD_DIM))], [], along_heads(dq))
    (input_grads,) = call(functools.partial(input_kernel, fsdp), [sds((rows, model))], [], (kv_grad, *w_parts))
    (weight_grads,) = call(total_kernel, [sds((span // devices, columns), f32)], [], (parts,))
    return query_grads[None], input_grads[None], weight_grads


def solution(mesh):
    return jax.shard_map(
        shards,
        mesh=mesh,
        in_specs=(
            P("fsdp", "ctx", None),
            P("fsdp", "ctx", None),
            P("fsdp", "ctx", None),
            P("fsdp", "ctx", None),
            P("fsdp", None, "ctx"),
            P("fsdp", None),
            P("fsdp", None),
        ),
        out_specs=(P("fsdp", "ctx", None), P("fsdp", "ctx", None), P(("fsdp", "ctx"), None)),
        check_vma=False,
    )
```

```python
import functools

import jax
import jax.numpy as jnp
from jax import lax
from jax.experimental import pallas as pl
from jax.experimental.pallas import tpu as pltpu
from jax.sharding import PartitionSpec as P

Q_HEADS = 16
KV_HEADS = 4
HEAD_DIM = 64
GROUPS = Q_HEADS // KV_HEADS
KEY_WIDTH = KV_HEADS * HEAD_DIM
PAIR = 2 * HEAD_DIM
TEAM = 2 * KV_HEADS
GROUP = GROUPS * HEAD_DIM
SCALE = HEAD_DIM ** -0.5
LOWER = HEAD_DIM

NT = (((1,), (1,)), ((), ()))
TN = (((0,), (0,)), ((), ()))
VMEM = pl.BlockSpec(memory_space=pltpu.VMEM)
SMEM = pl.BlockSpec(memory_space=pltpu.SMEM)
ANY = pl.BlockSpec(memory_space=pl.ANY)
HBM = pl.BlockSpec(memory_space=pltpu.HBM)
PARAMS = pltpu.CompilerParams(vmem_limit_bytes=40 * 1024 * 1024)
WHOLE = pltpu.CompilerParams(vmem_limit_bytes=60 * 1024 * 1024)


def matmul(left, right, dims=(((1,), (0,)), ((), ()))):
    return lax.dot_general(left, right, dims, preferred_element_type=jnp.float32)


def swapped(array, axis, bits):
    size = lax.axis_size(axis)
    return lax.ppermute(array, axis, [(i, i ^ bits) for i in range(size)])


def call(kernel, out_shape, scratch, args, smem=0, hbm=0, after=()):
    given = len(args)
    params = WHOLE if hbm else PARAMS

    def body(*refs):
        kernel(*refs[:given], *refs[given + len(after):])

    specs = [SMEM] * smem + [HBM] * hbm + [VMEM] * (given - smem - hbm) + [ANY] * len(after)
    return pl.pallas_call(
        body,
        out_shape=out_shape,
        in_specs=specs,
        out_specs=[VMEM] * len(out_shape),
        scratch_shapes=scratch,
        compiler_params=params,
    )(*args, *after)


def held(array, after):
    def body(*refs):
        pass

    return pl.pallas_call(
        body,
        out_shape=sds(array.shape, array.dtype),
        in_specs=[ANY] * (1 + len(after)),
        out_specs=ANY,
        input_output_aliases={0: 0},
        compiler_params=PARAMS,
    )(array, *after)


def sds(shape, dtype=jnp.bfloat16):
    return jax.ShapeDtypeStruct(shape, dtype)


def head_side():
    me = lax.rem(lax.axis_index("ctx"), TEAM)
    return me // 2, lax.rem(me, 2)


def split(exact):
    first = exact.astype(jnp.bfloat16).astype(jnp.float32)
    second = (exact - first).astype(jnp.bfloat16).astype(jnp.float32)
    return first, second, exact - first - second


def pieces_kernel(q_ref, go_ref, ao_ref, lse_ref, *rest):
    out_refs, (grad, output, lse, stat, sems) = rest[:KV_HEADS], rest[KV_HEADS:]
    rows, width = q_ref.shape
    head, _ = head_side()
    loads = [pltpu.make_async_copy(ref, to, sems.at[i])
             for i, (ref, to) in enumerate(((go_ref, grad), (ao_ref, output), (lse_ref, lse)))]
    moves = []
    for m in range(KV_HEADS):
        columns = pl.ds(pl.multiple_of(jnp.bitwise_xor(head, m) * GROUP, GROUP), GROUP)
        for i, ref in enumerate((q_ref, go_ref)):
            moves.append(pltpu.make_async_copy(
                ref.at[:, columns], out_refs[m].at[0:rows, i * GROUP:(i + 1) * GROUP], sems.at[3 + 2 * m + i]))
    for copy in loads + moves:
        copy.start()
    for copy in loads:
        copy.wait()
    product = grad[...].astype(jnp.float32) * output[...].astype(jnp.float32)
    high = product.astype(jnp.bfloat16)
    low = (product - high.astype(jnp.float32)).astype(jnp.bfloat16)
    head_of = lax.broadcasted_iota(jnp.int32, (Q_HEADS, width), 1) // HEAD_DIM
    ones = (head_of == lax.broadcasted_iota(jnp.int32, (Q_HEADS, width), 0)).astype(jnp.bfloat16)
    delta = matmul(ones, high, NT) + matmul(ones, low, NT)
    for g in range(KV_HEADS):
        part = slice(g * GROUPS, (g + 1) * GROUPS)
        stat[g] = jnp.concatenate([lse[part, :], delta[part, :]], axis=0)
    zero = jnp.zeros((2 * GROUPS, rows), jnp.float32)
    for m in range(KV_HEADS):
        lines = [*split(stat[jnp.bitwise_xor(head, m)]), zero]
        for i, one in enumerate(lines):
            full = jnp.concatenate([one, zero], axis=0).astype(jnp.bfloat16)
            out_refs[m][rows:, i * rows:(i + 1) * rows] = full
    for copy in moves:
        copy.wait()


def hidden_kernel(fsdp, hid_ref, *rest):
    near_refs, far_ref, sems = rest[:fsdp // 2], rest[fsdp // 2], rest[fsdp // 2 + 1]
    mine = lax.axis_index("fsdp")
    span = far_ref.shape[2]
    copies = []
    for m in range(fsdp):
        columns = pl.ds(pl.multiple_of(jnp.bitwise_xor(mine, m) * span, span), span)
        to = near_refs[m] if m < fsdp // 2 else far_ref.at[m - fsdp // 2]
        copies.append(pltpu.make_async_copy(hid_ref.at[:, columns], to, sems.at[m]))
    for copy in copies:
        copy.start()
    for copy in copies:
        copy.wait()


def project_kernel(fsdp, hid_ref, *rest):
    w_refs, out_refs, (parts,) = rest[:fsdp], rest[fsdp:fsdp + KV_HEADS], rest[fsdp + KV_HEADS:]
    mine = lax.axis_index("fsdp")
    head, _ = head_side()
    span = w_refs[0].shape[0]
    total = None
    for m in range(fsdp):
        start = pl.multiple_of(jnp.bitwise_xor(mine, m) * span, span)
        term = matmul(hid_ref[:, pl.ds(start, span)], w_refs[m][...])
        total = term if total is None else total + term
    low = total.astype(jnp.bfloat16)
    for g in range(KV_HEADS):
        key = low[:, g * HEAD_DIM:(g + 1) * HEAD_DIM]
        value = low[:, KEY_WIDTH + g * HEAD_DIM:KEY_WIDTH + (g + 1) * HEAD_DIM]
        parts[g] = jnp.concatenate([key, value], axis=1)
    for m in range(KV_HEADS):
        out_refs[m][...] = parts[jnp.bitwise_xor(head, m)]


def lower_half(shape):
    return lax.broadcasted_iota(jnp.int32, shape, len(shape) - 1) < LOWER


def stacked(key_value):
    wide = key_value.astype(jnp.float32)
    turned = pltpu.roll(wide, LOWER, 1)
    lower = lower_half(wide.shape)
    zero = jnp.zeros_like(wide)
    keys = jnp.concatenate([jnp.where(lower, wide, zero), jnp.where(lower, zero, turned)], axis=0) * SCALE
    values = jnp.concatenate([jnp.where(lower, turned, zero), jnp.where(lower, zero, wide)], axis=0)
    return keys.astype(jnp.bfloat16), values.astype(jnp.bfloat16)


def tile(keys, values, query, grad, stats, mask):
    size = keys.shape[0] // 2
    lse, delta = stats[:2], stats[2:]
    scores = matmul(keys, query, NT)
    prob_grad = matmul(values, grad, NT)
    lows, grads = [], []
    for head in range(2):
        part = slice(head * size, (head + 1) * size)
        probs = jnp.exp(scores[part] - lse[head])
        if mask is not None:
            probs = jnp.where(mask, probs, 0.0)
        lows.append(probs.astype(jnp.bfloat16))
        grads.append((probs * (prob_grad[part] - delta[head])).astype(jnp.bfloat16))
    low, score_grad = jnp.concatenate(lows, axis=0), jnp.concatenate(grads, axis=0)
    return matmul(score_grad, query), matmul(low, grad), matmul(score_grad, keys, TN)


def folded(key_sum, value_sum):
    size = key_sum.shape[0] // 2
    lower = lower_half((size, PAIR))
    straight = jnp.where(lower, key_sum[:size], value_sum[size:])
    crossed = jnp.where(lower, value_sum[:size], key_sum[size:])
    return (straight + pltpu.roll(crossed, LOWER, 1)) * jnp.where(lower, SCALE, 1.0)


def unpacked(part, rows):
    exact = part[rows:, 0:3 * rows].astype(jnp.float32)[0:2 * GROUPS]
    return exact[:, 0:rows] + exact[:, rows:2 * rows] + exact[:, 2 * rows:]


def pair_stats(stat, pair):
    first = 2 * pair
    return [stat[first:first + 1], stat[first + 1:first + 2],
            stat[GROUPS + first:GROUPS + first + 1], stat[GROUPS + first + 1:GROUPS + first + 2]]


def sequence_kernel(order_ref, *rest):
    qd_refs, kv_refs, rest = rest[:TEAM], rest[TEAM:TEAM + KV_HEADS], rest[TEAM + KV_HEADS:]
    dkv_refs, keep_ref, send_ref, rest = rest[:KV_HEADS], rest[KV_HEADS], rest[KV_HEADS + 1], rest[KV_HEADS + 2:]
    q_all, go_all, stat_all, key_all, value_all, dq_all, dkv_all = rest
    rows = kv_refs[0].shape[0]
    head, side = head_side()
    near = [order_ref[0, 2 * jnp.bitwise_xor(head, m) + side] for m in range(KV_HEADS)]
    far = [order_ref[0, 2 * jnp.bitwise_xor(head, m) + 1 - side] for m in range(KV_HEADS)]
    for place, ref in zip(near + far, qd_refs):
        q_all[place] = ref[0:rows, 0:GROUP]
        go_all[place] = ref[0:rows, GROUP:]
        stat_all[place] = unpacked(ref, rows)
    for place, ref in zip(near, kv_refs):
        key_all[place], value_all[place] = stacked(ref[...])
    dq_all[...] = jnp.zeros_like(dq_all)
    for block in range(TEAM):
        mine = functools.reduce(jnp.logical_or, [place == block for place in near])

        @pl.when(mine)
        def _():
            count = TEAM - block
            shape = (rows, count * rows)
            mask = lax.broadcasted_iota(jnp.int32, shape, 0) <= lax.broadcasted_iota(jnp.int32, shape, 1)
            stats = jnp.concatenate([stat_all[i] for i in range(block, TEAM)], axis=1)
            key_sum = value_sum = None
            for pair in range(GROUPS // 2):
                columns = slice(pair * PAIR, (pair + 1) * PAIR)
                query = q_all[block:, :, columns].reshape(count * rows, PAIR)
                grad = go_all[block:, :, columns].reshape(count * rows, PAIR)
                key_part, value_part, query_part = tile(
                    key_all[block], value_all[block], query, grad, pair_stats(stats, pair), mask)
                key_sum = key_part if key_sum is None else key_sum + key_part
                value_sum = value_part if value_sum is None else value_sum + value_part
                dq_all[block:, :, columns] += query_part.reshape(count, rows, PAIR)
            dkv_all[block] = folded(key_sum, value_sum)

    for m in range(KV_HEADS):
        dkv_refs[m][...] = dkv_all[near[m]].astype(jnp.bfloat16)
        keep_ref[m] = dq_all[near[m]]
        send_ref[m] = dq_all[far[m]].astype(jnp.bfloat16)


def teams_kernel(order_ref, qd_ref, kv_ref, dkv_ref, keep_ref, send_ref, dq_all):
    rows = kv_ref.shape[1]
    head, side = head_side()
    base = lax.axis_index("ctx") // TEAM * TEAM
    dq_all[...] = jnp.zeros_like(dq_all)

    @pl.loop(0, kv_ref.shape[0])
    def _(block):
        keys, values = stacked(kv_ref[block])
        dkv_ref[block] = jnp.zeros((rows, PAIR), jnp.float32)
        stored = block // KV_HEADS * TEAM + 2 * jnp.bitwise_xor(head, lax.rem(block, KV_HEADS)) + side
        place = order_ref[0, stored]

        @pl.loop(0, TEAM)
        def _(at):
            turned = jnp.where(at < KV_HEADS, side, 1 - side)
            own = order_ref[0, base + 2 * jnp.bitwise_xor(head, lax.rem(at, KV_HEADS)) + turned]

            @pl.when(place <= own)
            def _():
                shape = (rows, rows)
                mask = (place * rows + lax.broadcasted_iota(jnp.int32, shape, 0)
                        <= own * rows + lax.broadcasted_iota(jnp.int32, shape, 1))
                one = qd_ref.at[at]
                stats = unpacked(one, rows)
                for pair in range(GROUPS // 2):
                    first = pair * PAIR
                    key_part, value_part, query_part = tile(
                        keys, values, one[0:rows, first:first + PAIR], one[0:rows, GROUP + first:GROUP + first + PAIR],
                        pair_stats(stats, pair), mask)
                    dq_all[at, :, first:first + PAIR] += query_part
                    dkv_ref[block] += folded(key_part, value_part)

    keep_ref[...] = dq_all[0:KV_HEADS]
    send_ref[...] = dq_all[KV_HEADS:].astype(jnp.bfloat16)


def owner_kernel(*rest):
    dkv_refs, out_ref, parts = rest[:KV_HEADS], rest[KV_HEADS], rest[KV_HEADS + 1]
    head, _ = head_side()
    for m in range(KV_HEADS):
        parts[jnp.bitwise_xor(head, m)] = dkv_refs[m][...]
    keys = [parts[g, :, :HEAD_DIM] for g in range(KV_HEADS)]
    values = [parts[g, :, HEAD_DIM:] for g in range(KV_HEADS)]
    out_ref[...] = jnp.concatenate(keys + values, axis=1)


def pair_kernel(keep_ref, got_ref, *out_refs):
    for m in range(KV_HEADS):
        out_refs[m][...] = (keep_ref[m] + got_ref[m].astype(jnp.float32)).astype(jnp.bfloat16)


def query_kernel(*rest):
    dq_refs, out_ref = rest[:KV_HEADS], rest[KV_HEADS]
    head, _ = head_side()
    for m in range(KV_HEADS):
        columns = pl.ds(pl.multiple_of(jnp.bitwise_xor(head, m) * GROUP, GROUP), GROUP)
        out_ref[:, columns] = dq_refs[m][...]


def input_kernel(fsdp, grad_ref, *rest):
    w_refs, out_ref = rest[:fsdp], rest[fsdp]
    mine = lax.axis_index("fsdp")
    span = w_refs[0].shape[0]
    for m in range(fsdp):
        start = pl.multiple_of(jnp.bitwise_xor(mine, m) * span, span)
        out_ref[:, pl.ds(start, span)] = matmul(grad_ref[...], w_refs[m][...], NT).astype(jnp.bfloat16)


def weight_kernel(fsdp, *rest):
    hid_refs, grad_refs, out_ref = rest[:fsdp], rest[fsdp:2 * fsdp], rest[2 * fsdp]
    hid = jnp.concatenate([ref[...] for ref in hid_refs], axis=0)
    grad = jnp.concatenate([ref[...] for ref in grad_refs], axis=0)
    out_ref[...] = matmul(hid, grad, TN).astype(jnp.bfloat16)


def total_kernel(part_ref, out_ref):
    total = part_ref[0].astype(jnp.float32)
    for i in range(1, part_ref.shape[0]):
        total = total + part_ref[i].astype(jnp.float32)
    out_ref[...] = total


def over_fsdp(own, bits):
    got = list(own)
    while bits:
        for m in range(len(own)):
            if m & bits:
                got[m] = swapped(got[m], "fsdp", bits)
        bits //= 2
    return got


def shards(hidden, queries, attn_out, grad_out, log_sums, block_order, w_kv):
    rows, model = hidden.shape[1:]
    fsdp, devices = lax.axis_size("fsdp"), lax.axis_size("ctx")
    teams = devices // TEAM
    f32 = jnp.float32
    span = model // fsdp
    inputs = hidden[0]
    columns = 2 * KEY_WIDTH
    block, wide = (rows, PAIR), (rows, GROUP)

    def along_heads(arrays):
        return [arrays[0]] + [swapped(arrays[m], "ctx", 2 * m) for m in range(1, KV_HEADS)]

    far = fsdp // 2
    qd = call(
        pieces_kernel, [sds((rows + 16, 2 * GROUP))] * KV_HEADS,
        [pltpu.VMEM((rows, Q_HEADS * HEAD_DIM), jnp.bfloat16)] * 2
        + [pltpu.VMEM((Q_HEADS, rows), f32), pltpu.VMEM((KV_HEADS, 2 * GROUPS, rows), f32),
           pltpu.SemaphoreType.DMA((3 + 2 * KV_HEADS,))],
        (queries[0], grad_out[0], attn_out[0], log_sums[0]), hbm=4)
    qd = along_heads(qd)
    qd = qd + [swapped(one, "ctx", 1) for one in qd]
    w_far = held(swapped(w_kv, "fsdp", far), (qd[1], qd[2], qd[KV_HEADS]))
    w_parts = over_fsdp([w_kv] * far + [w_far] * (fsdp - far), far // 2)

    kv = call(
        functools.partial(project_kernel, fsdp), [sds(block)] * KV_HEADS,
        [pltpu.VMEM((KV_HEADS,) + block, jnp.bfloat16)], (inputs, *w_parts), after=(*qd[1:KV_HEADS], qd[KV_HEADS]))
    kv = along_heads(kv)

    *hid, hid_far = call(
        functools.partial(hidden_kernel, fsdp), [sds((rows, span))] * far + [sds((fsdp - far, rows, span))],
        [pltpu.SemaphoreType.DMA((fsdp,))], (inputs,), hbm=1)
    hid_far = swapped(hid_far, "fsdp", far)
    hid = over_fsdp(hid + [hid_far[m] for m in range(fsdp - far)], far // 2)

    half = (KV_HEADS,) + wide
    if teams == 1:
        *dkv, keep, give = call(
            sequence_kernel, [sds(block)] * KV_HEADS + [sds(half, f32), sds(half)],
            [pltpu.VMEM((TEAM,) + wide, jnp.bfloat16)] * 2 + [pltpu.VMEM((TEAM, 2 * GROUPS, rows), f32)]
            + [pltpu.VMEM((TEAM, 2 * rows, PAIR), jnp.bfloat16)] * 2
            + [pltpu.VMEM((TEAM,) + wide, f32), pltpu.VMEM((TEAM,) + block, f32)],
            (block_order, *qd, *kv), smem=1, after=hid[1:])
    else:
        alike = [[t * TEAM + i for t in range(teams)] for i in range(TEAM)]
        kv = lax.all_gather(jnp.stack(kv), "ctx", axis_index_groups=alike, axis=0, tiled=True)
        dkv, keep, give = call(
            teams_kernel, [sds((teams * KV_HEADS,) + block, f32), sds(half, f32), sds(half)],
            [pltpu.VMEM((TEAM,) + wide, f32)], (block_order, jnp.stack(qd), kv), smem=1)
        dkv = lax.psum_scatter(dkv, "ctx", axis_index_groups=alike, scatter_dimension=0, tiled=True)
        dkv = [dkv[m].astype(jnp.bfloat16) for m in range(KV_HEADS)]

    give = swapped(give, "ctx", 1)
    (kv_grad,) = call(
        owner_kernel, [sds((rows, columns))], [pltpu.VMEM((KV_HEADS,) + block, jnp.bfloat16)],
        along_heads(dkv), after=(give,))
    grads = over_fsdp([kv_grad] * fsdp, far)
    (parts,) = call(functools.partial(weight_kernel, fsdp), [sds((span, columns))], [], (*hid, *grads))
    sums = lax.all_to_all(parts.reshape(devices, span // devices, columns), "ctx", 0, 0, tiled=True)

    dq = call(pair_kernel, [sds(wide)] * KV_HEADS, [], (keep, give))
    (query_grads,) = call(query_kernel, [sds((rows, Q_HEADS * HEAD_DIM))], [], along_heads(dq), after=(parts,))
    (input_grads,) = call(functools.partial(input_kernel, fsdp), [sds((rows, model))], [], (kv_grad, *w_parts), after=(parts,))
    (weight_grads,) = call(total_kernel, [sds((span // devices, columns), f32)], [], (sums,))
    return query_grads[None], input_grads[None], weight_grads


def solution(mesh):
    return jax.shard_map(
        shards,
        mesh=mesh,
        in_specs=(
            P("fsdp", "ctx", None),
            P("fsdp", "ctx", None),
            P("fsdp", "ctx", None),
            P("fsdp", "ctx", None),
            P("fsdp", None, "ctx"),
            P("fsdp", None),
            P("fsdp", None),
        ),
        out_specs=(P("fsdp", "ctx", None), P("fsdp", "ctx", None), P(("fsdp", "ctx"), None)),
        check_vma=False,
    )
```

```python
import functools

import jax
import jax.numpy as jnp
from jax import lax
from jax.experimental import pallas as pl
from jax.experimental.pallas import tpu as pltpu
from jax.sharding import PartitionSpec as P

Q_HEADS = 16
KV_HEADS = 4
HEAD_DIM = 64
GROUPS = Q_HEADS // KV_HEADS
KEY_WIDTH = KV_HEADS * HEAD_DIM
PAIR = 2 * HEAD_DIM
TEAM = 2 * KV_HEADS
GROUP = GROUPS * HEAD_DIM
SCALE = HEAD_DIM ** -0.5
LOWER = HEAD_DIM

NT = (((1,), (1,)), ((), ()))
TN = (((0,), (0,)), ((), ()))
VMEM = pl.BlockSpec(memory_space=pltpu.VMEM)
SMEM = pl.BlockSpec(memory_space=pltpu.SMEM)
ANY = pl.BlockSpec(memory_space=pl.ANY)
HBM = pl.BlockSpec(memory_space=pltpu.HBM)
PARAMS = pltpu.CompilerParams(vmem_limit_bytes=40 * 1024 * 1024)
WHOLE = pltpu.CompilerParams(vmem_limit_bytes=60 * 1024 * 1024)


def matmul(left, right, dims=(((1,), (0,)), ((), ()))):
    return lax.dot_general(left, right, dims, preferred_element_type=jnp.float32)


def swapped(array, axis, bits):
    size = lax.axis_size(axis)
    return lax.ppermute(array, axis, [(i, i ^ bits) for i in range(size)])


def call(kernel, out_shape, scratch, args, smem=0, hbm=0, after=()):
    given = len(args)
    params = WHOLE if hbm else PARAMS

    def body(*refs):
        kernel(*refs[:given], *refs[given + len(after):])

    specs = [SMEM] * smem + [HBM] * hbm + [VMEM] * (given - smem - hbm) + [ANY] * len(after)
    return pl.pallas_call(
        body,
        out_shape=out_shape,
        in_specs=specs,
        out_specs=[VMEM] * len(out_shape),
        scratch_shapes=scratch,
        compiler_params=params,
    )(*args, *after)


def held(array, after):
    def body(*refs):
        pass

    return pl.pallas_call(
        body,
        out_shape=sds(array.shape, array.dtype),
        in_specs=[ANY] * (1 + len(after)),
        out_specs=ANY,
        input_output_aliases={0: 0},
        compiler_params=PARAMS,
    )(array, *after)


def sds(shape, dtype=jnp.bfloat16):
    return jax.ShapeDtypeStruct(shape, dtype)


def head_side():
    me = lax.rem(lax.axis_index("ctx"), TEAM)
    return me // 2, lax.rem(me, 2)


def split(exact):
    first = exact.astype(jnp.bfloat16).astype(jnp.float32)
    second = (exact - first).astype(jnp.bfloat16).astype(jnp.float32)
    return first, second, exact - first - second


def pieces_kernel(q_ref, go_ref, ao_ref, lse_ref, *rest):
    out_refs, (grad, output, lse, stat, sems) = rest[:KV_HEADS], rest[KV_HEADS:]
    rows, width = q_ref.shape
    head, _ = head_side()
    loads = [pltpu.make_async_copy(ref, to, sems.at[i])
             for i, (ref, to) in enumerate(((go_ref, grad), (ao_ref, output), (lse_ref, lse)))]
    moves = []
    for m in range(KV_HEADS):
        columns = pl.ds(pl.multiple_of(jnp.bitwise_xor(head, m) * GROUP, GROUP), GROUP)
        for i, ref in enumerate((q_ref, go_ref)):
            moves.append(pltpu.make_async_copy(
                ref.at[:, columns], out_refs[m].at[0:rows, i * GROUP:(i + 1) * GROUP], sems.at[3 + 2 * m + i]))
    for copy in loads + moves:
        copy.start()
    for copy in loads:
        copy.wait()
    product = grad[...].astype(jnp.float32) * output[...].astype(jnp.float32)
    high = product.astype(jnp.bfloat16)
    low = (product - high.astype(jnp.float32)).astype(jnp.bfloat16)
    head_of = lax.broadcasted_iota(jnp.int32, (Q_HEADS, width), 1) // HEAD_DIM
    ones = (head_of == lax.broadcasted_iota(jnp.int32, (Q_HEADS, width), 0)).astype(jnp.bfloat16)
    delta = matmul(ones, high, NT) + matmul(ones, low, NT)
    for g in range(KV_HEADS):
        part = slice(g * GROUPS, (g + 1) * GROUPS)
        stat[g] = jnp.concatenate([lse[part, :], delta[part, :]], axis=0)
    zero = jnp.zeros((2 * GROUPS, rows), jnp.float32)
    for m in range(KV_HEADS):
        lines = [*split(stat[jnp.bitwise_xor(head, m)]), zero]
        for i, one in enumerate(lines):
            full = jnp.concatenate([one, zero], axis=0).astype(jnp.bfloat16)
            out_refs[m][rows:, i * rows:(i + 1) * rows] = full
    for copy in moves:
        copy.wait()


def hidden_kernel(fsdp, hid_ref, *rest):
    near_refs, far_ref, sems = rest[:fsdp // 2], rest[fsdp // 2], rest[fsdp // 2 + 1]
    mine = lax.axis_index("fsdp")
    span = far_ref.shape[2]
    copies = []
    for m in range(fsdp):
        columns = pl.ds(pl.multiple_of(jnp.bitwise_xor(mine, m) * span, span), span)
        to = near_refs[m] if m < fsdp // 2 else far_ref.at[m - fsdp // 2]
        copies.append(pltpu.make_async_copy(hid_ref.at[:, columns], to, sems.at[m]))
    for copy in copies:
        copy.start()
    for copy in copies:
        copy.wait()


def project_kernel(fsdp, hid_ref, *rest):
    w_refs, out_refs, (parts,) = rest[:fsdp], rest[fsdp:fsdp + KV_HEADS], rest[fsdp + KV_HEADS:]
    mine = lax.axis_index("fsdp")
    head, _ = head_side()
    span = w_refs[0].shape[0]
    total = None
    for m in range(fsdp):
        start = pl.multiple_of(jnp.bitwise_xor(mine, m) * span, span)
        term = matmul(hid_ref[:, pl.ds(start, span)], w_refs[m][...])
        total = term if total is None else total + term
    low = total.astype(jnp.bfloat16)
    for g in range(KV_HEADS):
        key = low[:, g * HEAD_DIM:(g + 1) * HEAD_DIM]
        value = low[:, KEY_WIDTH + g * HEAD_DIM:KEY_WIDTH + (g + 1) * HEAD_DIM]
        parts[g] = jnp.concatenate([key, value], axis=1)
    for m in range(KV_HEADS):
        out_refs[m][...] = parts[jnp.bitwise_xor(head, m)]


def lower_half(shape):
    return lax.broadcasted_iota(jnp.int32, shape, len(shape) - 1) < LOWER


def stacked(key_value):
    wide = key_value.astype(jnp.float32)
    turned = pltpu.roll(wide, LOWER, 1)
    lower = lower_half(wide.shape)
    zero = jnp.zeros_like(wide)
    keys = jnp.concatenate([jnp.where(lower, wide, zero), jnp.where(lower, zero, turned)], axis=0) * SCALE
    values = jnp.concatenate([jnp.where(lower, turned, zero), jnp.where(lower, zero, wide)], axis=0)
    return keys.astype(jnp.bfloat16), values.astype(jnp.bfloat16)


def tile(keys, values, query, grad, stats, mask):
    size = keys.shape[0] // 2
    lse, delta = stats[:2], stats[2:]
    scores = matmul(keys, query, NT)
    prob_grad = matmul(values, grad, NT)
    lows, grads = [], []
    for head in range(2):
        part = slice(head * size, (head + 1) * size)
        probs = jnp.exp(scores[part] - lse[head])
        if mask is not None:
            probs = jnp.where(mask, probs, 0.0)
        lows.append(probs.astype(jnp.bfloat16))
        grads.append((probs * (prob_grad[part] - delta[head])).astype(jnp.bfloat16))
    low, score_grad = jnp.concatenate(lows, axis=0), jnp.concatenate(grads, axis=0)
    return matmul(score_grad, query), matmul(low, grad), matmul(score_grad, keys, TN)


def folded(key_sum, value_sum):
    size = key_sum.shape[0] // 2
    lower = lower_half((size, PAIR))
    straight = jnp.where(lower, key_sum[:size], value_sum[size:])
    crossed = jnp.where(lower, value_sum[:size], key_sum[size:])
    return (straight + pltpu.roll(crossed, LOWER, 1)) * jnp.where(lower, SCALE, 1.0)


def unpacked(part, rows):
    exact = part[rows:, 0:3 * rows].astype(jnp.float32)[0:2 * GROUPS]
    return exact[:, 0:rows] + exact[:, rows:2 * rows] + exact[:, 2 * rows:]


def pair_stats(stat, pair):
    first = 2 * pair
    return [stat[first:first + 1], stat[first + 1:first + 2],
            stat[GROUPS + first:GROUPS + first + 1], stat[GROUPS + first + 1:GROUPS + first + 2]]


def sequence_kernel(order_ref, *rest):
    qd_refs, kv_refs, rest = rest[:TEAM], rest[TEAM:TEAM + KV_HEADS], rest[TEAM + KV_HEADS:]
    dkv_refs, keep_ref, send_ref, rest = rest[:KV_HEADS], rest[KV_HEADS], rest[KV_HEADS + 1], rest[KV_HEADS + 2:]
    q_all, go_all, stat_all, key_all, value_all, dq_all, dkv_all = rest
    rows = kv_refs[0].shape[0]
    head, side = head_side()
    near = [order_ref[0, 2 * jnp.bitwise_xor(head, m) + side] for m in range(KV_HEADS)]
    far = [order_ref[0, 2 * jnp.bitwise_xor(head, m) + 1 - side] for m in range(KV_HEADS)]
    for place, ref in zip(near + far, qd_refs):
        q_all[place] = ref[0:rows, 0:GROUP]
        go_all[place] = ref[0:rows, GROUP:]
        stat_all[place] = unpacked(ref, rows)
    for place, ref in zip(near, kv_refs):
        key_all[place], value_all[place] = stacked(ref[...])
    dq_all[...] = jnp.zeros_like(dq_all)
    for block in range(TEAM):
        mine = functools.reduce(jnp.logical_or, [place == block for place in near])

        @pl.when(mine)
        def _():
            count = TEAM - block
            shape = (rows, count * rows)
            mask = lax.broadcasted_iota(jnp.int32, shape, 0) <= lax.broadcasted_iota(jnp.int32, shape, 1)
            stats = jnp.concatenate([stat_all[i] for i in range(block, TEAM)], axis=1)
            key_sum = value_sum = None
            for pair in range(GROUPS // 2):
                columns = slice(pair * PAIR, (pair + 1) * PAIR)
                query = q_all[block:, :, columns].reshape(count * rows, PAIR)
                grad = go_all[block:, :, columns].reshape(count * rows, PAIR)
                key_part, value_part, query_part = tile(
                    key_all[block], value_all[block], query, grad, pair_stats(stats, pair), mask)
                key_sum = key_part if key_sum is None else key_sum + key_part
                value_sum = value_part if value_sum is None else value_sum + value_part
                dq_all[block:, :, columns] += query_part.reshape(count, rows, PAIR)
            dkv_all[block] = folded(key_sum, value_sum)

    for m in range(KV_HEADS):
        dkv_refs[m][...] = dkv_all[near[m]].astype(jnp.bfloat16)
        keep_ref[m] = dq_all[near[m]]
        send_ref[m] = dq_all[far[m]].astype(jnp.bfloat16)


def teams_kernel(order_ref, qd_ref, kv_ref, dkv_ref, keep_ref, send_ref, dq_all):
    rows = kv_ref.shape[1]
    head, side = head_side()
    base = lax.axis_index("ctx") // TEAM * TEAM
    dq_all[...] = jnp.zeros_like(dq_all)

    @pl.loop(0, kv_ref.shape[0])
    def _(block):
        keys, values = stacked(kv_ref[block])
        dkv_ref[block] = jnp.zeros((rows, PAIR), jnp.float32)
        stored = block // KV_HEADS * TEAM + 2 * jnp.bitwise_xor(head, lax.rem(block, KV_HEADS)) + side
        place = order_ref[0, stored]

        @pl.loop(0, TEAM)
        def _(at):
            turned = jnp.where(at < KV_HEADS, side, 1 - side)
            own = order_ref[0, base + 2 * jnp.bitwise_xor(head, lax.rem(at, KV_HEADS)) + turned]

            @pl.when(place <= own)
            def _():
                shape = (rows, rows)
                mask = (place * rows + lax.broadcasted_iota(jnp.int32, shape, 0)
                        <= own * rows + lax.broadcasted_iota(jnp.int32, shape, 1))
                one = qd_ref.at[at]
                stats = unpacked(one, rows)
                for pair in range(GROUPS // 2):
                    first = pair * PAIR
                    key_part, value_part, query_part = tile(
                        keys, values, one[0:rows, first:first + PAIR], one[0:rows, GROUP + first:GROUP + first + PAIR],
                        pair_stats(stats, pair), mask)
                    dq_all[at, :, first:first + PAIR] += query_part
                    dkv_ref[block] += folded(key_part, value_part)

    keep_ref[...] = dq_all[0:KV_HEADS]
    send_ref[...] = dq_all[KV_HEADS:].astype(jnp.bfloat16)


def owner_kernel(*rest):
    dkv_refs, out_ref, parts = rest[:KV_HEADS], rest[KV_HEADS], rest[KV_HEADS + 1]
    head, _ = head_side()
    for m in range(KV_HEADS):
        parts[jnp.bitwise_xor(head, m)] = dkv_refs[m][...]
    keys = [parts[g, :, :HEAD_DIM] for g in range(KV_HEADS)]
    values = [parts[g, :, HEAD_DIM:] for g in range(KV_HEADS)]
    out_ref[...] = jnp.concatenate(keys + values, axis=1)


def pair_kernel(keep_ref, got_ref, *out_refs):
    for m in range(KV_HEADS):
        out_refs[m][...] = (keep_ref[m] + got_ref[m].astype(jnp.float32)).astype(out_refs[m].dtype)


def query_kernel(*rest):
    dq_refs, out_ref = rest[:KV_HEADS], rest[KV_HEADS]
    head, _ = head_side()
    for m in range(KV_HEADS):
        columns = pl.ds(pl.multiple_of(jnp.bitwise_xor(head, m) * GROUP, GROUP), GROUP)
        out_ref[:, columns] = dq_refs[m][...]


def input_kernel(fsdp, grad_ref, *rest):
    w_refs, out_ref = rest[:fsdp], rest[fsdp]
    mine = lax.axis_index("fsdp")
    span = w_refs[0].shape[0]
    for m in range(fsdp):
        start = pl.multiple_of(jnp.bitwise_xor(mine, m) * span, span)
        out_ref[:, pl.ds(start, span)] = matmul(grad_ref[...], w_refs[m][...], NT).astype(jnp.bfloat16)


def weight_sums(fsdp, refs):
    hid = jnp.concatenate([ref[...] for ref in refs[:fsdp]], axis=0)
    grad = jnp.concatenate([ref[...] for ref in refs[fsdp:2 * fsdp]], axis=0)
    return matmul(hid, grad, TN)


def weight_kernel(fsdp, *rest):
    rest[2 * fsdp][...] = weight_sums(fsdp, rest).astype(jnp.bfloat16)


def sides_kernel(fsdp, *rest):
    keep_ref, send_ref, parts = rest[2 * fsdp:]
    head, side = head_side()
    parts[...] = weight_sums(fsdp, rest).reshape(parts.shape)
    for m in range(KV_HEADS):
        to = 2 * jnp.bitwise_xor(head, m)
        keep_ref[m] = parts[to + side]
        send_ref[m] = parts[to + 1 - side].astype(jnp.bfloat16)


def own_total_kernel(own_ref, *rest):
    total = own_ref[...]
    for ref in rest[:-1]:
        total = total + ref[...].astype(jnp.float32)
    rest[-1][...] = total


def total_kernel(part_ref, out_ref):
    total = part_ref[0].astype(jnp.float32)
    for i in range(1, part_ref.shape[0]):
        total = total + part_ref[i].astype(jnp.float32)
    out_ref[...] = total


def over_fsdp(own, bits):
    got = list(own)
    while bits:
        for m in range(len(own)):
            if m & bits:
                got[m] = swapped(got[m], "fsdp", bits)
        bits //= 2
    return got


def shards(hidden, queries, attn_out, grad_out, log_sums, block_order, w_kv):
    rows, model = hidden.shape[1:]
    fsdp, devices = lax.axis_size("fsdp"), lax.axis_size("ctx")
    teams = devices // TEAM
    f32 = jnp.float32
    span = model // fsdp
    inputs = hidden[0]
    columns = 2 * KEY_WIDTH
    block, wide = (rows, PAIR), (rows, GROUP)

    def along_heads(arrays):
        return [arrays[0]] + [swapped(arrays[m], "ctx", 2 * m) for m in range(1, KV_HEADS)]

    far = fsdp // 2
    qd = call(
        pieces_kernel, [sds((rows + 16, 2 * GROUP))] * KV_HEADS,
        [pltpu.VMEM((rows, Q_HEADS * HEAD_DIM), jnp.bfloat16)] * 2
        + [pltpu.VMEM((Q_HEADS, rows), f32), pltpu.VMEM((KV_HEADS, 2 * GROUPS, rows), f32),
           pltpu.SemaphoreType.DMA((3 + 2 * KV_HEADS,))],
        (queries[0], grad_out[0], attn_out[0], log_sums[0]), hbm=4)
    qd = along_heads(qd)
    qd = qd + [swapped(one, "ctx", 1) for one in qd]
    *hid, hid_far = call(
        functools.partial(hidden_kernel, fsdp), [sds((rows, span))] * far + [sds((fsdp - far, rows, span))],
        [pltpu.SemaphoreType.DMA((fsdp,))], (inputs,), hbm=1)
    w_far = held(swapped(w_kv, "fsdp", far), (*qd[1:KV_HEADS + 3], hid_far))
    w_parts = over_fsdp([w_kv] * far + [w_far] * (fsdp - far), far // 2)

    kv = call(
        functools.partial(project_kernel, fsdp), [sds(block)] * KV_HEADS,
        [pltpu.VMEM((KV_HEADS,) + block, jnp.bfloat16)], (inputs, *w_parts))
    kv = along_heads(kv)

    hid_far = swapped(hid_far, "fsdp", far)
    hid = over_fsdp(hid + [hid_far[m] for m in range(fsdp - far)], far // 2)

    half = (KV_HEADS,) + wide
    if teams == 1:
        *dkv, keep, give = call(
            sequence_kernel, [sds(block)] * KV_HEADS + [sds(half, f32), sds(half)],
            [pltpu.VMEM((TEAM,) + wide, jnp.bfloat16)] * 2 + [pltpu.VMEM((TEAM, 2 * GROUPS, rows), f32)]
            + [pltpu.VMEM((TEAM, 2 * rows, PAIR), jnp.bfloat16)] * 2
            + [pltpu.VMEM((TEAM,) + wide, f32), pltpu.VMEM((TEAM,) + block, f32)],
            (block_order, *qd, *kv), smem=1, after=(hid_far,))
    else:
        alike = [[t * TEAM + i for t in range(teams)] for i in range(TEAM)]
        kv = lax.all_gather(jnp.stack(kv), "ctx", axis_index_groups=alike, axis=0, tiled=True)
        dkv, keep, give = call(
            teams_kernel, [sds((teams * KV_HEADS,) + block, f32), sds(half, f32), sds(half)],
            [pltpu.VMEM((TEAM,) + wide, f32)], (block_order, jnp.stack(qd), kv), smem=1)
        dkv = lax.psum_scatter(dkv, "ctx", axis_index_groups=alike, scatter_dimension=0, tiled=True)
        dkv = [dkv[m].astype(jnp.bfloat16) for m in range(KV_HEADS)]

    dkv = along_heads(dkv)
    give = swapped(held(give, dkv[1:]), "ctx", 1)
    (kv_grad,) = call(
        owner_kernel, [sds((rows, columns))], [pltpu.VMEM((KV_HEADS,) + block, jnp.bfloat16)],
        dkv)
    grads = over_fsdp([kv_grad] * fsdp, far)
    if teams == 1:
        share = (span // devices, columns)
        own_sums, send_sums = call(
            functools.partial(sides_kernel, fsdp), [sds((KV_HEADS,) + share, f32), sds((KV_HEADS,) + share)],
            [pltpu.VMEM((devices,) + share, f32)], (*hid, *grads))
        formed = (own_sums,)
        dq = along_heads(call(pair_kernel, [sds(wide)] * KV_HEADS, [], (keep, give), after=formed))
        sums = call(
            pair_kernel, [sds(share, f32)] + [sds(share)] * (KV_HEADS - 1), [],
            (own_sums, swapped(send_sums, "ctx", 1)), after=dq[1:])
        (weight_grads,) = call(own_total_kernel, [sds(share, f32)], [], along_heads(sums))
    else:
        formed = call(functools.partial(weight_kernel, fsdp), [sds((span, columns))], [], (*hid, *grads))
        dq = along_heads(call(pair_kernel, [sds(wide)] * KV_HEADS, [], (keep, give), after=formed))
        sums = lax.all_to_all(formed[0].reshape(devices, span // devices, columns), "ctx", 0, 0, tiled=True)
        (weight_grads,) = call(total_kernel, [sds((span // devices, columns), f32)], [], (sums,))
    (query_grads,) = call(query_kernel, [sds((rows, Q_HEADS * HEAD_DIM))], [], dq, after=formed)
    (input_grads,) = call(
        functools.partial(input_kernel, fsdp), [sds((rows, model))], [], (kv_grad, *w_parts), after=formed)
    return query_grads[None], input_grads[None], weight_grads


def solution(mesh):
    return jax.shard_map(
        shards,
        mesh=mesh,
        in_specs=(
            P("fsdp", "ctx", None),
            P("fsdp", "ctx", None),
            P("fsdp", "ctx", None),
            P("fsdp", "ctx", None),
            P("fsdp", None, "ctx"),
            P("fsdp", None),
            P("fsdp", None),
        ),
        out_specs=(P("fsdp", "ctx", None), P("fsdp", "ctx", None), P(("fsdp", "ctx"), None)),
        check_vma=False,
    )
```

```python
import functools

import jax
import jax.numpy as jnp
from jax import lax
from jax.experimental import pallas as pl
from jax.experimental.pallas import tpu as pltpu
from jax.sharding import PartitionSpec as P

Q_HEADS = 16
KV_HEADS = 4
HEAD_DIM = 64
GROUPS = Q_HEADS // KV_HEADS
KEY_WIDTH = KV_HEADS * HEAD_DIM
PAIR = 2 * HEAD_DIM
TEAM = 2 * KV_HEADS
GROUP = GROUPS * HEAD_DIM
SCALE = HEAD_DIM ** -0.5
LOWER = HEAD_DIM

NT = (((1,), (1,)), ((), ()))
TN = (((0,), (0,)), ((), ()))
VMEM = pl.BlockSpec(memory_space=pltpu.VMEM)
SMEM = pl.BlockSpec(memory_space=pltpu.SMEM)
ANY = pl.BlockSpec(memory_space=pl.ANY)
HBM = pl.BlockSpec(memory_space=pltpu.HBM)
PARAMS = pltpu.CompilerParams(vmem_limit_bytes=40 * 1024 * 1024)
WHOLE = pltpu.CompilerParams(vmem_limit_bytes=60 * 1024 * 1024)


def matmul(left, right, dims=(((1,), (0,)), ((), ()))):
    return lax.dot_general(left, right, dims, preferred_element_type=jnp.float32)


def swapped(array, axis, bits):
    size = lax.axis_size(axis)
    return lax.ppermute(array, axis, [(i, i ^ bits) for i in range(size)])


def call(kernel, out_shape, scratch, args, smem=0, hbm=0, after=()):
    given = len(args)
    params = WHOLE if hbm == given else PARAMS

    def body(*refs):
        kernel(*refs[:given], *refs[given + len(after):])

    specs = [SMEM] * smem + [HBM] * hbm + [VMEM] * (given - smem - hbm) + [ANY] * len(after)
    return pl.pallas_call(
        body,
        out_shape=out_shape,
        in_specs=specs,
        out_specs=[VMEM] * len(out_shape),
        scratch_shapes=scratch,
        compiler_params=params,
    )(*args, *after)


def held(array, after):
    def body(*refs):
        pass

    return pl.pallas_call(
        body,
        out_shape=sds(array.shape, array.dtype),
        in_specs=[ANY] * (1 + len(after)),
        out_specs=ANY,
        input_output_aliases={0: 0},
        compiler_params=PARAMS,
    )(array, *after)


def sds(shape, dtype=jnp.bfloat16):
    return jax.ShapeDtypeStruct(shape, dtype)


def head_side():
    me = lax.rem(lax.axis_index("ctx"), TEAM)
    return me // 2, lax.rem(me, 2)


def split(exact):
    first = exact.astype(jnp.bfloat16).astype(jnp.float32)
    second = (exact - first).astype(jnp.bfloat16).astype(jnp.float32)
    return first, second, exact - first - second


def pieces_kernel(q_ref, go_ref, ao_ref, lse_ref, *rest):
    out_refs, (grad, output, lse, stat, sems) = rest[:KV_HEADS], rest[KV_HEADS:]
    rows, width = q_ref.shape
    head, _ = head_side()
    loads = [pltpu.make_async_copy(ref, to, sems.at[i])
             for i, (ref, to) in enumerate(((go_ref, grad), (ao_ref, output), (lse_ref, lse)))]
    moves = []
    for m in range(KV_HEADS):
        columns = pl.ds(pl.multiple_of(jnp.bitwise_xor(head, m) * GROUP, GROUP), GROUP)
        for i, ref in enumerate((q_ref, go_ref)):
            moves.append(pltpu.make_async_copy(
                ref.at[:, columns], out_refs[m].at[0:rows, i * GROUP:(i + 1) * GROUP], sems.at[3 + 2 * m + i]))
    for copy in loads + moves:
        copy.start()
    for copy in loads:
        copy.wait()
    product = grad[...].astype(jnp.float32) * output[...].astype(jnp.float32)
    high = product.astype(jnp.bfloat16)
    low = (product - high.astype(jnp.float32)).astype(jnp.bfloat16)
    head_of = lax.broadcasted_iota(jnp.int32, (Q_HEADS, width), 1) // HEAD_DIM
    ones = (head_of == lax.broadcasted_iota(jnp.int32, (Q_HEADS, width), 0)).astype(jnp.bfloat16)
    delta = matmul(ones, high, NT) + matmul(ones, low, NT)
    for g in range(KV_HEADS):
        part = slice(g * GROUPS, (g + 1) * GROUPS)
        stat[g] = jnp.concatenate([lse[part, :], delta[part, :]], axis=0)
    zero = jnp.zeros((2 * GROUPS, rows), jnp.float32)
    for m in range(KV_HEADS):
        lines = [*split(stat[jnp.bitwise_xor(head, m)]), zero]
        for i, one in enumerate(lines):
            full = jnp.concatenate([one, zero], axis=0).astype(jnp.bfloat16)
            out_refs[m][rows:, i * rows:(i + 1) * rows] = full
    for copy in moves:
        copy.wait()


def hidden_moves(hid_ref, near_refs, far_ref, sems):
    mine = lax.axis_index("fsdp")
    near = len(near_refs)
    span = far_ref.shape[2]
    copies = []
    for m in range(near + far_ref.shape[0]):
        columns = pl.ds(pl.multiple_of(jnp.bitwise_xor(mine, m) * span, span), span)
        to = near_refs[m] if m < near else far_ref.at[m - near]
        copies.append(pltpu.make_async_copy(hid_ref.at[:, columns], to, sems.at[m]))
    for copy in copies:
        copy.start()
    return copies


def hidden_kernel(hid_ref, *rest):
    for copy in hidden_moves(hid_ref, rest[:-2], *rest[-2:]):
        copy.wait()


def project_kernel(fsdp, hid_ref, *rest):
    w_refs, out_refs, (parts,) = rest[:fsdp], rest[fsdp:fsdp + KV_HEADS], rest[fsdp + KV_HEADS:]
    mine = lax.axis_index("fsdp")
    head, _ = head_side()
    span = w_refs[0].shape[0]
    total = None
    for m in range(fsdp):
        start = pl.multiple_of(jnp.bitwise_xor(mine, m) * span, span)
        term = matmul(hid_ref[:, pl.ds(start, span)], w_refs[m][...])
        total = term if total is None else total + term
    low = total.astype(jnp.bfloat16)
    for g in range(KV_HEADS):
        key = low[:, g * HEAD_DIM:(g + 1) * HEAD_DIM]
        value = low[:, KEY_WIDTH + g * HEAD_DIM:KEY_WIDTH + (g + 1) * HEAD_DIM]
        parts[g] = jnp.concatenate([key, value], axis=1)
    for m in range(KV_HEADS):
        out_refs[m][...] = parts[jnp.bitwise_xor(head, m)]


def lower_half(shape):
    return lax.broadcasted_iota(jnp.int32, shape, len(shape) - 1) < LOWER


def stacked(key_value):
    wide = key_value.astype(jnp.float32)
    turned = pltpu.roll(wide, LOWER, 1)
    lower = lower_half(wide.shape)
    zero = jnp.zeros_like(wide)
    keys = jnp.concatenate([jnp.where(lower, wide, zero), jnp.where(lower, zero, turned)], axis=0) * SCALE
    values = jnp.concatenate([jnp.where(lower, turned, zero), jnp.where(lower, zero, wide)], axis=0)
    return keys.astype(jnp.bfloat16), values.astype(jnp.bfloat16)


def tile(keys, values, query, grad, stats, mask):
    size = keys.shape[0] // 2
    lse, delta = stats[:2], stats[2:]
    scores = matmul(keys, query, NT)
    prob_grad = matmul(values, grad, NT)
    lows, grads = [], []
    for head in range(2):
        part = slice(head * size, (head + 1) * size)
        probs = jnp.exp(scores[part] - lse[head])
        if mask is not None:
            probs = jnp.where(mask, probs, 0.0)
        lows.append(probs.astype(jnp.bfloat16))
        grads.append((probs * (prob_grad[part] - delta[head])).astype(jnp.bfloat16))
    low, score_grad = jnp.concatenate(lows, axis=0), jnp.concatenate(grads, axis=0)
    return matmul(score_grad, query), matmul(low, grad), matmul(score_grad, keys, TN)


def folded(key_sum, value_sum):
    size = key_sum.shape[0] // 2
    lower = lower_half((size, PAIR))
    straight = jnp.where(lower, key_sum[:size], value_sum[size:])
    crossed = jnp.where(lower, value_sum[:size], key_sum[size:])
    return (straight + pltpu.roll(crossed, LOWER, 1)) * jnp.where(lower, SCALE, 1.0)


def unpacked(part, rows):
    exact = part[rows:, 0:3 * rows].astype(jnp.float32)[0:2 * GROUPS]
    return exact[:, 0:rows] + exact[:, rows:2 * rows] + exact[:, 2 * rows:]


def pair_stats(stat, pair):
    first = 2 * pair
    return [stat[first:first + 1], stat[first + 1:first + 2],
            stat[GROUPS + first:GROUPS + first + 1], stat[GROUPS + first + 1:GROUPS + first + 2]]


def sequence_kernel(near_parts, order_ref, hid_ref, *rest):
    qd_refs, kv_refs, rest = rest[:TEAM], rest[TEAM:TEAM + KV_HEADS], rest[TEAM + KV_HEADS:]
    dkv_refs, keep_ref, send_ref, rest = rest[:KV_HEADS], rest[KV_HEADS], rest[KV_HEADS + 1], rest[KV_HEADS + 2:]
    near_refs, far_ref, rest = rest[:near_parts], rest[near_parts], rest[near_parts + 1:]
    q_all, go_all, stat_all, key_all, value_all, dq_all, dkv_all, sems = rest
    moves = hidden_moves(hid_ref, near_refs, far_ref, sems)
    rows = kv_refs[0].shape[0]
    head, side = head_side()
    near = [order_ref[0, 2 * jnp.bitwise_xor(head, m) + side] for m in range(KV_HEADS)]
    far = [order_ref[0, 2 * jnp.bitwise_xor(head, m) + 1 - side] for m in range(KV_HEADS)]
    for place, ref in zip(near + far, qd_refs):
        q_all[place] = ref[0:rows, 0:GROUP]
        go_all[place] = ref[0:rows, GROUP:]
        stat_all[place] = unpacked(ref, rows)
    for place, ref in zip(near, kv_refs):
        key_all[place], value_all[place] = stacked(ref[...])
    dq_all[...] = jnp.zeros_like(dq_all)
    for block in range(TEAM):
        mine = functools.reduce(jnp.logical_or, [place == block for place in near])

        @pl.when(mine)
        def _():
            count = TEAM - block
            shape = (rows, count * rows)
            mask = lax.broadcasted_iota(jnp.int32, shape, 0) <= lax.broadcasted_iota(jnp.int32, shape, 1)
            stats = jnp.concatenate([stat_all[i] for i in range(block, TEAM)], axis=1)
            key_sum = value_sum = None
            for pair in range(GROUPS // 2):
                columns = slice(pair * PAIR, (pair + 1) * PAIR)
                query = q_all[block:, :, columns].reshape(count * rows, PAIR)
                grad = go_all[block:, :, columns].reshape(count * rows, PAIR)
                key_part, value_part, query_part = tile(
                    key_all[block], value_all[block], query, grad, pair_stats(stats, pair), mask)
                key_sum = key_part if key_sum is None else key_sum + key_part
                value_sum = value_part if value_sum is None else value_sum + value_part
                dq_all[block:, :, columns] += query_part.reshape(count, rows, PAIR)
            dkv_all[block] = folded(key_sum, value_sum)

    for m in range(KV_HEADS):
        dkv_refs[m][...] = dkv_all[near[m]].astype(jnp.bfloat16)
        keep_ref[m] = dq_all[near[m]]
        send_ref[m] = dq_all[far[m]].astype(jnp.bfloat16)
    for copy in moves:
        copy.wait()


def teams_kernel(order_ref, qd_ref, kv_ref, dkv_ref, keep_ref, send_ref, dq_all):
    rows = kv_ref.shape[1]
    head, side = head_side()
    base = lax.axis_index("ctx") // TEAM * TEAM
    dq_all[...] = jnp.zeros_like(dq_all)

    @pl.loop(0, kv_ref.shape[0])
    def _(block):
        keys, values = stacked(kv_ref[block])
        dkv_ref[block] = jnp.zeros((rows, PAIR), jnp.float32)
        stored = block // KV_HEADS * TEAM + 2 * jnp.bitwise_xor(head, lax.rem(block, KV_HEADS)) + side
        place = order_ref[0, stored]

        @pl.loop(0, TEAM)
        def _(at):
            turned = jnp.where(at < KV_HEADS, side, 1 - side)
            own = order_ref[0, base + 2 * jnp.bitwise_xor(head, lax.rem(at, KV_HEADS)) + turned]

            @pl.when(place <= own)
            def _():
                shape = (rows, rows)
                mask = (place * rows + lax.broadcasted_iota(jnp.int32, shape, 0)
                        <= own * rows + lax.broadcasted_iota(jnp.int32, shape, 1))
                one = qd_ref.at[at]
                stats = unpacked(one, rows)
                for pair in range(GROUPS // 2):
                    first = pair * PAIR
                    key_part, value_part, query_part = tile(
                        keys, values, one[0:rows, first:first + PAIR], one[0:rows, GROUP + first:GROUP + first + PAIR],
                        pair_stats(stats, pair), mask)
                    dq_all[at, :, first:first + PAIR] += query_part
                    dkv_ref[block] += folded(key_part, value_part)

    keep_ref[...] = dq_all[0:KV_HEADS]
    send_ref[...] = dq_all[KV_HEADS:].astype(jnp.bfloat16)


def owner_kernel(*rest):
    dkv_refs, out_ref, parts = rest[:KV_HEADS], rest[KV_HEADS], rest[KV_HEADS + 1]
    head, _ = head_side()
    for m in range(KV_HEADS):
        parts[jnp.bitwise_xor(head, m)] = dkv_refs[m][...]
    keys = [parts[g, :, :HEAD_DIM] for g in range(KV_HEADS)]
    values = [parts[g, :, HEAD_DIM:] for g in range(KV_HEADS)]
    out_ref[...] = jnp.concatenate(keys + values, axis=1)


def pair_kernel(keep_ref, got_ref, *out_refs):
    for m in range(KV_HEADS):
        out_refs[m][...] = (keep_ref[m] + got_ref[m].astype(jnp.float32)).astype(out_refs[m].dtype)


def query_kernel(*rest):
    dq_refs, out_ref = rest[:KV_HEADS], rest[KV_HEADS]
    head, _ = head_side()
    for m in range(KV_HEADS):
        columns = pl.ds(pl.multiple_of(jnp.bitwise_xor(head, m) * GROUP, GROUP), GROUP)
        out_ref[:, columns] = dq_refs[m][...]


def input_kernel(fsdp, grad_ref, *rest):
    w_refs, out_ref = rest[:fsdp], rest[fsdp]
    mine = lax.axis_index("fsdp")
    span = w_refs[0].shape[0]
    for m in range(fsdp):
        start = pl.multiple_of(jnp.bitwise_xor(mine, m) * span, span)
        out_ref[:, pl.ds(start, span)] = matmul(grad_ref[...], w_refs[m][...], NT).astype(jnp.bfloat16)


def weight_sums(fsdp, refs):
    hid = jnp.concatenate([ref[...] for ref in refs[:fsdp]], axis=0)
    grad = jnp.concatenate([ref[...] for ref in refs[fsdp:2 * fsdp]], axis=0)
    return matmul(hid, grad, TN)


def weight_kernel(fsdp, *rest):
    rest[2 * fsdp][...] = weight_sums(fsdp, rest).astype(jnp.bfloat16)


def sides_kernel(fsdp, *rest):
    keep_ref, send_ref, parts = rest[2 * fsdp:]
    head, side = head_side()
    parts[...] = weight_sums(fsdp, rest).reshape(parts.shape)
    for m in range(KV_HEADS):
        to = 2 * jnp.bitwise_xor(head, m)
        keep_ref[m] = parts[to + side]
        send_ref[m] = parts[to + 1 - side].astype(jnp.bfloat16)


def own_total_kernel(own_ref, *rest):
    total = own_ref[...]
    for ref in rest[:-1]:
        total = total + ref[...].astype(jnp.float32)
    rest[-1][...] = total


def total_kernel(part_ref, out_ref):
    total = part_ref[0].astype(jnp.float32)
    for i in range(1, part_ref.shape[0]):
        total = total + part_ref[i].astype(jnp.float32)
    out_ref[...] = total


def over_fsdp(own, bits):
    got = list(own)
    while bits:
        for m in range(len(own)):
            if m & bits:
                got[m] = swapped(got[m], "fsdp", bits)
        bits //= 2
    return got


def shards(hidden, queries, attn_out, grad_out, log_sums, block_order, w_kv):
    rows, model = hidden.shape[1:]
    fsdp, devices = lax.axis_size("fsdp"), lax.axis_size("ctx")
    teams = devices // TEAM
    f32 = jnp.float32
    span = model // fsdp
    inputs = hidden[0]
    columns = 2 * KEY_WIDTH
    block, wide = (rows, PAIR), (rows, GROUP)

    def along_heads(arrays):
        return [arrays[0]] + [swapped(arrays[m], "ctx", 2 * m) for m in range(1, KV_HEADS)]

    far = fsdp // 2
    qd = call(
        pieces_kernel, [sds((rows + 16, 2 * GROUP))] * KV_HEADS,
        [pltpu.VMEM((rows, Q_HEADS * HEAD_DIM), jnp.bfloat16)] * 2
        + [pltpu.VMEM((Q_HEADS, rows), f32), pltpu.VMEM((KV_HEADS, 2 * GROUPS, rows), f32),
           pltpu.SemaphoreType.DMA((3 + 2 * KV_HEADS,))],
        (queries[0], grad_out[0], attn_out[0], log_sums[0]), hbm=4)
    qd = along_heads(qd)
    turned = [swapped(one, "ctx", 1) for one in qd[:2]]
    w_far = held(swapped(w_kv, "fsdp", far), (*qd[1:KV_HEADS - 1], turned[0]))
    w_parts = over_fsdp([w_kv] * far + [w_far] * (fsdp - far), far // 2)

    kv = call(
        functools.partial(project_kernel, fsdp), [sds(block)] * KV_HEADS,
        [pltpu.VMEM((KV_HEADS,) + block, jnp.bfloat16)], (inputs, *w_parts))
    own_kv, kv = kv[:1], along_heads(kv)
    late = [held(qd[2], own_kv), held(qd[3], kv[1:3])]
    qd = qd[:2] + late + turned + [swapped(one, "ctx", 1) for one in late]

    half = (KV_HEADS,) + wide
    cut = [sds((rows, span))] * far + [sds((fsdp - far, rows, span))]
    cut_sems = pltpu.SemaphoreType.DMA((fsdp,))
    if teams == 1:
        outs = call(
            functools.partial(sequence_kernel, far), [sds(block)] * KV_HEADS + [sds(half, f32), sds(half)] + cut,
            [pltpu.VMEM((TEAM,) + wide, jnp.bfloat16)] * 2 + [pltpu.VMEM((TEAM, 2 * GROUPS, rows), f32)]
            + [pltpu.VMEM((TEAM, 2 * rows, PAIR), jnp.bfloat16)] * 2
            + [pltpu.VMEM((TEAM,) + wide, f32), pltpu.VMEM((TEAM,) + block, f32), cut_sems],
            (block_order, inputs, *qd, *kv), smem=1, hbm=1)
        dkv, (keep, give, *hid, hid_far) = outs[:KV_HEADS], outs[KV_HEADS:]
    else:
        alike = [[t * TEAM + i for t in range(teams)] for i in range(TEAM)]
        kv = lax.all_gather(jnp.stack(kv), "ctx", axis_index_groups=alike, axis=0, tiled=True)
        dkv, keep, give = call(
            teams_kernel, [sds((teams * KV_HEADS,) + block, f32), sds(half, f32), sds(half)],
            [pltpu.VMEM((TEAM,) + wide, f32)], (block_order, jnp.stack(qd), kv), smem=1)
        dkv = lax.psum_scatter(dkv, "ctx", axis_index_groups=alike, scatter_dimension=0, tiled=True)
        dkv = [dkv[m].astype(jnp.bfloat16) for m in range(KV_HEADS)]
        *hid, hid_far = call(hidden_kernel, cut, [cut_sems], (inputs,), hbm=1)

    hid_far = swapped(hid_far, "fsdp", far)
    hid = over_fsdp(hid + [hid_far[m] for m in range(fsdp - far)], far // 2)
    dkv = along_heads(dkv)
    give = swapped(held(give, dkv[1:]), "ctx", 1)
    (kv_grad,) = call(
        owner_kernel, [sds((rows, columns))], [pltpu.VMEM((KV_HEADS,) + block, jnp.bfloat16)],
        dkv)
    grads = over_fsdp([kv_grad] * fsdp, far)
    if teams == 1:
        share = (span // devices, columns)
        own_sums, send_sums = call(
            functools.partial(sides_kernel, fsdp), [sds((KV_HEADS,) + share, f32), sds((KV_HEADS,) + share)],
            [pltpu.VMEM((devices,) + share, f32)], (*hid, *grads), after=(give,))
        formed = (own_sums,)
        dq = along_heads(call(pair_kernel, [sds(wide)] * KV_HEADS, [], (keep, give), after=formed))
        sums = call(
            pair_kernel, [sds(share, f32)] + [sds(share)] * (KV_HEADS - 1), [],
            (own_sums, swapped(send_sums, "ctx", 1)), after=dq[1:])
        (weight_grads,) = call(own_total_kernel, [sds(share, f32)], [], along_heads(sums))
    else:
        formed = call(functools.partial(weight_kernel, fsdp), [sds((span, columns))], [], (*hid, *grads))
        dq = along_heads(call(pair_kernel, [sds(wide)] * KV_HEADS, [], (keep, give), after=formed))
        sums = lax.all_to_all(formed[0].reshape(devices, span // devices, columns), "ctx", 0, 0, tiled=True)
        (weight_grads,) = call(total_kernel, [sds((span // devices, columns), f32)], [], (sums,))
    (query_grads,) = call(query_kernel, [sds((rows, Q_HEADS * HEAD_DIM))], [], dq, after=formed)
    (input_grads,) = call(
        functools.partial(input_kernel, fsdp), [sds((rows, model))], [], (kv_grad, *w_parts), after=formed)
    return query_grads[None], input_grads[None], weight_grads


def solution(mesh):
    return jax.shard_map(
        shards,
        mesh=mesh,
        in_specs=(
            P("fsdp", "ctx", None),
            P("fsdp", "ctx", None),
            P("fsdp", "ctx", None),
            P("fsdp", "ctx", None),
            P("fsdp", None, "ctx"),
            P("fsdp", None),
            P("fsdp", None),
        ),
        out_specs=(P("fsdp", "ctx", None), P("fsdp", "ctx", None), P(("fsdp", "ctx"), None)),
        check_vma=False,
    )
```

```python
import functools

import jax
import jax.numpy as jnp
from jax import lax
from jax.experimental import pallas as pl
from jax.experimental.pallas import tpu as pltpu
from jax.sharding import PartitionSpec as P

Q_HEADS = 16
KV_HEADS = 4
HEAD_DIM = 64
GROUPS = Q_HEADS // KV_HEADS
KEY_WIDTH = KV_HEADS * HEAD_DIM
PAIR = 2 * HEAD_DIM
TEAM = 2 * KV_HEADS
GROUP = GROUPS * HEAD_DIM
SCALE = HEAD_DIM ** -0.5
LOWER = HEAD_DIM

NT = (((1,), (1,)), ((), ()))
TN = (((0,), (0,)), ((), ()))
VMEM = pl.BlockSpec(memory_space=pltpu.VMEM)
SMEM = pl.BlockSpec(memory_space=pltpu.SMEM)
ANY = pl.BlockSpec(memory_space=pl.ANY)
HBM = pl.BlockSpec(memory_space=pltpu.HBM)
PARAMS = pltpu.CompilerParams(vmem_limit_bytes=40 * 1024 * 1024)
WHOLE = pltpu.CompilerParams(vmem_limit_bytes=60 * 1024 * 1024)


def matmul(left, right, dims=(((1,), (0,)), ((), ()))):
    return lax.dot_general(left, right, dims, preferred_element_type=jnp.float32)


def swapped(array, axis, bits):
    size = lax.axis_size(axis)
    return lax.ppermute(array, axis, [(i, i ^ bits) for i in range(size)])


def call(kernel, out_shape, scratch, args, smem=0, hbm=0, after=()):
    given = len(args)
    params = WHOLE if hbm == given else PARAMS

    def body(*refs):
        kernel(*refs[:given], *refs[given + len(after):])

    specs = [SMEM] * smem + [HBM] * hbm + [VMEM] * (given - smem - hbm) + [ANY] * len(after)
    return pl.pallas_call(
        body,
        out_shape=out_shape,
        in_specs=specs,
        out_specs=[VMEM] * len(out_shape),
        scratch_shapes=scratch,
        compiler_params=params,
    )(*args, *after)


def held(array, after):
    def body(*refs):
        pass

    return pl.pallas_call(
        body,
        out_shape=sds(array.shape, array.dtype),
        in_specs=[ANY] * (1 + len(after)),
        out_specs=ANY,
        input_output_aliases={0: 0},
        compiler_params=PARAMS,
    )(array, *after)


def sds(shape, dtype=jnp.bfloat16):
    return jax.ShapeDtypeStruct(shape, dtype)


def head_side():
    me = lax.rem(lax.axis_index("ctx"), TEAM)
    return me // 2, lax.rem(me, 2)


def split(exact):
    first = exact.astype(jnp.bfloat16).astype(jnp.float32)
    second = (exact - first).astype(jnp.bfloat16).astype(jnp.float32)
    return first, second, exact - first - second


def pieces_kernel(q_ref, go_ref, ao_ref, lse_ref, *rest):
    out_refs, (grad, output, lse, stat, sems) = rest[:KV_HEADS], rest[KV_HEADS:]
    rows, width = q_ref.shape
    head, _ = head_side()
    loads = [pltpu.make_async_copy(ref, to, sems.at[i])
             for i, (ref, to) in enumerate(((go_ref, grad), (ao_ref, output), (lse_ref, lse)))]
    moves = []
    for m in range(KV_HEADS):
        columns = pl.ds(pl.multiple_of(jnp.bitwise_xor(head, m) * GROUP, GROUP), GROUP)
        for i, ref in enumerate((q_ref, go_ref)):
            moves.append(pltpu.make_async_copy(
                ref.at[:, columns], out_refs[m].at[0:rows, i * GROUP:(i + 1) * GROUP], sems.at[3 + 2 * m + i]))
    for copy in loads + moves:
        copy.start()
    for copy in loads:
        copy.wait()
    product = grad[...].astype(jnp.float32) * output[...].astype(jnp.float32)
    high = product.astype(jnp.bfloat16)
    low = (product - high.astype(jnp.float32)).astype(jnp.bfloat16)
    head_of = lax.broadcasted_iota(jnp.int32, (Q_HEADS, width), 1) // HEAD_DIM
    ones = (head_of == lax.broadcasted_iota(jnp.int32, (Q_HEADS, width), 0)).astype(jnp.bfloat16)
    delta = matmul(ones, high, NT) + matmul(ones, low, NT)
    for g in range(KV_HEADS):
        part = slice(g * GROUPS, (g + 1) * GROUPS)
        stat[g] = jnp.concatenate([lse[part, :], delta[part, :]], axis=0)
    zero = jnp.zeros((2 * GROUPS, rows), jnp.float32)
    for m in range(KV_HEADS):
        lines = [*split(stat[jnp.bitwise_xor(head, m)]), zero]
        for i, one in enumerate(lines):
            full = jnp.concatenate([one, zero], axis=0).astype(jnp.bfloat16)
            out_refs[m][rows:, i * rows:(i + 1) * rows] = full
    for copy in moves:
        copy.wait()


def hidden_moves(hid_ref, near_refs, far_ref, sems):
    mine = lax.axis_index("fsdp")
    near = len(near_refs)
    span = far_ref.shape[2]
    copies = []
    for m in range(near + far_ref.shape[0]):
        columns = pl.ds(pl.multiple_of(jnp.bitwise_xor(mine, m) * span, span), span)
        to = near_refs[m] if m < near else far_ref.at[m - near]
        copies.append(pltpu.make_async_copy(hid_ref.at[:, columns], to, sems.at[m]))
    for copy in copies:
        copy.start()
    return copies


def hidden_kernel(hid_ref, *rest):
    for copy in hidden_moves(hid_ref, rest[:-2], *rest[-2:]):
        copy.wait()


def project_kernel(fsdp, hid_ref, *rest):
    w_refs, out_refs, (parts,) = rest[:fsdp], rest[fsdp:fsdp + KV_HEADS], rest[fsdp + KV_HEADS:]
    mine = lax.axis_index("fsdp")
    head, _ = head_side()
    span = w_refs[0].shape[0]
    total = None
    for m in range(fsdp):
        start = pl.multiple_of(jnp.bitwise_xor(mine, m) * span, span)
        term = matmul(hid_ref[:, pl.ds(start, span)], w_refs[m][...])
        total = term if total is None else total + term
    low = total.astype(jnp.bfloat16)
    for g in range(KV_HEADS):
        key = low[:, g * HEAD_DIM:(g + 1) * HEAD_DIM]
        value = low[:, KEY_WIDTH + g * HEAD_DIM:KEY_WIDTH + (g + 1) * HEAD_DIM]
        parts[g] = jnp.concatenate([key, value], axis=1)
    for m in range(KV_HEADS):
        out_refs[m][...] = parts[jnp.bitwise_xor(head, m)]


def lower_half(shape):
    return lax.broadcasted_iota(jnp.int32, shape, len(shape) - 1) < LOWER


def stacked(key_value):
    wide = key_value.astype(jnp.float32)
    turned = pltpu.roll(wide, LOWER, 1)
    lower = lower_half(wide.shape)
    zero = jnp.zeros_like(wide)
    keys = jnp.concatenate([jnp.where(lower, wide, zero), jnp.where(lower, zero, turned)], axis=0) * SCALE
    values = jnp.concatenate([jnp.where(lower, turned, zero), jnp.where(lower, zero, wide)], axis=0)
    return keys.astype(jnp.bfloat16), values.astype(jnp.bfloat16)


def tile(keys, values, query, grad, stats, mask):
    size = keys.shape[0] // 2
    lse, delta = stats[:2], stats[2:]
    scores = matmul(keys, query, NT)
    prob_grad = matmul(values, grad, NT)
    lows, grads = [], []
    for head in range(2):
        part = slice(head * size, (head + 1) * size)
        probs = jnp.exp(scores[part] - lse[head])
        edge = mask.shape[1]
        seen = jnp.where(mask, probs[:, :edge], 0.0)
        probs = seen if edge == probs.shape[1] else jnp.concatenate([seen, probs[:, edge:]], axis=1)
        lows.append(probs.astype(jnp.bfloat16))
        grads.append((probs * (prob_grad[part] - delta[head])).astype(jnp.bfloat16))
    low, score_grad = jnp.concatenate(lows, axis=0), jnp.concatenate(grads, axis=0)
    return matmul(score_grad, query), matmul(low, grad), matmul(score_grad, keys, TN)


def folded(key_sum, value_sum):
    size = key_sum.shape[0] // 2
    lower = lower_half((size, PAIR))
    straight = jnp.where(lower, key_sum[:size], value_sum[size:])
    crossed = jnp.where(lower, value_sum[:size], key_sum[size:])
    return (straight + pltpu.roll(crossed, LOWER, 1)) * jnp.where(lower, SCALE, 1.0)


def unpacked(part, rows):
    exact = part[rows:, 0:3 * rows].astype(jnp.float32)[0:2 * GROUPS]
    return exact[:, 0:rows] + exact[:, rows:2 * rows] + exact[:, 2 * rows:]


def pair_stats(stat, pair):
    first = 2 * pair
    return [stat[first:first + 1], stat[first + 1:first + 2],
            stat[GROUPS + first:GROUPS + first + 1], stat[GROUPS + first + 1:GROUPS + first + 2]]


def sequence_kernel(near_parts, order_ref, hid_ref, *rest):
    qd_refs, kv_refs, rest = rest[:TEAM], rest[TEAM:TEAM + KV_HEADS], rest[TEAM + KV_HEADS:]
    dkv_refs, keep_ref, send_ref, rest = rest[:KV_HEADS], rest[KV_HEADS], rest[KV_HEADS + 1], rest[KV_HEADS + 2:]
    near_refs, far_ref, rest = rest[:near_parts], rest[near_parts], rest[near_parts + 1:]
    q_all, go_all, stat_all, key_all, value_all, dq_all, dkv_all, sems = rest
    moves = hidden_moves(hid_ref, near_refs, far_ref, sems)
    rows = kv_refs[0].shape[0]
    head, side = head_side()
    near = [order_ref[0, 2 * jnp.bitwise_xor(head, m) + side] for m in range(KV_HEADS)]
    far = [order_ref[0, 2 * jnp.bitwise_xor(head, m) + 1 - side] for m in range(KV_HEADS)]
    for place, ref in zip(near + far, qd_refs):
        q_all[place] = ref[0:rows, 0:GROUP]
        go_all[place] = ref[0:rows, GROUP:]
        stat_all[place] = unpacked(ref, rows)
    for place, ref in zip(near, kv_refs):
        key_all[place], value_all[place] = stacked(ref[...])
    dq_all[...] = jnp.zeros_like(dq_all)
    for block in range(TEAM):
        mine = functools.reduce(jnp.logical_or, [place == block for place in near])

        @pl.when(mine)
        def _():
            count = TEAM - block
            shape = (rows, rows)
            mask = lax.broadcasted_iota(jnp.int32, shape, 0) <= lax.broadcasted_iota(jnp.int32, shape, 1)
            stats = jnp.concatenate([stat_all[i] for i in range(block, TEAM)], axis=1)
            key_sum = value_sum = None
            for pair in range(GROUPS // 2):
                columns = slice(pair * PAIR, (pair + 1) * PAIR)
                query = q_all[block:, :, columns].reshape(count * rows, PAIR)
                grad = go_all[block:, :, columns].reshape(count * rows, PAIR)
                key_part, value_part, query_part = tile(
                    key_all[block], value_all[block], query, grad, pair_stats(stats, pair), mask)
                key_sum = key_part if key_sum is None else key_sum + key_part
                value_sum = value_part if value_sum is None else value_sum + value_part
                dq_all[block:, :, columns] += query_part.reshape(count, rows, PAIR)
            dkv_all[block] = folded(key_sum, value_sum)

    for m in range(KV_HEADS):
        dkv_refs[m][...] = dkv_all[near[m]].astype(jnp.bfloat16)
        keep_ref[m] = dq_all[near[m]]
        send_ref[m] = dq_all[far[m]].astype(jnp.bfloat16)
    for copy in moves:
        copy.wait()


def teams_kernel(order_ref, qd_ref, kv_ref, dkv_ref, keep_ref, send_ref, dq_all):
    rows = kv_ref.shape[1]
    head, side = head_side()
    base = lax.axis_index("ctx") // TEAM * TEAM
    dq_all[...] = jnp.zeros_like(dq_all)

    @pl.loop(0, kv_ref.shape[0])
    def _(block):
        keys, values = stacked(kv_ref[block])
        dkv_ref[block] = jnp.zeros((rows, PAIR), jnp.float32)
        stored = block // KV_HEADS * TEAM + 2 * jnp.bitwise_xor(head, lax.rem(block, KV_HEADS)) + side
        place = order_ref[0, stored]

        @pl.loop(0, TEAM)
        def _(at):
            turned = jnp.where(at < KV_HEADS, side, 1 - side)
            own = order_ref[0, base + 2 * jnp.bitwise_xor(head, lax.rem(at, KV_HEADS)) + turned]

            @pl.when(place <= own)
            def _():
                shape = (rows, rows)
                mask = (place * rows + lax.broadcasted_iota(jnp.int32, shape, 0)
                        <= own * rows + lax.broadcasted_iota(jnp.int32, shape, 1))
                one = qd_ref.at[at]
                stats = unpacked(one, rows)
                for pair in range(GROUPS // 2):
                    first = pair * PAIR
                    key_part, value_part, query_part = tile(
                        keys, values, one[0:rows, first:first + PAIR], one[0:rows, GROUP + first:GROUP + first + PAIR],
                        pair_stats(stats, pair), mask)
                    dq_all[at, :, first:first + PAIR] += query_part
                    dkv_ref[block] += folded(key_part, value_part)

    keep_ref[...] = dq_all[0:KV_HEADS]
    send_ref[...] = dq_all[KV_HEADS:].astype(jnp.bfloat16)


def owner_kernel(*rest):
    dkv_refs, out_ref, parts = rest[:KV_HEADS], rest[KV_HEADS], rest[KV_HEADS + 1]
    head, _ = head_side()
    for m in range(KV_HEADS):
        parts[jnp.bitwise_xor(head, m)] = dkv_refs[m][...]
    keys = [parts[g, :, :HEAD_DIM] for g in range(KV_HEADS)]
    values = [parts[g, :, HEAD_DIM:] for g in range(KV_HEADS)]
    out_ref[...] = jnp.concatenate(keys + values, axis=1)


def pair_kernel(keep_ref, got_ref, *out_refs):
    for m in range(KV_HEADS):
        out_refs[m][...] = (keep_ref[m] + got_ref[m].astype(jnp.float32)).astype(out_refs[m].dtype)


def query_kernel(*rest):
    dq_refs, out_ref = rest[:KV_HEADS], rest[KV_HEADS]
    head, _ = head_side()
    for m in range(KV_HEADS):
        columns = pl.ds(pl.multiple_of(jnp.bitwise_xor(head, m) * GROUP, GROUP), GROUP)
        out_ref[:, columns] = dq_refs[m][...]


def input_kernel(fsdp, grad_ref, *rest):
    w_refs, out_ref = rest[:fsdp], rest[fsdp]
    mine = lax.axis_index("fsdp")
    span = w_refs[0].shape[0]
    for m in range(fsdp):
        start = pl.multiple_of(jnp.bitwise_xor(mine, m) * span, span)
        out_ref[:, pl.ds(start, span)] = matmul(grad_ref[...], w_refs[m][...], NT).astype(jnp.bfloat16)


def weight_sums(fsdp, refs):
    hid = jnp.concatenate([ref[...] for ref in refs[:fsdp]], axis=0)
    grad = jnp.concatenate([ref[...] for ref in refs[fsdp:2 * fsdp]], axis=0)
    return matmul(hid, grad, TN)


def weight_kernel(fsdp, *rest):
    rest[2 * fsdp][...] = weight_sums(fsdp, rest).astype(jnp.bfloat16)


def sides_kernel(fsdp, *rest):
    keep_ref, send_ref, parts = rest[2 * fsdp:]
    head, side = head_side()
    parts[...] = weight_sums(fsdp, rest).reshape(parts.shape)
    for m in range(KV_HEADS):
        to = 2 * jnp.bitwise_xor(head, m)
        keep_ref[m] = parts[to + side]
        send_ref[m] = parts[to + 1 - side].astype(jnp.bfloat16)


def own_total_kernel(own_ref, *rest):
    total = own_ref[...]
    for ref in rest[:-1]:
        total = total + ref[...].astype(jnp.float32)
    rest[-1][...] = total


def total_kernel(part_ref, out_ref):
    total = part_ref[0].astype(jnp.float32)
    for i in range(1, part_ref.shape[0]):
        total = total + part_ref[i].astype(jnp.float32)
    out_ref[...] = total


def over_fsdp(own, bits):
    got = list(own)
    while bits:
        for m in range(len(own)):
            if m & bits:
                got[m] = swapped(got[m], "fsdp", bits)
        bits //= 2
    return got


def shards(hidden, queries, attn_out, grad_out, log_sums, block_order, w_kv):
    rows, model = hidden.shape[1:]
    fsdp, devices = lax.axis_size("fsdp"), lax.axis_size("ctx")
    teams = devices // TEAM
    f32 = jnp.float32
    span = model // fsdp
    inputs = hidden[0]
    columns = 2 * KEY_WIDTH
    block, wide = (rows, PAIR), (rows, GROUP)

    def along_heads(arrays):
        return [arrays[0]] + [swapped(arrays[m], "ctx", 2 * m) for m in range(1, KV_HEADS)]

    far = fsdp // 2
    qd = call(
        pieces_kernel, [sds((rows + 16, 2 * GROUP))] * KV_HEADS,
        [pltpu.VMEM((rows, Q_HEADS * HEAD_DIM), jnp.bfloat16)] * 2
        + [pltpu.VMEM((Q_HEADS, rows), f32), pltpu.VMEM((KV_HEADS, 2 * GROUPS, rows), f32),
           pltpu.SemaphoreType.DMA((3 + 2 * KV_HEADS,))],
        (queries[0], grad_out[0], attn_out[0], log_sums[0]), hbm=4)
    qd = along_heads(qd)
    turned = [swapped(one, "ctx", 1) for one in qd[:2]]
    w_far = held(swapped(w_kv, "fsdp", far), (*qd[1:KV_HEADS - 1], turned[0]))
    w_parts = over_fsdp([w_kv] * far + [w_far] * (fsdp - far), far // 2)

    kv = call(
        functools.partial(project_kernel, fsdp), [sds(block)] * KV_HEADS,
        [pltpu.VMEM((KV_HEADS,) + block, jnp.bfloat16)], (inputs, *w_parts))
    own_kv, kv = kv[:1], along_heads(kv)
    late = [held(qd[2], own_kv), held(qd[3], kv[1:])]
    qd = qd[:2] + late + turned + [swapped(one, "ctx", 1) for one in late]

    half = (KV_HEADS,) + wide
    cut = [sds((rows, span))] * far + [sds((fsdp - far, rows, span))]
    cut_sems = pltpu.SemaphoreType.DMA((fsdp,))
    if teams == 1:
        outs = call(
            functools.partial(sequence_kernel, far), [sds(block)] * KV_HEADS + [sds(half, f32), sds(half)] + cut,
            [pltpu.VMEM((TEAM,) + wide, jnp.bfloat16)] * 2 + [pltpu.VMEM((TEAM, 2 * GROUPS, rows), f32)]
            + [pltpu.VMEM((TEAM, 2 * rows, PAIR), jnp.bfloat16)] * 2
            + [pltpu.VMEM((TEAM,) + wide, f32), pltpu.VMEM((TEAM,) + block, f32), cut_sems],
            (block_order, inputs, *qd, *kv), smem=1, hbm=1)
        dkv, (keep, give, *hid, hid_far) = outs[:KV_HEADS], outs[KV_HEADS:]
    else:
        alike = [[t * TEAM + i for t in range(teams)] for i in range(TEAM)]
        kv = lax.all_gather(jnp.stack(kv), "ctx", axis_index_groups=alike, axis=0, tiled=True)
        dkv, keep, give = call(
            teams_kernel, [sds((teams * KV_HEADS,) + block, f32), sds(half, f32), sds(half)],
            [pltpu.VMEM((TEAM,) + wide, f32)], (block_order, jnp.stack(qd), kv), smem=1)
        dkv = lax.psum_scatter(dkv, "ctx", axis_index_groups=alike, scatter_dimension=0, tiled=True)
        dkv = [dkv[m].astype(jnp.bfloat16) for m in range(KV_HEADS)]
        *hid, hid_far = call(hidden_kernel, cut, [cut_sems], (inputs,), hbm=1)

    hid_far = swapped(hid_far, "fsdp", far)
    hid = over_fsdp(hid + [hid_far[m] for m in range(fsdp - far)], far // 2)
    dkv = along_heads(dkv)
    give = swapped(give, "ctx", 1)
    (kv_grad,) = call(
        owner_kernel, [sds((rows, columns))], [pltpu.VMEM((KV_HEADS,) + block, jnp.bfloat16)],
        dkv, after=(give,))
    grads = over_fsdp([kv_grad] * fsdp, far)
    if teams == 1:
        share = (span // devices, columns)
        own_sums, send_sums = call(
            functools.partial(sides_kernel, fsdp), [sds((KV_HEADS,) + share, f32), sds((KV_HEADS,) + share)],
            [pltpu.VMEM((devices,) + share, f32)], (*hid, *grads))
        formed = (own_sums,)
        dq = along_heads(call(pair_kernel, [sds(wide)] * KV_HEADS, [], (keep, give), after=formed))
        sums = call(
            pair_kernel, [sds(share, f32)] + [sds(share)] * (KV_HEADS - 1), [],
            (own_sums, swapped(send_sums, "ctx", 1)), after=dq[1:])
        (weight_grads,) = call(own_total_kernel, [sds(share, f32)], [], along_heads(sums))
    else:
        formed = call(functools.partial(weight_kernel, fsdp), [sds((span, columns))], [], (*hid, *grads))
        dq = along_heads(call(pair_kernel, [sds(wide)] * KV_HEADS, [], (keep, give), after=formed))
        sums = lax.all_to_all(formed[0].reshape(devices, span // devices, columns), "ctx", 0, 0, tiled=True)
        (weight_grads,) = call(total_kernel, [sds((span // devices, columns), f32)], [], (sums,))
    (query_grads,) = call(query_kernel, [sds((rows, Q_HEADS * HEAD_DIM))], [], dq, after=formed)
    (input_grads,) = call(
        functools.partial(input_kernel, fsdp), [sds((rows, model))], [], (kv_grad, *w_parts), after=formed)
    return query_grads[None], input_grads[None], weight_grads


def solution(mesh):
    return jax.shard_map(
        shards,
        mesh=mesh,
        in_specs=(
            P("fsdp", "ctx", None),
            P("fsdp", "ctx", None),
            P("fsdp", "ctx", None),
            P("fsdp", "ctx", None),
            P("fsdp", None, "ctx"),
            P("fsdp", None),
            P("fsdp", None),
        ),
        out_specs=(P("fsdp", "ctx", None), P("fsdp", "ctx", None), P(("fsdp", "ctx"), None)),
        check_vma=False,
    )
```

```python
import functools

import jax
import jax.numpy as jnp
from jax import lax
from jax.experimental import pallas as pl
from jax.experimental.pallas import tpu as pltpu
from jax.sharding import PartitionSpec as P

Q_HEADS = 16
KV_HEADS = 4
HEAD_DIM = 64
GROUPS = Q_HEADS // KV_HEADS
KEY_WIDTH = KV_HEADS * HEAD_DIM
PAIR = 2 * HEAD_DIM
TEAM = 2 * KV_HEADS
GROUP = GROUPS * HEAD_DIM
SCALE = HEAD_DIM ** -0.5
LOWER = HEAD_DIM

NT = (((1,), (1,)), ((), ()))
TN = (((0,), (0,)), ((), ()))
VMEM = pl.BlockSpec(memory_space=pltpu.VMEM)
SMEM = pl.BlockSpec(memory_space=pltpu.SMEM)
ANY = pl.BlockSpec(memory_space=pl.ANY)
HBM = pl.BlockSpec(memory_space=pltpu.HBM)
PARAMS = pltpu.CompilerParams(vmem_limit_bytes=40 * 1024 * 1024)
WHOLE = pltpu.CompilerParams(vmem_limit_bytes=60 * 1024 * 1024)


def matmul(left, right, dims=(((1,), (0,)), ((), ()))):
    return lax.dot_general(left, right, dims, preferred_element_type=jnp.float32)


def swapped(array, axis, bits):
    size = lax.axis_size(axis)
    return lax.ppermute(array, axis, [(i, i ^ bits) for i in range(size)])


def call(kernel, out_shape, scratch, args, smem=0, hbm=0, after=()):
    given = len(args)
    params = WHOLE if hbm == given else PARAMS

    def body(*refs):
        kernel(*refs[:given], *refs[given + len(after):])

    specs = [SMEM] * smem + [HBM] * hbm + [VMEM] * (given - smem - hbm) + [ANY] * len(after)
    return pl.pallas_call(
        body,
        out_shape=out_shape,
        in_specs=specs,
        out_specs=[VMEM] * len(out_shape),
        scratch_shapes=scratch,
        compiler_params=params,
    )(*args, *after)


def held(array, after):
    def body(*refs):
        pass

    return pl.pallas_call(
        body,
        out_shape=sds(array.shape, array.dtype),
        in_specs=[ANY] * (1 + len(after)),
        out_specs=ANY,
        input_output_aliases={0: 0},
        compiler_params=PARAMS,
    )(array, *after)


def sds(shape, dtype=jnp.bfloat16):
    return jax.ShapeDtypeStruct(shape, dtype)


def head_side():
    me = lax.rem(lax.axis_index("ctx"), TEAM)
    return me // 2, lax.rem(me, 2)


def split(exact):
    first = exact.astype(jnp.bfloat16).astype(jnp.float32)
    second = (exact - first).astype(jnp.bfloat16).astype(jnp.float32)
    return first, second, exact - first - second


def pieces_kernel(q_ref, go_ref, ao_ref, lse_ref, *rest):
    out_refs, (grad, output, lse, stat, sems) = rest[:KV_HEADS], rest[KV_HEADS:]
    rows, width = q_ref.shape
    head, _ = head_side()
    loads = [pltpu.make_async_copy(ref, to, sems.at[i])
             for i, (ref, to) in enumerate(((go_ref, grad), (ao_ref, output), (lse_ref, lse)))]
    moves = []
    for m in range(KV_HEADS):
        columns = pl.ds(pl.multiple_of(jnp.bitwise_xor(head, m) * GROUP, GROUP), GROUP)
        for i, ref in enumerate((q_ref, go_ref)):
            moves.append(pltpu.make_async_copy(
                ref.at[:, columns], out_refs[m].at[0:rows, i * GROUP:(i + 1) * GROUP], sems.at[3 + 2 * m + i]))
    for copy in loads + moves:
        copy.start()
    for copy in loads:
        copy.wait()
    product = grad[...].astype(jnp.float32) * output[...].astype(jnp.float32)
    high = product.astype(jnp.bfloat16)
    low = (product - high.astype(jnp.float32)).astype(jnp.bfloat16)
    head_of = lax.broadcasted_iota(jnp.int32, (Q_HEADS, width), 1) // HEAD_DIM
    ones = (head_of == lax.broadcasted_iota(jnp.int32, (Q_HEADS, width), 0)).astype(jnp.bfloat16)
    delta = matmul(ones, high, NT) + matmul(ones, low, NT)
    for g in range(KV_HEADS):
        part = slice(g * GROUPS, (g + 1) * GROUPS)
        stat[g] = jnp.concatenate([lse[part, :], delta[part, :]], axis=0)
    zero = jnp.zeros((2 * GROUPS, rows), jnp.float32)
    for m in range(KV_HEADS):
        lines = [*split(stat[jnp.bitwise_xor(head, m)]), zero]
        for i, one in enumerate(lines):
            full = jnp.concatenate([one, zero], axis=0).astype(jnp.bfloat16)
            out_refs[m][rows:, i * rows:(i + 1) * rows] = full
    for copy in moves:
        copy.wait()


def hidden_moves(hid_ref, near_refs, far_ref, sems):
    mine = lax.axis_index("fsdp")
    near = len(near_refs)
    span = far_ref.shape[2]
    copies = []
    for m in range(near + far_ref.shape[0]):
        columns = pl.ds(pl.multiple_of(jnp.bitwise_xor(mine, m) * span, span), span)
        to = near_refs[m] if m < near else far_ref.at[m - near]
        copies.append(pltpu.make_async_copy(hid_ref.at[:, columns], to, sems.at[m]))
    for copy in copies:
        copy.start()
    return copies


def hidden_kernel(hid_ref, *rest):
    for copy in hidden_moves(hid_ref, rest[:-2], *rest[-2:]):
        copy.wait()


def project_kernel(fsdp, hid_ref, *rest):
    w_refs, out_refs, (parts,) = rest[:fsdp], rest[fsdp:fsdp + KV_HEADS], rest[fsdp + KV_HEADS:]
    mine = lax.axis_index("fsdp")
    head, _ = head_side()
    span = w_refs[0].shape[0]
    total = None
    for m in range(fsdp):
        start = pl.multiple_of(jnp.bitwise_xor(mine, m) * span, span)
        term = matmul(hid_ref[:, pl.ds(start, span)], w_refs[m][...])
        total = term if total is None else total + term
    low = total.astype(jnp.bfloat16)
    for g in range(KV_HEADS):
        key = low[:, g * HEAD_DIM:(g + 1) * HEAD_DIM]
        value = low[:, KEY_WIDTH + g * HEAD_DIM:KEY_WIDTH + (g + 1) * HEAD_DIM]
        parts[g] = jnp.concatenate([key, value], axis=1)
    for m in range(KV_HEADS):
        out_refs[m][...] = parts[jnp.bitwise_xor(head, m)]


def lower_half(shape):
    return lax.broadcasted_iota(jnp.int32, shape, len(shape) - 1) < LOWER


def stacked(key_value):
    wide = key_value.astype(jnp.float32)
    turned = pltpu.roll(wide, LOWER, 1)
    lower = lower_half(wide.shape)
    zero = jnp.zeros_like(wide)
    keys = jnp.concatenate([jnp.where(lower, wide, zero), jnp.where(lower, zero, turned)], axis=0) * SCALE
    values = jnp.concatenate([jnp.where(lower, turned, zero), jnp.where(lower, zero, wide)], axis=0)
    return keys.astype(jnp.bfloat16), values.astype(jnp.bfloat16)


def tile(keys, values, query, grad, stats, mask):
    size = keys.shape[0] // 2
    lse, delta = stats[:2], stats[2:]
    scores = matmul(keys, query, NT)
    prob_grad = matmul(values, grad, NT)
    lows, grads = [], []
    for head in range(2):
        part = slice(head * size, (head + 1) * size)
        probs = jnp.exp(scores[part] - lse[head])
        edge = mask.shape[1]
        seen = jnp.where(mask, probs[:, :edge], 0.0)
        probs = seen if edge == probs.shape[1] else jnp.concatenate([seen, probs[:, edge:]], axis=1)
        lows.append(probs.astype(jnp.bfloat16))
        grads.append((probs * (prob_grad[part] - delta[head])).astype(jnp.bfloat16))
    low, score_grad = jnp.concatenate(lows, axis=0), jnp.concatenate(grads, axis=0)
    return matmul(score_grad, query), matmul(low, grad), matmul(score_grad, keys, TN)


def folded(key_sum, value_sum):
    size = key_sum.shape[0] // 2
    lower = lower_half((size, PAIR))
    straight = jnp.where(lower, key_sum[:size], value_sum[size:])
    crossed = jnp.where(lower, value_sum[:size], key_sum[size:])
    return (straight + pltpu.roll(crossed, LOWER, 1)) * jnp.where(lower, SCALE, 1.0)


def unpacked(part, rows):
    exact = part[rows:, 0:3 * rows].astype(jnp.float32)[0:2 * GROUPS]
    return exact[:, 0:rows] + exact[:, rows:2 * rows] + exact[:, 2 * rows:]


def pair_stats(stat, pair):
    first = 2 * pair
    return [stat[first:first + 1], stat[first + 1:first + 2],
            stat[GROUPS + first:GROUPS + first + 1], stat[GROUPS + first + 1:GROUPS + first + 2]]


def sequence_kernel(near_parts, order_ref, hid_ref, *rest):
    qd_refs, kv_refs, rest = rest[:TEAM], rest[TEAM:TEAM + KV_HEADS], rest[TEAM + KV_HEADS:]
    dkv_refs, keep_ref, send_ref, rest = rest[:KV_HEADS], rest[KV_HEADS], rest[KV_HEADS + 1], rest[KV_HEADS + 2:]
    near_refs, far_ref, rest = rest[:near_parts], rest[near_parts], rest[near_parts + 1:]
    q_all, go_all, stat_all, key_all, value_all, dq_all, dkv_all, sems = rest
    moves = hidden_moves(hid_ref, near_refs, far_ref, sems)
    rows = kv_refs[0].shape[0]
    head, side = head_side()
    near = [order_ref[0, 2 * jnp.bitwise_xor(head, m) + side] for m in range(KV_HEADS)]
    far = [order_ref[0, 2 * jnp.bitwise_xor(head, m) + 1 - side] for m in range(KV_HEADS)]
    for place, ref in zip(near + far, qd_refs):
        q_all[place] = ref[0:rows, 0:GROUP]
        go_all[place] = ref[0:rows, GROUP:]
        stat_all[place] = unpacked(ref, rows)
    for place, ref in zip(near, kv_refs):
        key_all[place], value_all[place] = stacked(ref[...])
    dq_all[...] = jnp.zeros_like(dq_all)
    for block in range(TEAM):
        mine = functools.reduce(jnp.logical_or, [place == block for place in near])

        @pl.when(mine)
        def _():
            count = TEAM - block
            shape = (rows, rows)
            mask = lax.broadcasted_iota(jnp.int32, shape, 0) <= lax.broadcasted_iota(jnp.int32, shape, 1)
            stats = jnp.concatenate([stat_all[i] for i in range(block, TEAM)], axis=1)
            key_sum = value_sum = None
            for pair in range(GROUPS // 2):
                columns = slice(pair * PAIR, (pair + 1) * PAIR)
                query = q_all[block:, :, columns].reshape(count * rows, PAIR)
                grad = go_all[block:, :, columns].reshape(count * rows, PAIR)
                key_part, value_part, query_part = tile(
                    key_all[block], value_all[block], query, grad, pair_stats(stats, pair), mask)
                key_sum = key_part if key_sum is None else key_sum + key_part
                value_sum = value_part if value_sum is None else value_sum + value_part
                dq_all[block:, :, columns] += query_part.reshape(count, rows, PAIR)
            dkv_all[block] = folded(key_sum, value_sum)

    for m in range(KV_HEADS):
        dkv_refs[m][...] = dkv_all[near[m]].astype(jnp.bfloat16)
        keep_ref[m] = dq_all[near[m]]
        send_ref[m] = dq_all[far[m]].astype(jnp.bfloat16)
    for copy in moves:
        copy.wait()


def teams_kernel(order_ref, qd_ref, kv_ref, dkv_ref, keep_ref, send_ref, dq_all):
    rows = kv_ref.shape[1]
    head, side = head_side()
    base = lax.axis_index("ctx") // TEAM * TEAM
    dq_all[...] = jnp.zeros_like(dq_all)

    @pl.loop(0, kv_ref.shape[0])
    def _(block):
        keys, values = stacked(kv_ref[block])
        dkv_ref[block] = jnp.zeros((rows, PAIR), jnp.float32)
        stored = block // KV_HEADS * TEAM + 2 * jnp.bitwise_xor(head, lax.rem(block, KV_HEADS)) + side
        place = order_ref[0, stored]

        @pl.loop(0, TEAM)
        def _(at):
            turned = jnp.where(at < KV_HEADS, side, 1 - side)
            own = order_ref[0, base + 2 * jnp.bitwise_xor(head, lax.rem(at, KV_HEADS)) + turned]

            @pl.when(place <= own)
            def _():
                shape = (rows, rows)
                mask = (place * rows + lax.broadcasted_iota(jnp.int32, shape, 0)
                        <= own * rows + lax.broadcasted_iota(jnp.int32, shape, 1))
                one = qd_ref.at[at]
                stats = unpacked(one, rows)
                for pair in range(GROUPS // 2):
                    first = pair * PAIR
                    key_part, value_part, query_part = tile(
                        keys, values, one[0:rows, first:first + PAIR], one[0:rows, GROUP + first:GROUP + first + PAIR],
                        pair_stats(stats, pair), mask)
                    dq_all[at, :, first:first + PAIR] += query_part
                    dkv_ref[block] += folded(key_part, value_part)

    keep_ref[...] = dq_all[0:KV_HEADS]
    send_ref[...] = dq_all[KV_HEADS:].astype(jnp.bfloat16)


def owner_kernel(*rest):
    dkv_refs, out_ref, parts = rest[:KV_HEADS], rest[KV_HEADS], rest[KV_HEADS + 1]
    head, _ = head_side()
    for m in range(KV_HEADS):
        parts[jnp.bitwise_xor(head, m)] = dkv_refs[m][...]
    keys = [parts[g, :, :HEAD_DIM] for g in range(KV_HEADS)]
    values = [parts[g, :, HEAD_DIM:] for g in range(KV_HEADS)]
    out_ref[...] = jnp.concatenate(keys + values, axis=1)


def pair_kernel(keep_ref, got_ref, *out_refs):
    for m in range(KV_HEADS):
        out_refs[m][...] = (keep_ref[m] + got_ref[m].astype(jnp.float32)).astype(out_refs[m].dtype)


def query_kernel(*rest):
    dq_refs, out_ref = rest[:KV_HEADS], rest[KV_HEADS]
    head, _ = head_side()
    for m in range(KV_HEADS):
        columns = pl.ds(pl.multiple_of(jnp.bitwise_xor(head, m) * GROUP, GROUP), GROUP)
        out_ref[:, columns] = dq_refs[m][...]


def input_kernel(fsdp, grad_ref, *rest):
    w_refs, out_ref = rest[:fsdp], rest[fsdp]
    mine = lax.axis_index("fsdp")
    span = w_refs[0].shape[0]
    for m in range(fsdp):
        start = pl.multiple_of(jnp.bitwise_xor(mine, m) * span, span)
        out_ref[:, pl.ds(start, span)] = matmul(grad_ref[...], w_refs[m][...], NT).astype(jnp.bfloat16)


def weight_sums(fsdp, refs):
    hid = jnp.concatenate([ref[...] for ref in refs[:fsdp]], axis=0)
    grad = jnp.concatenate([ref[...] for ref in refs[fsdp:2 * fsdp]], axis=0)
    return matmul(hid, grad, TN)


def weight_kernel(fsdp, *rest):
    rest[2 * fsdp][...] = weight_sums(fsdp, rest).astype(jnp.bfloat16)


def sides_kernel(fsdp, *rest):
    keep_ref, send_ref, parts = rest[2 * fsdp:]
    head, side = head_side()
    parts[...] = weight_sums(fsdp, rest).reshape(parts.shape)
    for m in range(KV_HEADS):
        to = 2 * jnp.bitwise_xor(head, m)
        keep_ref[m] = parts[to + side]
        send_ref[m] = parts[to + 1 - side].astype(jnp.bfloat16)


def own_total_kernel(own_ref, *rest):
    total = own_ref[...]
    for ref in rest[:-1]:
        total = total + ref[...].astype(jnp.float32)
    rest[-1][...] = total


def total_kernel(part_ref, out_ref):
    total = part_ref[0].astype(jnp.float32)
    for i in range(1, part_ref.shape[0]):
        total = total + part_ref[i].astype(jnp.float32)
    out_ref[...] = total


def over_fsdp(own, bits):
    got = list(own)
    while bits:
        for m in range(len(own)):
            if m & bits:
                got[m] = swapped(got[m], "fsdp", bits)
        bits //= 2
    return got


def shards(hidden, queries, attn_out, grad_out, log_sums, block_order, w_kv):
    rows, model = hidden.shape[1:]
    fsdp, devices = lax.axis_size("fsdp"), lax.axis_size("ctx")
    teams = devices // TEAM
    f32 = jnp.float32
    span = model // fsdp
    inputs = hidden[0]
    columns = 2 * KEY_WIDTH
    block, wide = (rows, PAIR), (rows, GROUP)

    def along_heads(arrays):
        return [arrays[0]] + [swapped(arrays[m], "ctx", 2 * m) for m in range(1, KV_HEADS)]

    far = fsdp // 2
    qd = call(
        pieces_kernel, [sds((rows + 16, 2 * GROUP))] * KV_HEADS,
        [pltpu.VMEM((rows, Q_HEADS * HEAD_DIM), jnp.bfloat16)] * 2
        + [pltpu.VMEM((Q_HEADS, rows), f32), pltpu.VMEM((KV_HEADS, 2 * GROUPS, rows), f32),
           pltpu.SemaphoreType.DMA((3 + 2 * KV_HEADS,))],
        (queries[0], grad_out[0], attn_out[0], log_sums[0]), hbm=4)
    qd = along_heads(qd)
    turned = [swapped(one, "ctx", 1) for one in qd[:2]]
    w_far = held(swapped(w_kv, "fsdp", far), (*qd[1:KV_HEADS - 1], *turned))
    w_parts = over_fsdp([w_kv] * far + [w_far] * (fsdp - far), far // 2)

    kv = call(
        functools.partial(project_kernel, fsdp), [sds(block)] * KV_HEADS,
        [pltpu.VMEM((KV_HEADS,) + block, jnp.bfloat16)], (inputs, *w_parts))
    own_kv, kv = kv[:1], along_heads(kv)
    late = [held(qd[2], own_kv), held(qd[3], kv[1:])]
    qd = qd[:2] + late + turned + [swapped(one, "ctx", 1) for one in late]

    half = (KV_HEADS,) + wide
    cut = [sds((rows, span))] * far + [sds((fsdp - far, rows, span))]
    cut_sems = pltpu.SemaphoreType.DMA((fsdp,))
    if teams == 1:
        outs = call(
            functools.partial(sequence_kernel, far), [sds(block)] * KV_HEADS + [sds(half, f32), sds(half)] + cut,
            [pltpu.VMEM((TEAM,) + wide, jnp.bfloat16)] * 2 + [pltpu.VMEM((TEAM, 2 * GROUPS, rows), f32)]
            + [pltpu.VMEM((TEAM, 2 * rows, PAIR), jnp.bfloat16)] * 2
            + [pltpu.VMEM((TEAM,) + wide, f32), pltpu.VMEM((TEAM,) + block, f32), cut_sems],
            (block_order, inputs, *qd, *kv), smem=1, hbm=1)
        dkv, (keep, give, *hid, hid_far) = outs[:KV_HEADS], outs[KV_HEADS:]
    else:
        alike = [[t * TEAM + i for t in range(teams)] for i in range(TEAM)]
        kv = lax.all_gather(jnp.stack(kv), "ctx", axis_index_groups=alike, axis=0, tiled=True)
        dkv, keep, give = call(
            teams_kernel, [sds((teams * KV_HEADS,) + block, f32), sds(half, f32), sds(half)],
            [pltpu.VMEM((TEAM,) + wide, f32)], (block_order, jnp.stack(qd), kv), smem=1)
        dkv = lax.psum_scatter(dkv, "ctx", axis_index_groups=alike, scatter_dimension=0, tiled=True)
        dkv = [dkv[m].astype(jnp.bfloat16) for m in range(KV_HEADS)]
        *hid, hid_far = call(hidden_kernel, cut, [cut_sems], (inputs,), hbm=1)

    hid_far = swapped(hid_far, "fsdp", far)
    hid = over_fsdp(hid + [hid_far[m] for m in range(fsdp - far)], far // 2)
    dkv = along_heads(dkv)
    give = swapped(give, "ctx", 1)
    (kv_grad,) = call(
        owner_kernel, [sds((rows, columns))], [pltpu.VMEM((KV_HEADS,) + block, jnp.bfloat16)],
        dkv, after=(give,))
    grads = over_fsdp([kv_grad] * fsdp, far)
    if teams == 1:
        share = (span // devices, columns)
        own_sums, send_sums = call(
            functools.partial(sides_kernel, fsdp), [sds((KV_HEADS,) + share, f32), sds((KV_HEADS,) + share)],
            [pltpu.VMEM((devices,) + share, f32)], (*hid, *grads))
        formed = (own_sums,)
        dq = along_heads(call(pair_kernel, [sds(wide)] * KV_HEADS, [], (keep, give), after=formed))
        sums = call(
            pair_kernel, [sds(share, f32)] + [sds(share)] * (KV_HEADS - 1), [],
            (own_sums, swapped(send_sums, "ctx", 1)), after=dq[2:3])
        (weight_grads,) = call(own_total_kernel, [sds(share, f32)], [], along_heads(sums))
    else:
        formed = call(functools.partial(weight_kernel, fsdp), [sds((span, columns))], [], (*hid, *grads))
        dq = along_heads(call(pair_kernel, [sds(wide)] * KV_HEADS, [], (keep, give), after=formed))
        sums = lax.all_to_all(formed[0].reshape(devices, span // devices, columns), "ctx", 0, 0, tiled=True)
        (weight_grads,) = call(total_kernel, [sds((span // devices, columns), f32)], [], (sums,))
    (query_grads,) = call(query_kernel, [sds((rows, Q_HEADS * HEAD_DIM))], [], dq, after=formed)
    (input_grads,) = call(
        functools.partial(input_kernel, fsdp), [sds((rows, model))], [], (kv_grad, *w_parts), after=formed)
    return query_grads[None], input_grads[None], weight_grads


def solution(mesh):
    return jax.shard_map(
        shards,
        mesh=mesh,
        in_specs=(
            P("fsdp", "ctx", None),
            P("fsdp", "ctx", None),
            P("fsdp", "ctx", None),
            P("fsdp", "ctx", None),
            P("fsdp", None, "ctx"),
            P("fsdp", None),
            P("fsdp", None),
        ),
        out_specs=(P("fsdp", "ctx", None), P("fsdp", "ctx", None), P(("fsdp", "ctx"), None)),
        check_vma=False,
    )
```

```python
import functools

import jax
import jax.numpy as jnp
from jax import lax
from jax.experimental import pallas as pl
from jax.experimental.pallas import tpu as pltpu
from jax.sharding import PartitionSpec as P

Q_HEADS = 16
KV_HEADS = 4
HEAD_DIM = 64
GROUPS = Q_HEADS // KV_HEADS
KEY_WIDTH = KV_HEADS * HEAD_DIM
PAIR = 2 * HEAD_DIM
TEAM = 2 * KV_HEADS
PAIRS = GROUPS // 2
GROUP = GROUPS * HEAD_DIM
SCALE = HEAD_DIM ** -0.5
LOWER = HEAD_DIM

NT = (((1,), (1,)), ((), ()))
TN = (((0,), (0,)), ((), ()))
VMEM = pl.BlockSpec(memory_space=pltpu.VMEM)
SMEM = pl.BlockSpec(memory_space=pltpu.SMEM)
ANY = pl.BlockSpec(memory_space=pl.ANY)
HBM = pl.BlockSpec(memory_space=pltpu.HBM)
PARAMS = pltpu.CompilerParams(vmem_limit_bytes=40 * 1024 * 1024)
WHOLE = pltpu.CompilerParams(vmem_limit_bytes=60 * 1024 * 1024)


def matmul(left, right, dims=(((1,), (0,)), ((), ()))):
    return lax.dot_general(left, right, dims, preferred_element_type=jnp.float32)


def swapped(array, axis, bits):
    size = lax.axis_size(axis)
    return lax.ppermute(array, axis, [(i, i ^ bits) for i in range(size)])


def call(kernel, out_shape, scratch, args, smem=0, hbm=0, after=()):
    given = len(args)
    params = WHOLE if hbm == given else PARAMS

    def body(*refs):
        kernel(*refs[:given], *refs[given + len(after):])

    specs = [SMEM] * smem + [HBM] * hbm + [VMEM] * (given - smem - hbm) + [ANY] * len(after)
    return pl.pallas_call(
        body,
        out_shape=out_shape,
        in_specs=specs,
        out_specs=[VMEM] * len(out_shape),
        scratch_shapes=scratch,
        compiler_params=params,
    )(*args, *after)


def held(array, after):
    def body(*refs):
        pass

    return pl.pallas_call(
        body,
        out_shape=sds(array.shape, array.dtype),
        in_specs=[ANY] * (1 + len(after)),
        out_specs=ANY,
        input_output_aliases={0: 0},
        compiler_params=PARAMS,
    )(array, *after)


def sds(shape, dtype=jnp.bfloat16):
    return jax.ShapeDtypeStruct(shape, dtype)


def head_side():
    me = lax.rem(lax.axis_index("ctx"), TEAM)
    return me // 2, lax.rem(me, 2)


def split(exact):
    first = exact.astype(jnp.bfloat16).astype(jnp.float32)
    second = (exact - first).astype(jnp.bfloat16).astype(jnp.float32)
    return first, second, exact - first - second


def pieces_kernel(q_ref, go_ref, ao_ref, lse_ref, *rest):
    out_refs, (grad, output, lse, stat, sems) = rest[:KV_HEADS], rest[KV_HEADS:]
    rows, width = q_ref.shape
    head, _ = head_side()
    loads = [pltpu.make_async_copy(ref, to, sems.at[i])
             for i, (ref, to) in enumerate(((go_ref, grad), (ao_ref, output), (lse_ref, lse)))]
    moves = []
    for m in range(KV_HEADS):
        columns = pl.ds(pl.multiple_of(jnp.bitwise_xor(head, m) * GROUP, GROUP), GROUP)
        for i, ref in enumerate((q_ref, go_ref)):
            moves.append(pltpu.make_async_copy(
                ref.at[:, columns], out_refs[m].at[0:rows, i * GROUP:(i + 1) * GROUP], sems.at[3 + 2 * m + i]))
    for copy in loads + moves:
        copy.start()
    for copy in loads:
        copy.wait()
    product = grad[...].astype(jnp.float32) * output[...].astype(jnp.float32)
    high = product.astype(jnp.bfloat16)
    low = (product - high.astype(jnp.float32)).astype(jnp.bfloat16)
    head_of = lax.broadcasted_iota(jnp.int32, (Q_HEADS, width), 1) // HEAD_DIM
    ones = (head_of == lax.broadcasted_iota(jnp.int32, (Q_HEADS, width), 0)).astype(jnp.bfloat16)
    delta = matmul(ones, high, NT) + matmul(ones, low, NT)
    for g in range(KV_HEADS):
        part = slice(g * GROUPS, (g + 1) * GROUPS)
        stat[g] = jnp.concatenate([lse[part, :], delta[part, :]], axis=0)
    zero = jnp.zeros((2 * GROUPS, rows), jnp.float32)
    for m in range(KV_HEADS):
        lines = [*split(stat[jnp.bitwise_xor(head, m)]), zero]
        for i, one in enumerate(lines):
            full = jnp.concatenate([one, zero], axis=0).astype(jnp.bfloat16)
            out_refs[m][rows:, i * rows:(i + 1) * rows] = full
    for copy in moves:
        copy.wait()


def hidden_moves(hid_ref, near_refs, far_ref, sems):
    mine = lax.axis_index("fsdp")
    near = len(near_refs)
    span = far_ref.shape[2]
    copies = []
    for m in range(near + far_ref.shape[0]):
        columns = pl.ds(pl.multiple_of(jnp.bitwise_xor(mine, m) * span, span), span)
        to = near_refs[m] if m < near else far_ref.at[m - near]
        copies.append(pltpu.make_async_copy(hid_ref.at[:, columns], to, sems.at[m]))
    for copy in copies:
        copy.start()
    return copies


def hidden_kernel(hid_ref, *rest):
    for copy in hidden_moves(hid_ref, rest[:-2], *rest[-2:]):
        copy.wait()


def project_kernel(fsdp, hid_ref, *rest):
    w_refs, out_refs, (parts,) = rest[:fsdp], rest[fsdp:fsdp + KV_HEADS], rest[fsdp + KV_HEADS:]
    mine = lax.axis_index("fsdp")
    head, _ = head_side()
    span = w_refs[0].shape[0]
    total = None
    for m in range(fsdp):
        start = pl.multiple_of(jnp.bitwise_xor(mine, m) * span, span)
        term = matmul(hid_ref[:, pl.ds(start, span)], w_refs[m][...])
        total = term if total is None else total + term
    low = total.astype(jnp.bfloat16)
    for g in range(KV_HEADS):
        key = low[:, g * HEAD_DIM:(g + 1) * HEAD_DIM]
        value = low[:, KEY_WIDTH + g * HEAD_DIM:KEY_WIDTH + (g + 1) * HEAD_DIM]
        parts[g] = jnp.concatenate([key, value], axis=1)
    for m in range(KV_HEADS):
        out_refs[m][...] = parts[jnp.bitwise_xor(head, m)]


def lower_half(shape):
    return lax.broadcasted_iota(jnp.int32, shape, len(shape) - 1) < LOWER


def stacked(key_value):
    wide = key_value.astype(jnp.float32)
    turned = pltpu.roll(wide, LOWER, 1)
    lower = lower_half(wide.shape)
    zero = jnp.zeros_like(wide)
    keys = jnp.concatenate([jnp.where(lower, wide, zero), jnp.where(lower, zero, turned)], axis=0) * SCALE
    values = jnp.concatenate([jnp.where(lower, turned, zero), jnp.where(lower, zero, wide)], axis=0)
    return keys.astype(jnp.bfloat16), values.astype(jnp.bfloat16)


def tile(keys, values, query, grad, stats, mask):
    size, edge = keys.shape[0] // 2, mask.shape[1]
    pairs = len(stats)
    width = query.shape[0] // pairs
    scores = matmul(keys, query, NT)
    prob_grad = matmul(values, grad, NT)
    lows, grads = [], []
    for head in range(2):
        part = slice(head * size, (head + 1) * size)
        lse = jnp.concatenate([lines[head] for lines in stats], axis=1)
        delta = jnp.concatenate([lines[2 + head] for lines in stats], axis=1)
        probs = jnp.exp(scores[part] - lse)
        pieces = []
        for first in range(0, pairs * width, width):
            pieces.append(jnp.where(mask, probs[:, first:first + edge], 0.0))
            if edge < width:
                pieces.append(probs[:, first + edge:first + width])
        probs = jnp.concatenate(pieces, axis=1)
        lows.append(probs.astype(jnp.bfloat16))
        grads.append((probs * (prob_grad[part] - delta)).astype(jnp.bfloat16))
    low, score_grad = jnp.concatenate(lows, axis=0), jnp.concatenate(grads, axis=0)
    return matmul(score_grad, query), matmul(low, grad), matmul(score_grad, keys, TN)


def folded(key_sum, value_sum):
    size = key_sum.shape[0] // 2
    lower = lower_half((size, PAIR))
    straight = jnp.where(lower, key_sum[:size], value_sum[size:])
    crossed = jnp.where(lower, value_sum[:size], key_sum[size:])
    return (straight + pltpu.roll(crossed, LOWER, 1)) * jnp.where(lower, SCALE, 1.0)


def unpacked(part, rows):
    exact = part[rows:, 0:3 * rows].astype(jnp.float32)[0:2 * GROUPS]
    return exact[:, 0:rows] + exact[:, rows:2 * rows] + exact[:, 2 * rows:]


def pair_stats(stat, pair):
    first = 2 * pair
    return [stat[first:first + 1], stat[first + 1:first + 2],
            stat[GROUPS + first:GROUPS + first + 1], stat[GROUPS + first + 1:GROUPS + first + 2]]


def sequence_kernel(near_parts, order_ref, hid_ref, *rest):
    qd_refs, kv_refs, rest = rest[:TEAM], rest[TEAM:TEAM + KV_HEADS], rest[TEAM + KV_HEADS:]
    dkv_refs, keep_ref, send_ref, rest = rest[:KV_HEADS], rest[KV_HEADS], rest[KV_HEADS + 1], rest[KV_HEADS + 2:]
    near_refs, far_ref, rest = rest[:near_parts], rest[near_parts], rest[near_parts + 1:]
    q_all, go_all, stat_all, key_all, value_all, dq_all, dkv_all, sems = rest
    moves = hidden_moves(hid_ref, near_refs, far_ref, sems)
    rows = kv_refs[0].shape[0]
    head, side = head_side()
    near = [order_ref[0, 2 * jnp.bitwise_xor(head, m) + side] for m in range(KV_HEADS)]
    far = [order_ref[0, 2 * jnp.bitwise_xor(head, m) + 1 - side] for m in range(KV_HEADS)]
    for place, ref in zip(near + far, qd_refs):
        for pair in range(PAIRS):
            q_all[pair, place] = ref[0:rows, pair * PAIR:(pair + 1) * PAIR]
            go_all[pair, place] = ref[0:rows, GROUP + pair * PAIR:GROUP + (pair + 1) * PAIR]
        stat_all[place] = unpacked(ref, rows)
    for place, ref in zip(near, kv_refs):
        key_all[place], value_all[place] = stacked(ref[...])
    dq_all[...] = jnp.zeros_like(dq_all)
    for block in range(TEAM):
        mine = functools.reduce(jnp.logical_or, [place == block for place in near])

        @pl.when(mine)
        def _():
            count = TEAM - block
            shape = (rows, rows)
            mask = lax.broadcasted_iota(jnp.int32, shape, 0) <= lax.broadcasted_iota(jnp.int32, shape, 1)
            stats = jnp.concatenate([stat_all[i] for i in range(block, TEAM)], axis=1)
            query = q_all[:, block:].reshape(PAIRS * count * rows, PAIR)
            grad = go_all[:, block:].reshape(PAIRS * count * rows, PAIR)
            key_sum, value_sum, query_part = tile(
                key_all[block], value_all[block], query, grad, [pair_stats(stats, pair) for pair in range(PAIRS)], mask)
            dq_all[:, block:] += query_part.reshape(PAIRS, count, rows, PAIR)
            dkv_all[block] = folded(key_sum, value_sum)

    for m in range(KV_HEADS):
        dkv_refs[m][...] = dkv_all[near[m]].astype(jnp.bfloat16)
        for pair in range(PAIRS):
            columns = slice(pair * PAIR, (pair + 1) * PAIR)
            keep_ref[m, :, columns] = dq_all[pair, near[m]]
            send_ref[m, :, columns] = dq_all[pair, far[m]].astype(jnp.bfloat16)
    for copy in moves:
        copy.wait()


def teams_kernel(order_ref, qd_ref, kv_ref, dkv_ref, keep_ref, send_ref, dq_all):
    rows = kv_ref.shape[1]
    head, side = head_side()
    base = lax.axis_index("ctx") // TEAM * TEAM
    dq_all[...] = jnp.zeros_like(dq_all)

    @pl.loop(0, kv_ref.shape[0])
    def _(block):
        keys, values = stacked(kv_ref[block])
        dkv_ref[block] = jnp.zeros((rows, PAIR), jnp.float32)
        stored = block // KV_HEADS * TEAM + 2 * jnp.bitwise_xor(head, lax.rem(block, KV_HEADS)) + side
        place = order_ref[0, stored]

        @pl.loop(0, TEAM)
        def _(at):
            turned = jnp.where(at < KV_HEADS, side, 1 - side)
            own = order_ref[0, base + 2 * jnp.bitwise_xor(head, lax.rem(at, KV_HEADS)) + turned]

            @pl.when(place <= own)
            def _():
                shape = (rows, rows)
                mask = (place * rows + lax.broadcasted_iota(jnp.int32, shape, 0)
                        <= own * rows + lax.broadcasted_iota(jnp.int32, shape, 1))
                one = qd_ref.at[at]
                stats = unpacked(one, rows)
                for pair in range(PAIRS):
                    first = pair * PAIR
                    key_part, value_part, query_part = tile(
                        keys, values, one[0:rows, first:first + PAIR], one[0:rows, GROUP + first:GROUP + first + PAIR],
                        [pair_stats(stats, pair)], mask)
                    dq_all[at, :, first:first + PAIR] += query_part
                    dkv_ref[block] += folded(key_part, value_part)

    keep_ref[...] = dq_all[0:KV_HEADS]
    send_ref[...] = dq_all[KV_HEADS:].astype(jnp.bfloat16)


def owner_kernel(*rest):
    dkv_refs, out_ref, parts = rest[:KV_HEADS], rest[KV_HEADS], rest[KV_HEADS + 1]
    head, _ = head_side()
    for m in range(KV_HEADS):
        parts[jnp.bitwise_xor(head, m)] = dkv_refs[m][...]
    keys = [parts[g, :, :HEAD_DIM] for g in range(KV_HEADS)]
    values = [parts[g, :, HEAD_DIM:] for g in range(KV_HEADS)]
    out_ref[...] = jnp.concatenate(keys + values, axis=1)


def pair_kernel(keep_ref, got_ref, *out_refs):
    for m in range(KV_HEADS):
        out_refs[m][...] = (keep_ref[m] + got_ref[m].astype(jnp.float32)).astype(out_refs[m].dtype)


def query_kernel(*rest):
    dq_refs, out_ref = rest[:KV_HEADS], rest[KV_HEADS]
    head, _ = head_side()
    for m in range(KV_HEADS):
        columns = pl.ds(pl.multiple_of(jnp.bitwise_xor(head, m) * GROUP, GROUP), GROUP)
        out_ref[:, columns] = dq_refs[m][...]


def input_kernel(fsdp, grad_ref, *rest):
    w_refs, out_ref = rest[:fsdp], rest[fsdp]
    mine = lax.axis_index("fsdp")
    span = w_refs[0].shape[0]
    for m in range(fsdp):
        start = pl.multiple_of(jnp.bitwise_xor(mine, m) * span, span)
        out_ref[:, pl.ds(start, span)] = matmul(grad_ref[...], w_refs[m][...], NT).astype(jnp.bfloat16)


def weight_sums(fsdp, refs):
    hid = jnp.concatenate([ref[...] for ref in refs[:fsdp]], axis=0)
    grad = jnp.concatenate([ref[...] for ref in refs[fsdp:2 * fsdp]], axis=0)
    return matmul(hid, grad, TN)


def weight_kernel(fsdp, *rest):
    rest[2 * fsdp][...] = weight_sums(fsdp, rest).astype(jnp.bfloat16)


def sides_kernel(fsdp, *rest):
    keep_ref, send_ref, parts = rest[2 * fsdp:]
    head, side = head_side()
    parts[...] = weight_sums(fsdp, rest).reshape(parts.shape)
    for m in range(KV_HEADS):
        to = 2 * jnp.bitwise_xor(head, m)
        keep_ref[m] = parts[to + side]
        send_ref[m] = parts[to + 1 - side].astype(jnp.bfloat16)


def own_total_kernel(own_ref, *rest):
    total = own_ref[...]
    for ref in rest[:-1]:
        total = total + ref[...].astype(jnp.float32)
    rest[-1][...] = total


def total_kernel(part_ref, out_ref):
    total = part_ref[0].astype(jnp.float32)
    for i in range(1, part_ref.shape[0]):
        total = total + part_ref[i].astype(jnp.float32)
    out_ref[...] = total


def over_fsdp(own, bits):
    got = list(own)
    while bits:
        for m in range(len(own)):
            if m & bits:
                got[m] = swapped(got[m], "fsdp", bits)
        bits //= 2
    return got


def shards(hidden, queries, attn_out, grad_out, log_sums, block_order, w_kv):
    rows, model = hidden.shape[1:]
    fsdp, devices = lax.axis_size("fsdp"), lax.axis_size("ctx")
    teams = devices // TEAM
    f32 = jnp.float32
    span = model // fsdp
    inputs = hidden[0]
    columns = 2 * KEY_WIDTH
    block, wide = (rows, PAIR), (rows, GROUP)

    def along_heads(arrays):
        return [arrays[0]] + [swapped(arrays[m], "ctx", 2 * m) for m in range(1, KV_HEADS)]

    far = fsdp // 2
    qd = call(
        pieces_kernel, [sds((rows + 16, 2 * GROUP))] * KV_HEADS,
        [pltpu.VMEM((rows, Q_HEADS * HEAD_DIM), jnp.bfloat16)] * 2
        + [pltpu.VMEM((Q_HEADS, rows), f32), pltpu.VMEM((KV_HEADS, 2 * GROUPS, rows), f32),
           pltpu.SemaphoreType.DMA((3 + 2 * KV_HEADS,))],
        (queries[0], grad_out[0], attn_out[0], log_sums[0]), hbm=4)
    qd = along_heads(qd)
    turned = [swapped(one, "ctx", 1) for one in qd[:2]]
    w_far = held(swapped(w_kv, "fsdp", far), (*qd[1:], *turned))
    w_parts = over_fsdp([w_kv] * far + [w_far] * (fsdp - far), far // 2)

    kv = call(
        functools.partial(project_kernel, fsdp), [sds(block)] * KV_HEADS,
        [pltpu.VMEM((KV_HEADS,) + block, jnp.bfloat16)], (inputs, *w_parts))
    kv = along_heads(kv)
    qd = qd + turned + [swapped(one, "ctx", 1) for one in qd[2:]]

    half = (KV_HEADS,) + wide
    cut = [sds((rows, span))] * far + [sds((fsdp - far, rows, span))]
    cut_sems = pltpu.SemaphoreType.DMA((fsdp,))
    if teams == 1:
        outs = call(
            functools.partial(sequence_kernel, far), [sds(block)] * KV_HEADS + [sds(half, f32), sds(half)] + cut,
            [pltpu.VMEM((PAIRS, TEAM) + block, jnp.bfloat16)] * 2 + [pltpu.VMEM((TEAM, 2 * GROUPS, rows), f32)]
            + [pltpu.VMEM((TEAM, 2 * rows, PAIR), jnp.bfloat16)] * 2
            + [pltpu.VMEM((PAIRS, TEAM) + block, f32), pltpu.VMEM((TEAM,) + block, f32), cut_sems],
            (block_order, inputs, *qd, *kv), smem=1, hbm=1)
        dkv, (keep, give, *hid, hid_far) = outs[:KV_HEADS], outs[KV_HEADS:]
    else:
        alike = [[t * TEAM + i for t in range(teams)] for i in range(TEAM)]
        kv = lax.all_gather(jnp.stack(kv), "ctx", axis_index_groups=alike, axis=0, tiled=True)
        dkv, keep, give = call(
            teams_kernel, [sds((teams * KV_HEADS,) + block, f32), sds(half, f32), sds(half)],
            [pltpu.VMEM((TEAM,) + wide, f32)], (block_order, jnp.stack(qd), kv), smem=1)
        dkv = lax.psum_scatter(dkv, "ctx", axis_index_groups=alike, scatter_dimension=0, tiled=True)
        dkv = [dkv[m].astype(jnp.bfloat16) for m in range(KV_HEADS)]
        *hid, hid_far = call(hidden_kernel, cut, [cut_sems], (inputs,), hbm=1)

    hid_far = swapped(hid_far, "fsdp", far)
    hid = over_fsdp(hid + [hid_far[m] for m in range(fsdp - far)], far // 2)
    dkv = along_heads(dkv)
    give = swapped(give, "ctx", 1)
    (kv_grad,) = call(
        owner_kernel, [sds((rows, columns))], [pltpu.VMEM((KV_HEADS,) + block, jnp.bfloat16)],
        dkv, after=(give,))
    grads = over_fsdp([kv_grad] * fsdp, far)
    if teams == 1:
        share = (span // devices, columns)
        own_sums, send_sums = call(
            functools.partial(sides_kernel, fsdp), [sds((KV_HEADS,) + share, f32), sds((KV_HEADS,) + share)],
            [pltpu.VMEM((devices,) + share, f32)], (*hid, *grads))
        formed = (own_sums,)
        dq = along_heads(call(pair_kernel, [sds(wide)] * KV_HEADS, [], (keep, give), after=formed))
        sums = call(
            pair_kernel, [sds(share, f32)] + [sds(share)] * (KV_HEADS - 1), [],
            (own_sums, swapped(send_sums, "ctx", 1)), after=dq[2:3])
        (weight_grads,) = call(own_total_kernel, [sds(share, f32)], [], along_heads(sums))
    else:
        formed = call(functools.partial(weight_kernel, fsdp), [sds((span, columns))], [], (*hid, *grads))
        dq = along_heads(call(pair_kernel, [sds(wide)] * KV_HEADS, [], (keep, give), after=formed))
        sums = lax.all_to_all(formed[0].reshape(devices, span // devices, columns), "ctx", 0, 0, tiled=True)
        (weight_grads,) = call(total_kernel, [sds((span // devices, columns), f32)], [], (sums,))
    (query_grads,) = call(query_kernel, [sds((rows, Q_HEADS * HEAD_DIM))], [], dq, after=formed)
    (input_grads,) = call(
        functools.partial(input_kernel, fsdp), [sds((rows, model))], [], (kv_grad, *w_parts), after=formed)
    return query_grads[None], input_grads[None], weight_grads


def solution(mesh):
    return jax.shard_map(
        shards,
        mesh=mesh,
        in_specs=(
            P("fsdp", "ctx", None),
            P("fsdp", "ctx", None),
            P("fsdp", "ctx", None),
            P("fsdp", "ctx", None),
            P("fsdp", None, "ctx"),
            P("fsdp", None),
            P("fsdp", None),
        ),
        out_specs=(P("fsdp", "ctx", None), P("fsdp", "ctx", None), P(("fsdp", "ctx"), None)),
        check_vma=False,
    )
```

```python
import functools

import jax
import jax.numpy as jnp
from jax import lax
from jax.experimental import pallas as pl
from jax.experimental.pallas import tpu as pltpu
from jax.sharding import PartitionSpec as P

Q_HEADS = 16
KV_HEADS = 4
HEAD_DIM = 64
GROUPS = Q_HEADS // KV_HEADS
KEY_WIDTH = KV_HEADS * HEAD_DIM
PAIR = 2 * HEAD_DIM
TEAM = 2 * KV_HEADS
PAIRS = GROUPS // 2
GROUP = GROUPS * HEAD_DIM
SCALE = HEAD_DIM ** -0.5
LOWER = HEAD_DIM

NT = (((1,), (1,)), ((), ()))
TN = (((0,), (0,)), ((), ()))
VMEM = pl.BlockSpec(memory_space=pltpu.VMEM)
SMEM = pl.BlockSpec(memory_space=pltpu.SMEM)
ANY = pl.BlockSpec(memory_space=pl.ANY)
HBM = pl.BlockSpec(memory_space=pltpu.HBM)
PARAMS = pltpu.CompilerParams(vmem_limit_bytes=40 * 1024 * 1024)
WHOLE = pltpu.CompilerParams(vmem_limit_bytes=60 * 1024 * 1024)


def matmul(left, right, dims=(((1,), (0,)), ((), ()))):
    return lax.dot_general(left, right, dims, preferred_element_type=jnp.float32)


def swapped(array, axis, bits):
    size = lax.axis_size(axis)
    return lax.ppermute(array, axis, [(i, i ^ bits) for i in range(size)])


def call(kernel, out_shape, scratch, args, smem=0, hbm=0, after=()):
    given = len(args)
    params = WHOLE if hbm == given else PARAMS

    def body(*refs):
        kernel(*refs[:given], *refs[given + len(after):])

    specs = [SMEM] * smem + [HBM] * hbm + [VMEM] * (given - smem - hbm) + [ANY] * len(after)
    return pl.pallas_call(
        body,
        out_shape=out_shape,
        in_specs=specs,
        out_specs=[VMEM] * len(out_shape),
        scratch_shapes=scratch,
        compiler_params=params,
    )(*args, *after)


def held(array, after):
    def body(*refs):
        pass

    return pl.pallas_call(
        body,
        out_shape=sds(array.shape, array.dtype),
        in_specs=[ANY] * (1 + len(after)),
        out_specs=ANY,
        input_output_aliases={0: 0},
        compiler_params=PARAMS,
    )(array, *after)


def sds(shape, dtype=jnp.bfloat16):
    return jax.ShapeDtypeStruct(shape, dtype)


def head_side():
    me = lax.rem(lax.axis_index("ctx"), TEAM)
    return me // 2, lax.rem(me, 2)


def far_first(arrays):
    return [arrays[m] for m in (0, 2, 3, 1)]


def by_head(refs):
    return [refs[i] for i in (0, 3, 1, 2)]


def split(exact):
    first = exact.astype(jnp.bfloat16).astype(jnp.float32)
    second = (exact - first).astype(jnp.bfloat16).astype(jnp.float32)
    return first, second, exact - first - second


def pieces_kernel(q_ref, go_ref, ao_ref, lse_ref, *rest):
    out_refs, (grad, output, lse, stat, sems) = rest[:KV_HEADS], rest[KV_HEADS:]
    rows, width = q_ref.shape
    head, _ = head_side()
    loads = [pltpu.make_async_copy(ref, to, sems.at[i])
             for i, (ref, to) in enumerate(((go_ref, grad), (ao_ref, output), (lse_ref, lse)))]
    moves = []
    for m in range(KV_HEADS):
        columns = pl.ds(pl.multiple_of(jnp.bitwise_xor(head, m) * GROUP, GROUP), GROUP)
        for i, ref in enumerate((q_ref, go_ref)):
            moves.append(pltpu.make_async_copy(
                ref.at[:, columns], out_refs[m].at[0:rows, i * GROUP:(i + 1) * GROUP], sems.at[3 + 2 * m + i]))
    for copy in loads + moves:
        copy.start()
    for copy in loads:
        copy.wait()
    product = grad[...].astype(jnp.float32) * output[...].astype(jnp.float32)
    high = product.astype(jnp.bfloat16)
    low = (product - high.astype(jnp.float32)).astype(jnp.bfloat16)
    head_of = lax.broadcasted_iota(jnp.int32, (Q_HEADS, width), 1) // HEAD_DIM
    ones = (head_of == lax.broadcasted_iota(jnp.int32, (Q_HEADS, width), 0)).astype(jnp.bfloat16)
    delta = matmul(ones, high, NT) + matmul(ones, low, NT)
    for g in range(KV_HEADS):
        part = slice(g * GROUPS, (g + 1) * GROUPS)
        stat[g] = jnp.concatenate([lse[part, :], delta[part, :]], axis=0)
    zero = jnp.zeros((2 * GROUPS, rows), jnp.float32)
    for m in range(KV_HEADS):
        lines = [*split(stat[jnp.bitwise_xor(head, m)]), zero]
        for i, one in enumerate(lines):
            full = jnp.concatenate([one, zero], axis=0).astype(jnp.bfloat16)
            out_refs[m][rows:, i * rows:(i + 1) * rows] = full
    for copy in moves:
        copy.wait()


def hidden_moves(hid_ref, near_refs, far_ref, sems):
    mine = lax.axis_index("fsdp")
    near = len(near_refs)
    span = far_ref.shape[2]
    copies = []
    for m in range(near + far_ref.shape[0]):
        columns = pl.ds(pl.multiple_of(jnp.bitwise_xor(mine, m) * span, span), span)
        to = near_refs[m] if m < near else far_ref.at[m - near]
        copies.append(pltpu.make_async_copy(hid_ref.at[:, columns], to, sems.at[m]))
    for copy in copies:
        copy.start()
    return copies


def hidden_kernel(hid_ref, *rest):
    for copy in hidden_moves(hid_ref, rest[:-2], *rest[-2:]):
        copy.wait()


def project_kernel(fsdp, hid_ref, *rest):
    w_refs, out_refs, (parts,) = rest[:fsdp], rest[fsdp:fsdp + KV_HEADS], rest[fsdp + KV_HEADS:]
    mine = lax.axis_index("fsdp")
    head, _ = head_side()
    span = w_refs[0].shape[0]
    total = None
    for m in range(fsdp):
        start = pl.multiple_of(jnp.bitwise_xor(mine, m) * span, span)
        term = matmul(hid_ref[:, pl.ds(start, span)], w_refs[m][...])
        total = term if total is None else total + term
    low = total.astype(jnp.bfloat16)
    for g in range(KV_HEADS):
        key = low[:, g * HEAD_DIM:(g + 1) * HEAD_DIM]
        value = low[:, KEY_WIDTH + g * HEAD_DIM:KEY_WIDTH + (g + 1) * HEAD_DIM]
        parts[g] = jnp.concatenate([key, value], axis=1)
    for m in range(KV_HEADS):
        out_refs[m][...] = parts[jnp.bitwise_xor(head, m)]


def lower_half(shape):
    return lax.broadcasted_iota(jnp.int32, shape, len(shape) - 1) < LOWER


def stacked(key_value):
    wide = key_value.astype(jnp.float32)
    turned = pltpu.roll(wide, LOWER, 1)
    lower = lower_half(wide.shape)
    zero = jnp.zeros_like(wide)
    keys = jnp.concatenate([jnp.where(lower, wide, zero), jnp.where(lower, zero, turned)], axis=0) * SCALE
    values = jnp.concatenate([jnp.where(lower, turned, zero), jnp.where(lower, zero, wide)], axis=0)
    return keys.astype(jnp.bfloat16), values.astype(jnp.bfloat16)


def tile(keys, values, query, grad, stats, mask):
    size, edge = keys.shape[0] // 2, mask.shape[1]
    pairs = len(stats)
    width = query.shape[0] // pairs
    scores = matmul(keys, query, NT)
    prob_grad = matmul(values, grad, NT)
    lows, grads = [], []
    for head in range(2):
        part = slice(head * size, (head + 1) * size)
        lse = jnp.concatenate([lines[head] for lines in stats], axis=1)
        delta = jnp.concatenate([lines[2 + head] for lines in stats], axis=1)
        probs = jnp.exp(scores[part] - lse)
        pieces = []
        for first in range(0, pairs * width, width):
            pieces.append(jnp.where(mask, probs[:, first:first + edge], 0.0))
            if edge < width:
                pieces.append(probs[:, first + edge:first + width])
        probs = jnp.concatenate(pieces, axis=1)
        lows.append(probs.astype(jnp.bfloat16))
        grads.append((probs * (prob_grad[part] - delta)).astype(jnp.bfloat16))
    low, score_grad = jnp.concatenate(lows, axis=0), jnp.concatenate(grads, axis=0)
    return matmul(score_grad, query), matmul(low, grad), matmul(score_grad, keys, TN)


def folded(key_sum, value_sum):
    size = key_sum.shape[0] // 2
    lower = lower_half((size, PAIR))
    straight = jnp.where(lower, key_sum[:size], value_sum[size:])
    crossed = jnp.where(lower, value_sum[:size], key_sum[size:])
    return (straight + pltpu.roll(crossed, LOWER, 1)) * jnp.where(lower, SCALE, 1.0)


def unpacked(part, rows):
    exact = part[rows:, 0:3 * rows].astype(jnp.float32)[0:2 * GROUPS]
    return exact[:, 0:rows] + exact[:, rows:2 * rows] + exact[:, 2 * rows:]


def pair_stats(stat, pair):
    first = 2 * pair
    return [stat[first:first + 1], stat[first + 1:first + 2],
            stat[GROUPS + first:GROUPS + first + 1], stat[GROUPS + first + 1:GROUPS + first + 2]]


def sequence_kernel(near_parts, order_ref, hid_ref, *rest):
    qd_refs, kv_refs, rest = rest[:TEAM], rest[TEAM:TEAM + KV_HEADS], rest[TEAM + KV_HEADS:]
    dkv_refs, keep_ref, send_ref, rest = rest[:KV_HEADS], rest[KV_HEADS], rest[KV_HEADS + 1], rest[KV_HEADS + 2:]
    near_refs, far_ref, rest = rest[:near_parts], rest[near_parts], rest[near_parts + 1:]
    q_all, go_all, stat_all, key_all, value_all, dq_all, dkv_all, sems = rest
    moves = hidden_moves(hid_ref, near_refs, far_ref, sems)
    rows = kv_refs[0].shape[0]
    head, side = head_side()
    near = [order_ref[0, 2 * jnp.bitwise_xor(head, m) + side] for m in range(KV_HEADS)]
    far = [order_ref[0, 2 * jnp.bitwise_xor(head, m) + 1 - side] for m in range(KV_HEADS)]
    for place, ref in zip(near + far, qd_refs):
        for pair in range(PAIRS):
            q_all[pair, place] = ref[0:rows, pair * PAIR:(pair + 1) * PAIR]
            go_all[pair, place] = ref[0:rows, GROUP + pair * PAIR:GROUP + (pair + 1) * PAIR]
        stat_all[place] = unpacked(ref, rows)
    for place, ref in zip(near, by_head(kv_refs)):
        key_all[place], value_all[place] = stacked(ref[...])
    dq_all[...] = jnp.zeros_like(dq_all)
    for block in range(TEAM):
        mine = functools.reduce(jnp.logical_or, [place == block for place in near])

        @pl.when(mine)
        def _():
            count = TEAM - block
            shape = (rows, rows)
            mask = lax.broadcasted_iota(jnp.int32, shape, 0) <= lax.broadcasted_iota(jnp.int32, shape, 1)
            stats = jnp.concatenate([stat_all[i] for i in range(block, TEAM)], axis=1)
            query = q_all[:, block:].reshape(PAIRS * count * rows, PAIR)
            grad = go_all[:, block:].reshape(PAIRS * count * rows, PAIR)
            key_sum, value_sum, query_part = tile(
                key_all[block], value_all[block], query, grad, [pair_stats(stats, pair) for pair in range(PAIRS)], mask)
            dq_all[:, block:] += query_part.reshape(PAIRS, count, rows, PAIR)
            dkv_all[block] = folded(key_sum, value_sum)

    for m in range(KV_HEADS):
        dkv_refs[m][...] = dkv_all[near[m]].astype(jnp.bfloat16)
        for pair in range(PAIRS):
            columns = slice(pair * PAIR, (pair + 1) * PAIR)
            keep_ref[m, :, columns] = dq_all[pair, near[m]]
            send_ref[m, :, columns] = dq_all[pair, far[m]].astype(jnp.bfloat16)
    for copy in moves:
        copy.wait()


def teams_kernel(order_ref, qd_ref, kv_ref, dkv_ref, keep_ref, send_ref, dq_all):
    rows = kv_ref.shape[1]
    head, side = head_side()
    base = lax.axis_index("ctx") // TEAM * TEAM
    dq_all[...] = jnp.zeros_like(dq_all)

    @pl.loop(0, kv_ref.shape[0])
    def _(block):
        keys, values = stacked(kv_ref[block])
        dkv_ref[block] = jnp.zeros((rows, PAIR), jnp.float32)
        stored = block // KV_HEADS * TEAM + 2 * jnp.bitwise_xor(head, lax.rem(block, KV_HEADS)) + side
        place = order_ref[0, stored]

        @pl.loop(0, TEAM)
        def _(at):
            turned = jnp.where(at < KV_HEADS, side, 1 - side)
            own = order_ref[0, base + 2 * jnp.bitwise_xor(head, lax.rem(at, KV_HEADS)) + turned]

            @pl.when(place <= own)
            def _():
                shape = (rows, rows)
                mask = (place * rows + lax.broadcasted_iota(jnp.int32, shape, 0)
                        <= own * rows + lax.broadcasted_iota(jnp.int32, shape, 1))
                one = qd_ref.at[at]
                stats = unpacked(one, rows)
                for pair in range(PAIRS):
                    first = pair * PAIR
                    key_part, value_part, query_part = tile(
                        keys, values, one[0:rows, first:first + PAIR], one[0:rows, GROUP + first:GROUP + first + PAIR],
                        [pair_stats(stats, pair)], mask)
                    dq_all[at, :, first:first + PAIR] += query_part
                    dkv_ref[block] += folded(key_part, value_part)

    keep_ref[...] = dq_all[0:KV_HEADS]
    send_ref[...] = dq_all[KV_HEADS:].astype(jnp.bfloat16)


def owner_kernel(*rest):
    dkv_refs, out_ref, parts = rest[:KV_HEADS], rest[KV_HEADS], rest[KV_HEADS + 1]
    head, _ = head_side()
    for m, ref in enumerate(by_head(dkv_refs)):
        parts[jnp.bitwise_xor(head, m)] = ref[...]
    keys = [parts[g, :, :HEAD_DIM] for g in range(KV_HEADS)]
    values = [parts[g, :, HEAD_DIM:] for g in range(KV_HEADS)]
    out_ref[...] = jnp.concatenate(keys + values, axis=1)


def pair_kernel(keep_ref, got_ref, *out_refs):
    for m in range(KV_HEADS):
        out_refs[m][...] = (keep_ref[m] + got_ref[m].astype(jnp.float32)).astype(out_refs[m].dtype)


def query_kernel(*rest):
    dq_refs, out_ref = rest[:KV_HEADS], rest[KV_HEADS]
    head, _ = head_side()
    for m, ref in enumerate(by_head(dq_refs)):
        columns = pl.ds(pl.multiple_of(jnp.bitwise_xor(head, m) * GROUP, GROUP), GROUP)
        out_ref[:, columns] = ref[...]


def input_kernel(fsdp, grad_ref, *rest):
    w_refs, out_ref = rest[:fsdp], rest[fsdp]
    mine = lax.axis_index("fsdp")
    span = w_refs[0].shape[0]
    for m in range(fsdp):
        start = pl.multiple_of(jnp.bitwise_xor(mine, m) * span, span)
        out_ref[:, pl.ds(start, span)] = matmul(grad_ref[...], w_refs[m][...], NT).astype(jnp.bfloat16)


def weight_sums(fsdp, refs):
    hid = jnp.concatenate([ref[...] for ref in refs[:fsdp]], axis=0)
    grad = jnp.concatenate([ref[...] for ref in refs[fsdp:2 * fsdp]], axis=0)
    return matmul(hid, grad, TN)


def weight_kernel(fsdp, *rest):
    rest[2 * fsdp][...] = weight_sums(fsdp, rest).astype(jnp.bfloat16)


def sides_kernel(fsdp, *rest):
    keep_ref, send_ref, parts = rest[2 * fsdp:]
    head, side = head_side()
    parts[...] = weight_sums(fsdp, rest).reshape(parts.shape)
    for m in range(KV_HEADS):
        to = 2 * jnp.bitwise_xor(head, m)
        keep_ref[m] = parts[to + side]
        send_ref[m] = parts[to + 1 - side].astype(jnp.bfloat16)


def own_total_kernel(own_ref, *rest):
    total = own_ref[...]
    for ref in rest[:-1]:
        total = total + ref[...].astype(jnp.float32)
    rest[-1][...] = total


def total_kernel(part_ref, out_ref):
    total = part_ref[0].astype(jnp.float32)
    for i in range(1, part_ref.shape[0]):
        total = total + part_ref[i].astype(jnp.float32)
    out_ref[...] = total


def over_fsdp(own, bits):
    got = list(own)
    while bits:
        for m in range(len(own)):
            if m & bits:
                got[m] = swapped(got[m], "fsdp", bits)
        bits //= 2
    return got


def shards(hidden, queries, attn_out, grad_out, log_sums, block_order, w_kv):
    rows, model = hidden.shape[1:]
    fsdp, devices = lax.axis_size("fsdp"), lax.axis_size("ctx")
    teams = devices // TEAM
    f32 = jnp.float32
    span = model // fsdp
    inputs = hidden[0]
    columns = 2 * KEY_WIDTH
    block, wide = (rows, PAIR), (rows, GROUP)

    def along_heads(arrays):
        return [arrays[0]] + [swapped(arrays[m], "ctx", 2 * m) for m in range(1, KV_HEADS)]

    far = fsdp // 2
    qd = call(
        pieces_kernel, [sds((rows + 16, 2 * GROUP))] * KV_HEADS,
        [pltpu.VMEM((rows, Q_HEADS * HEAD_DIM), jnp.bfloat16)] * 2
        + [pltpu.VMEM((Q_HEADS, rows), f32), pltpu.VMEM((KV_HEADS, 2 * GROUPS, rows), f32),
           pltpu.SemaphoreType.DMA((3 + 2 * KV_HEADS,))],
        (queries[0], grad_out[0], attn_out[0], log_sums[0]), hbm=4)
    qd = along_heads(qd)
    turned = [swapped(one, "ctx", 1) for one in qd[:2]]
    w_far = held(swapped(w_kv, "fsdp", far), (*far_first(qd[:KV_HEADS])[1:], *turned))
    w_parts = over_fsdp([w_kv] * far + [w_far] * (fsdp - far), far // 2)

    kv = call(
        functools.partial(project_kernel, fsdp), [sds(block)] * KV_HEADS,
        [pltpu.VMEM((KV_HEADS,) + block, jnp.bfloat16)], (inputs, *w_parts))
    kv = along_heads(kv)
    qd = qd + turned + [swapped(one, "ctx", 1) for one in qd[2:]]

    half = (KV_HEADS,) + wide
    cut = [sds((rows, span))] * far + [sds((fsdp - far, rows, span))]
    cut_sems = pltpu.SemaphoreType.DMA((fsdp,))
    if teams == 1:
        outs = call(
            functools.partial(sequence_kernel, far), [sds(block)] * KV_HEADS + [sds(half, f32), sds(half)] + cut,
            [pltpu.VMEM((PAIRS, TEAM) + block, jnp.bfloat16)] * 2 + [pltpu.VMEM((TEAM, 2 * GROUPS, rows), f32)]
            + [pltpu.VMEM((TEAM, 2 * rows, PAIR), jnp.bfloat16)] * 2
            + [pltpu.VMEM((PAIRS, TEAM) + block, f32), pltpu.VMEM((TEAM,) + block, f32), cut_sems],
            (block_order, inputs, *qd, *far_first(kv)), smem=1, hbm=1)
        dkv, (keep, give, *hid, hid_far) = outs[:KV_HEADS], outs[KV_HEADS:]
    else:
        alike = [[t * TEAM + i for t in range(teams)] for i in range(TEAM)]
        kv = lax.all_gather(jnp.stack(kv), "ctx", axis_index_groups=alike, axis=0, tiled=True)
        dkv, keep, give = call(
            teams_kernel, [sds((teams * KV_HEADS,) + block, f32), sds(half, f32), sds(half)],
            [pltpu.VMEM((TEAM,) + wide, f32)], (block_order, jnp.stack(qd), kv), smem=1)
        dkv = lax.psum_scatter(dkv, "ctx", axis_index_groups=alike, scatter_dimension=0, tiled=True)
        dkv = [dkv[m].astype(jnp.bfloat16) for m in range(KV_HEADS)]
        *hid, hid_far = call(hidden_kernel, cut, [cut_sems], (inputs,), hbm=1)

    hid_far = swapped(hid_far, "fsdp", far)
    hid = over_fsdp(hid + [hid_far[m] for m in range(fsdp - far)], far // 2)
    dkv = along_heads(dkv)
    give = swapped(give, "ctx", 1)
    (kv_grad,) = call(
        owner_kernel, [sds((rows, columns))], [pltpu.VMEM((KV_HEADS,) + block, jnp.bfloat16)],
        far_first(dkv), after=(give,))
    grads = over_fsdp([kv_grad] * fsdp, far)
    if teams == 1:
        share = (span // devices, columns)
        own_sums, send_sums = call(
            functools.partial(sides_kernel, fsdp), [sds((KV_HEADS,) + share, f32), sds((KV_HEADS,) + share)],
            [pltpu.VMEM((devices,) + share, f32)], (*hid, *grads))
        formed = (own_sums,)
        dq = along_heads(call(pair_kernel, [sds(wide)] * KV_HEADS, [], (keep, give), after=formed))
        sums = call(
            pair_kernel, [sds(share, f32)] + [sds(share)] * (KV_HEADS - 1), [],
            (own_sums, swapped(send_sums, "ctx", 1)), after=dq[2:3])
        (weight_grads,) = call(own_total_kernel, [sds(share, f32)], [], far_first(along_heads(sums)))
    else:
        formed = call(functools.partial(weight_kernel, fsdp), [sds((span, columns))], [], (*hid, *grads))
        dq = along_heads(call(pair_kernel, [sds(wide)] * KV_HEADS, [], (keep, give), after=formed))
        sums = lax.all_to_all(formed[0].reshape(devices, span // devices, columns), "ctx", 0, 0, tiled=True)
        (weight_grads,) = call(total_kernel, [sds((span // devices, columns), f32)], [], (sums,))
    (query_grads,) = call(query_kernel, [sds((rows, Q_HEADS * HEAD_DIM))], [], far_first(dq), after=formed)
    (input_grads,) = call(
        functools.partial(input_kernel, fsdp), [sds((rows, model))], [], (kv_grad, *w_parts), after=formed)
    return query_grads[None], input_grads[None], weight_grads


def solution(mesh):
    return jax.shard_map(
        shards,
        mesh=mesh,
        in_specs=(
            P("fsdp", "ctx", None),
            P("fsdp", "ctx", None),
            P("fsdp", "ctx", None),
            P("fsdp", "ctx", None),
            P("fsdp", None, "ctx"),
            P("fsdp", None),
            P("fsdp", None),
        ),
        out_specs=(P("fsdp", "ctx", None), P("fsdp", "ctx", None), P(("fsdp", "ctx"), None)),
        check_vma=False,
    )
```

```python
import functools

import jax
import jax.numpy as jnp
from jax import lax
from jax.experimental import pallas as pl
from jax.experimental.pallas import tpu as pltpu
from jax.sharding import PartitionSpec as P

Q_HEADS = 16
KV_HEADS = 4
HEAD_DIM = 64
GROUPS = Q_HEADS // KV_HEADS
KEY_WIDTH = KV_HEADS * HEAD_DIM
PAIR = 2 * HEAD_DIM
TEAM = 2 * KV_HEADS
PAIRS = GROUPS // 2
GROUP = GROUPS * HEAD_DIM
SCALE = HEAD_DIM ** -0.5
LOWER = HEAD_DIM

NT = (((1,), (1,)), ((), ()))
TN = (((0,), (0,)), ((), ()))
VMEM = pl.BlockSpec(memory_space=pltpu.VMEM)
SMEM = pl.BlockSpec(memory_space=pltpu.SMEM)
ANY = pl.BlockSpec(memory_space=pl.ANY)
HBM = pl.BlockSpec(memory_space=pltpu.HBM)
PARAMS = pltpu.CompilerParams(vmem_limit_bytes=40 * 1024 * 1024)
WHOLE = pltpu.CompilerParams(vmem_limit_bytes=60 * 1024 * 1024)


def matmul(left, right, dims=(((1,), (0,)), ((), ()))):
    return lax.dot_general(left, right, dims, preferred_element_type=jnp.float32)


def swapped(array, axis, bits):
    size = lax.axis_size(axis)
    return lax.ppermute(array, axis, [(i, i ^ bits) for i in range(size)])


def call(kernel, out_shape, scratch, args, smem=0, hbm=0, after=()):
    given = len(args)
    params = WHOLE if hbm == given else PARAMS

    def body(*refs):
        kernel(*refs[:given], *refs[given + len(after):])

    specs = [SMEM] * smem + [HBM] * hbm + [VMEM] * (given - smem - hbm) + [ANY] * len(after)
    return pl.pallas_call(
        body,
        out_shape=out_shape,
        in_specs=specs,
        out_specs=[VMEM] * len(out_shape),
        scratch_shapes=scratch,
        compiler_params=params,
    )(*args, *after)


def held(array, after):
    def body(*refs):
        pass

    return pl.pallas_call(
        body,
        out_shape=sds(array.shape, array.dtype),
        in_specs=[ANY] * (1 + len(after)),
        out_specs=ANY,
        input_output_aliases={0: 0},
        compiler_params=PARAMS,
    )(array, *after)


def sds(shape, dtype=jnp.bfloat16):
    return jax.ShapeDtypeStruct(shape, dtype)


def head_side():
    me = lax.rem(lax.axis_index("ctx"), TEAM)
    return me // 2, lax.rem(me, 2)


def far_first(arrays):
    return [arrays[m] for m in (0, 2, 3, 1)]


def by_head(refs):
    return [refs[i] for i in (0, 3, 1, 2)]


def split(exact):
    first = exact.astype(jnp.bfloat16).astype(jnp.float32)
    second = (exact - first).astype(jnp.bfloat16).astype(jnp.float32)
    return first, second, exact - first - second


def pieces_kernel(q_ref, go_ref, ao_ref, lse_ref, *rest):
    out_refs, (grad, output, lse, stat, sems) = rest[:KV_HEADS], rest[KV_HEADS:]
    rows, width = q_ref.shape
    head, _ = head_side()
    loads = [pltpu.make_async_copy(ref, to, sems.at[i])
             for i, (ref, to) in enumerate(((go_ref, grad), (ao_ref, output), (lse_ref, lse)))]
    moves = []
    for m in range(KV_HEADS):
        columns = pl.ds(pl.multiple_of(jnp.bitwise_xor(head, m) * GROUP, GROUP), GROUP)
        for i, ref in enumerate((q_ref, go_ref)):
            moves.append(pltpu.make_async_copy(
                ref.at[:, columns], out_refs[m].at[0:rows, i * GROUP:(i + 1) * GROUP], sems.at[3 + 2 * m + i]))
    for copy in loads + moves:
        copy.start()
    for copy in loads:
        copy.wait()
    product = grad[...].astype(jnp.float32) * output[...].astype(jnp.float32)
    high = product.astype(jnp.bfloat16)
    low = (product - high.astype(jnp.float32)).astype(jnp.bfloat16)
    head_of = lax.broadcasted_iota(jnp.int32, (Q_HEADS, width), 1) // HEAD_DIM
    ones = (head_of == lax.broadcasted_iota(jnp.int32, (Q_HEADS, width), 0)).astype(jnp.bfloat16)
    delta = matmul(ones, high, NT) + matmul(ones, low, NT)
    for g in range(KV_HEADS):
        part = slice(g * GROUPS, (g + 1) * GROUPS)
        stat[g] = jnp.concatenate([lse[part, :], delta[part, :]], axis=0)
    zero = jnp.zeros((2 * GROUPS, rows), jnp.float32)
    for m in range(KV_HEADS):
        lines = [*split(stat[jnp.bitwise_xor(head, m)]), zero]
        for i, one in enumerate(lines):
            full = jnp.concatenate([one, zero], axis=0).astype(jnp.bfloat16)
            out_refs[m][rows:, i * rows:(i + 1) * rows] = full
    for copy in moves:
        copy.wait()


def hidden_moves(hid_ref, near_refs, far_ref, sems):
    mine = lax.axis_index("fsdp")
    near = len(near_refs)
    span = far_ref.shape[2]
    copies = []
    for m in range(near + far_ref.shape[0]):
        columns = pl.ds(pl.multiple_of(jnp.bitwise_xor(mine, m) * span, span), span)
        to = near_refs[m] if m < near else far_ref.at[m - near]
        copies.append(pltpu.make_async_copy(hid_ref.at[:, columns], to, sems.at[m]))
    for copy in copies:
        copy.start()
    return copies


def hidden_kernel(hid_ref, *rest):
    for copy in hidden_moves(hid_ref, rest[:-2], *rest[-2:]):
        copy.wait()


def project_kernel(fsdp, hid_ref, *rest):
    w_refs, out_refs, (parts,) = rest[:fsdp], rest[fsdp:fsdp + KV_HEADS], rest[fsdp + KV_HEADS:]
    mine = lax.axis_index("fsdp")
    head, _ = head_side()
    span = w_refs[0].shape[0]
    total = None
    for m in range(fsdp):
        start = pl.multiple_of(jnp.bitwise_xor(mine, m) * span, span)
        term = matmul(hid_ref[:, pl.ds(start, span)], w_refs[m][...])
        total = term if total is None else total + term
    low = total.astype(jnp.bfloat16)
    for g in range(KV_HEADS):
        key = low[:, g * HEAD_DIM:(g + 1) * HEAD_DIM]
        value = low[:, KEY_WIDTH + g * HEAD_DIM:KEY_WIDTH + (g + 1) * HEAD_DIM]
        parts[g] = jnp.concatenate([key, value], axis=1)
    for m in range(KV_HEADS):
        out_refs[m][...] = parts[jnp.bitwise_xor(head, m)]


def lower_half(shape):
    return lax.broadcasted_iota(jnp.int32, shape, len(shape) - 1) < LOWER


def stacked(key_value):
    wide = key_value.astype(jnp.float32)
    turned = pltpu.roll(wide, LOWER, 1)
    lower = lower_half(wide.shape)
    zero = jnp.zeros_like(wide)
    keys = jnp.concatenate([jnp.where(lower, wide, zero), jnp.where(lower, zero, turned)], axis=0) * SCALE
    values = jnp.concatenate([jnp.where(lower, turned, zero), jnp.where(lower, zero, wide)], axis=0)
    return keys.astype(jnp.bfloat16), values.astype(jnp.bfloat16)


def tile(keys, values, query, grad, stats, mask):
    size, edge = keys.shape[0] // 2, mask.shape[1]
    pairs = len(stats)
    width = query.shape[0] // pairs
    scores = matmul(keys, query, NT)
    prob_grad = matmul(values, grad, NT)
    lows, grads = [], []
    for head in range(2):
        part = slice(head * size, (head + 1) * size)
        lse = jnp.concatenate([lines[head] for lines in stats], axis=1)
        delta = jnp.concatenate([lines[2 + head] for lines in stats], axis=1)
        probs = jnp.exp(scores[part] - lse)
        pieces = []
        for first in range(0, pairs * width, width):
            pieces.append(jnp.where(mask, probs[:, first:first + edge], 0.0))
            if edge < width:
                pieces.append(probs[:, first + edge:first + width])
        probs = jnp.concatenate(pieces, axis=1)
        lows.append(probs.astype(jnp.bfloat16))
        grads.append((probs * (prob_grad[part] - delta)).astype(jnp.bfloat16))
    low, score_grad = jnp.concatenate(lows, axis=0), jnp.concatenate(grads, axis=0)
    return matmul(score_grad, query), matmul(low, grad), matmul(score_grad, keys, TN)


def folded(key_sum, value_sum):
    size = key_sum.shape[0] // 2
    lower = lower_half((size, PAIR))
    straight = jnp.where(lower, key_sum[:size], value_sum[size:])
    crossed = jnp.where(lower, value_sum[:size], key_sum[size:])
    return (straight + pltpu.roll(crossed, LOWER, 1)) * jnp.where(lower, SCALE, 1.0)


def unpacked(part, rows):
    exact = part[rows:, 0:3 * rows].astype(jnp.float32)[0:2 * GROUPS]
    return exact[:, 0:rows] + exact[:, rows:2 * rows] + exact[:, 2 * rows:]


def pair_stats(stat, pair):
    first = 2 * pair
    return [stat[first:first + 1], stat[first + 1:first + 2],
            stat[GROUPS + first:GROUPS + first + 1], stat[GROUPS + first + 1:GROUPS + first + 2]]


def sequence_kernel(near_parts, order_ref, hid_ref, *rest):
    qd_refs, kv_refs, rest = rest[:TEAM], rest[TEAM:TEAM + KV_HEADS], rest[TEAM + KV_HEADS:]
    dkv_refs, keep_ref, send_ref, rest = rest[:KV_HEADS], rest[KV_HEADS], rest[KV_HEADS + 1], rest[KV_HEADS + 2:]
    near_refs, far_ref, rest = rest[:near_parts], rest[near_parts], rest[near_parts + 1:]
    q_all, go_all, stat_all, key_all, value_all, dq_all, dkv_all, sems = rest
    moves = hidden_moves(hid_ref, near_refs, far_ref, sems)
    rows = kv_refs[0].shape[0]
    head, side = head_side()
    near = [order_ref[0, 2 * jnp.bitwise_xor(head, m) + side] for m in range(KV_HEADS)]
    far = [order_ref[0, 2 * jnp.bitwise_xor(head, m) + 1 - side] for m in range(KV_HEADS)]
    for place, ref in zip(near + far, by_head(qd_refs[:KV_HEADS]) + list(qd_refs[KV_HEADS:])):
        for pair in range(PAIRS):
            q_all[pair, place] = ref[0:rows, pair * PAIR:(pair + 1) * PAIR]
            go_all[pair, place] = ref[0:rows, GROUP + pair * PAIR:GROUP + (pair + 1) * PAIR]
        stat_all[place] = unpacked(ref, rows)
    for place, ref in zip(near, by_head(kv_refs)):
        key_all[place], value_all[place] = stacked(ref[...])
    dq_all[...] = jnp.zeros_like(dq_all)
    for block in range(TEAM):
        mine = functools.reduce(jnp.logical_or, [place == block for place in near])

        @pl.when(mine)
        def _():
            count = TEAM - block
            shape = (rows, rows)
            mask = lax.broadcasted_iota(jnp.int32, shape, 0) <= lax.broadcasted_iota(jnp.int32, shape, 1)
            stats = jnp.concatenate([stat_all[i] for i in range(block, TEAM)], axis=1)
            query = q_all[:, block:].reshape(PAIRS * count * rows, PAIR)
            grad = go_all[:, block:].reshape(PAIRS * count * rows, PAIR)
            key_sum, value_sum, query_part = tile(
                key_all[block], value_all[block], query, grad, [pair_stats(stats, pair) for pair in range(PAIRS)], mask)
            dq_all[:, block:] += query_part.reshape(PAIRS, count, rows, PAIR)
            dkv_all[block] = folded(key_sum, value_sum)

    for m in range(KV_HEADS):
        dkv_refs[m][...] = dkv_all[near[m]].astype(jnp.bfloat16)
        for pair in range(PAIRS):
            columns = slice(pair * PAIR, (pair + 1) * PAIR)
            keep_ref[m, :, columns] = dq_all[pair, near[m]]
            send_ref[m, :, columns] = dq_all[pair, far[m]].astype(jnp.bfloat16)
    for copy in moves:
        copy.wait()


def teams_kernel(order_ref, qd_ref, kv_ref, dkv_ref, keep_ref, send_ref, dq_all):
    rows = kv_ref.shape[1]
    head, side = head_side()
    base = lax.axis_index("ctx") // TEAM * TEAM
    dq_all[...] = jnp.zeros_like(dq_all)

    @pl.loop(0, kv_ref.shape[0])
    def _(block):
        keys, values = stacked(kv_ref[block])
        dkv_ref[block] = jnp.zeros((rows, PAIR), jnp.float32)
        stored = block // KV_HEADS * TEAM + 2 * jnp.bitwise_xor(head, lax.rem(block, KV_HEADS)) + side
        place = order_ref[0, stored]

        @pl.loop(0, TEAM)
        def _(at):
            turned = jnp.where(at < KV_HEADS, side, 1 - side)
            own = order_ref[0, base + 2 * jnp.bitwise_xor(head, lax.rem(at, KV_HEADS)) + turned]

            @pl.when(place <= own)
            def _():
                shape = (rows, rows)
                mask = (place * rows + lax.broadcasted_iota(jnp.int32, shape, 0)
                        <= own * rows + lax.broadcasted_iota(jnp.int32, shape, 1))
                one = qd_ref.at[at]
                stats = unpacked(one, rows)
                for pair in range(PAIRS):
                    first = pair * PAIR
                    key_part, value_part, query_part = tile(
                        keys, values, one[0:rows, first:first + PAIR], one[0:rows, GROUP + first:GROUP + first + PAIR],
                        [pair_stats(stats, pair)], mask)
                    dq_all[at, :, first:first + PAIR] += query_part
                    dkv_ref[block] += folded(key_part, value_part)

    keep_ref[...] = dq_all[0:KV_HEADS]
    send_ref[...] = dq_all[KV_HEADS:].astype(jnp.bfloat16)


def owner_kernel(*rest):
    dkv_refs, out_ref, parts = rest[:KV_HEADS], rest[KV_HEADS], rest[KV_HEADS + 1]
    head, _ = head_side()
    for m, ref in enumerate(by_head(dkv_refs)):
        parts[jnp.bitwise_xor(head, m)] = ref[...]
    keys = [parts[g, :, :HEAD_DIM] for g in range(KV_HEADS)]
    values = [parts[g, :, HEAD_DIM:] for g in range(KV_HEADS)]
    out_ref[...] = jnp.concatenate(keys + values, axis=1)


def pair_kernel(keep_ref, got_ref, *out_refs):
    for m in range(KV_HEADS):
        out_refs[m][...] = (keep_ref[m] + got_ref[m].astype(jnp.float32)).astype(out_refs[m].dtype)


def query_kernel(*rest):
    dq_refs, out_ref = rest[:KV_HEADS], rest[KV_HEADS]
    head, _ = head_side()
    for m, ref in enumerate(by_head(dq_refs)):
        columns = pl.ds(pl.multiple_of(jnp.bitwise_xor(head, m) * GROUP, GROUP), GROUP)
        out_ref[:, columns] = ref[...]


def input_kernel(fsdp, grad_ref, *rest):
    w_refs, out_ref = rest[:fsdp], rest[fsdp]
    mine = lax.axis_index("fsdp")
    span = w_refs[0].shape[0]
    for m in range(fsdp):
        start = pl.multiple_of(jnp.bitwise_xor(mine, m) * span, span)
        out_ref[:, pl.ds(start, span)] = matmul(grad_ref[...], w_refs[m][...], NT).astype(jnp.bfloat16)


def weight_sums(fsdp, refs):
    hid = jnp.concatenate([ref[...] for ref in refs[:fsdp]], axis=0)
    grad = jnp.concatenate([ref[...] for ref in refs[fsdp:2 * fsdp]], axis=0)
    return matmul(hid, grad, TN)


def weight_kernel(fsdp, *rest):
    rest[2 * fsdp][...] = weight_sums(fsdp, rest).astype(jnp.bfloat16)


def sides_kernel(fsdp, *rest):
    keep_ref, send_ref, parts = rest[2 * fsdp:]
    head, side = head_side()
    parts[...] = weight_sums(fsdp, rest).reshape(parts.shape)
    for m in range(KV_HEADS):
        to = 2 * jnp.bitwise_xor(head, m)
        keep_ref[m] = parts[to + side]
        send_ref[m] = parts[to + 1 - side].astype(jnp.bfloat16)


def own_total_kernel(own_ref, *rest):
    total = own_ref[...]
    for ref in rest[:-1]:
        total = total + ref[...].astype(jnp.float32)
    rest[-1][...] = total


def total_kernel(part_ref, out_ref):
    total = part_ref[0].astype(jnp.float32)
    for i in range(1, part_ref.shape[0]):
        total = total + part_ref[i].astype(jnp.float32)
    out_ref[...] = total


def over_fsdp(own, bits):
    got = list(own)
    while bits:
        for m in range(len(own)):
            if m & bits:
                got[m] = swapped(got[m], "fsdp", bits)
        bits //= 2
    return got


def shards(hidden, queries, attn_out, grad_out, log_sums, block_order, w_kv):
    rows, model = hidden.shape[1:]
    fsdp, devices = lax.axis_size("fsdp"), lax.axis_size("ctx")
    teams = devices // TEAM
    f32 = jnp.float32
    span = model // fsdp
    inputs = hidden[0]
    columns = 2 * KEY_WIDTH
    block, wide = (rows, PAIR), (rows, GROUP)

    def along_heads(arrays):
        return [arrays[0]] + [swapped(arrays[m], "ctx", 2 * m) for m in range(1, KV_HEADS)]

    far = fsdp // 2
    qd = call(
        pieces_kernel, [sds((rows + 16, 2 * GROUP))] * KV_HEADS,
        [pltpu.VMEM((rows, Q_HEADS * HEAD_DIM), jnp.bfloat16)] * 2
        + [pltpu.VMEM((Q_HEADS, rows), f32), pltpu.VMEM((KV_HEADS, 2 * GROUPS, rows), f32),
           pltpu.SemaphoreType.DMA((3 + 2 * KV_HEADS,))],
        (queries[0], grad_out[0], attn_out[0], log_sums[0]), hbm=4)
    qd = along_heads(qd)
    turned = [swapped(one, "ctx", 1) for one in qd[:2]]
    w_far = held(swapped(w_kv, "fsdp", far), (*far_first(qd[:KV_HEADS])[1:], turned[0]))
    w_parts = over_fsdp([w_kv] * far + [w_far] * (fsdp - far), far // 2)

    kv = call(
        functools.partial(project_kernel, fsdp), [sds(block)] * KV_HEADS,
        [pltpu.VMEM((KV_HEADS,) + block, jnp.bfloat16)], (inputs, *w_parts))
    kv = along_heads(kv)
    qd = qd + turned + [swapped(one, "ctx", 1) for one in qd[2:]]

    half = (KV_HEADS,) + wide
    cut = [sds((rows, span))] * far + [sds((fsdp - far, rows, span))]
    cut_sems = pltpu.SemaphoreType.DMA((fsdp,))
    if teams == 1:
        outs = call(
            functools.partial(sequence_kernel, far), [sds(block)] * KV_HEADS + [sds(half, f32), sds(half)] + cut,
            [pltpu.VMEM((PAIRS, TEAM) + block, jnp.bfloat16)] * 2 + [pltpu.VMEM((TEAM, 2 * GROUPS, rows), f32)]
            + [pltpu.VMEM((TEAM, 2 * rows, PAIR), jnp.bfloat16)] * 2
            + [pltpu.VMEM((PAIRS, TEAM) + block, f32), pltpu.VMEM((TEAM,) + block, f32), cut_sems],
            (block_order, inputs, *far_first(qd[:KV_HEADS]), *qd[KV_HEADS:], *far_first(kv)), smem=1, hbm=1)
        dkv, (keep, give, *hid, hid_far) = outs[:KV_HEADS], outs[KV_HEADS:]
    else:
        alike = [[t * TEAM + i for t in range(teams)] for i in range(TEAM)]
        kv = lax.all_gather(jnp.stack(kv), "ctx", axis_index_groups=alike, axis=0, tiled=True)
        dkv, keep, give = call(
            teams_kernel, [sds((teams * KV_HEADS,) + block, f32), sds(half, f32), sds(half)],
            [pltpu.VMEM((TEAM,) + wide, f32)], (block_order, jnp.stack(qd), kv), smem=1)
        dkv = lax.psum_scatter(dkv, "ctx", axis_index_groups=alike, scatter_dimension=0, tiled=True)
        dkv = [dkv[m].astype(jnp.bfloat16) for m in range(KV_HEADS)]
        *hid, hid_far = call(hidden_kernel, cut, [cut_sems], (inputs,), hbm=1)

    hid_far = swapped(hid_far, "fsdp", far)
    hid = over_fsdp(hid + [hid_far[m] for m in range(fsdp - far)], far // 2)
    dkv = along_heads(dkv)
    give = swapped(give, "ctx", 1)
    (kv_grad,) = call(
        owner_kernel, [sds((rows, columns))], [pltpu.VMEM((KV_HEADS,) + block, jnp.bfloat16)],
        far_first(dkv), after=(give,))
    grads = over_fsdp([kv_grad] * fsdp, far)
    if teams == 1:
        share = (span // devices, columns)
        own_sums, send_sums = call(
            functools.partial(sides_kernel, fsdp), [sds((KV_HEADS,) + share, f32), sds((KV_HEADS,) + share)],
            [pltpu.VMEM((devices,) + share, f32)], (*hid, *grads))
        formed = (own_sums,)
        dq = along_heads(call(pair_kernel, [sds(wide)] * KV_HEADS, [], (keep, give), after=formed))
        sums = call(
            pair_kernel, [sds(share, f32)] + [sds(share)] * (KV_HEADS - 1), [],
            (own_sums, swapped(send_sums, "ctx", 1)), after=dq[1:2])
        (weight_grads,) = call(own_total_kernel, [sds(share, f32)], [], far_first(along_heads(sums)))
    else:
        formed = call(functools.partial(weight_kernel, fsdp), [sds((span, columns))], [], (*hid, *grads))
        dq = along_heads(call(pair_kernel, [sds(wide)] * KV_HEADS, [], (keep, give), after=formed))
        sums = lax.all_to_all(formed[0].reshape(devices, span // devices, columns), "ctx", 0, 0, tiled=True)
        (weight_grads,) = call(total_kernel, [sds((span // devices, columns), f32)], [], (sums,))
    (query_grads,) = call(query_kernel, [sds((rows, Q_HEADS * HEAD_DIM))], [], far_first(dq), after=formed)
    (input_grads,) = call(
        functools.partial(input_kernel, fsdp), [sds((rows, model))], [], (kv_grad, *w_parts), after=formed)
    return query_grads[None], input_grads[None], weight_grads


def solution(mesh):
    return jax.shard_map(
        shards,
        mesh=mesh,
        in_specs=(
            P("fsdp", "ctx", None),
            P("fsdp", "ctx", None),
            P("fsdp", "ctx", None),
            P("fsdp", "ctx", None),
            P("fsdp", None, "ctx"),
            P("fsdp", None),
            P("fsdp", None),
        ),
        out_specs=(P("fsdp", "ctx", None), P("fsdp", "ctx", None), P(("fsdp", "ctx"), None)),
        check_vma=False,
    )
```

```python
import functools

import jax
import jax.numpy as jnp
from jax import lax
from jax.experimental import pallas as pl
from jax.experimental.pallas import tpu as pltpu
from jax.sharding import PartitionSpec as P

Q_HEADS = 16
KV_HEADS = 4
HEAD_DIM = 64
GROUPS = Q_HEADS // KV_HEADS
KEY_WIDTH = KV_HEADS * HEAD_DIM
PAIR = 2 * HEAD_DIM
TEAM = 2 * KV_HEADS
PAIRS = GROUPS // 2
GROUP = GROUPS * HEAD_DIM
SCALE = HEAD_DIM ** -0.5
LOWER = HEAD_DIM

NT = (((1,), (1,)), ((), ()))
TN = (((0,), (0,)), ((), ()))
VMEM = pl.BlockSpec(memory_space=pltpu.VMEM)
SMEM = pl.BlockSpec(memory_space=pltpu.SMEM)
ANY = pl.BlockSpec(memory_space=pl.ANY)
HBM = pl.BlockSpec(memory_space=pltpu.HBM)
PARAMS = pltpu.CompilerParams(vmem_limit_bytes=40 * 1024 * 1024)
WHOLE = pltpu.CompilerParams(vmem_limit_bytes=60 * 1024 * 1024)


def matmul(left, right, dims=(((1,), (0,)), ((), ()))):
    return lax.dot_general(left, right, dims, preferred_element_type=jnp.float32)


def swapped(array, axis, bits):
    size = lax.axis_size(axis)
    return lax.ppermute(array, axis, [(i, i ^ bits) for i in range(size)])


def call(kernel, out_shape, scratch, args, smem=0, hbm=0, after=()):
    given = len(args)
    params = WHOLE if hbm == given else PARAMS

    def body(*refs):
        kernel(*refs[:given], *refs[given + len(after):])

    specs = [SMEM] * smem + [HBM] * hbm + [VMEM] * (given - smem - hbm) + [ANY] * len(after)
    return pl.pallas_call(
        body,
        out_shape=out_shape,
        in_specs=specs,
        out_specs=[VMEM] * len(out_shape),
        scratch_shapes=scratch,
        compiler_params=params,
    )(*args, *after)


def held(array, after):
    def body(*refs):
        pass

    return pl.pallas_call(
        body,
        out_shape=sds(array.shape, array.dtype),
        in_specs=[ANY] * (1 + len(after)),
        out_specs=ANY,
        input_output_aliases={0: 0},
        compiler_params=PARAMS,
    )(array, *after)


def sds(shape, dtype=jnp.bfloat16):
    return jax.ShapeDtypeStruct(shape, dtype)


def head_side():
    me = lax.rem(lax.axis_index("ctx"), TEAM)
    return me // 2, lax.rem(me, 2)


def far_first(arrays):
    return [arrays[m] for m in (0, 2, 3, 1)]


def by_head(refs):
    return [refs[i] for i in (0, 3, 1, 2)]


def split(exact):
    first = exact.astype(jnp.bfloat16).astype(jnp.float32)
    second = (exact - first).astype(jnp.bfloat16).astype(jnp.float32)
    return first, second, exact - first - second


def pieces_kernel(q_ref, go_ref, ao_ref, lse_ref, *rest):
    out_refs, (grad, output, lse, stat, sems) = rest[:KV_HEADS], rest[KV_HEADS:]
    rows, width = q_ref.shape
    head, _ = head_side()
    loads = [pltpu.make_async_copy(ref, to, sems.at[i])
             for i, (ref, to) in enumerate(((go_ref, grad), (ao_ref, output), (lse_ref, lse)))]
    moves = []
    for m in range(KV_HEADS):
        columns = pl.ds(pl.multiple_of(jnp.bitwise_xor(head, m) * GROUP, GROUP), GROUP)
        for i, ref in enumerate((q_ref, go_ref)):
            moves.append(pltpu.make_async_copy(
                ref.at[:, columns], out_refs[m].at[0:rows, i * GROUP:(i + 1) * GROUP], sems.at[3 + 2 * m + i]))
    for copy in loads + moves:
        copy.start()
    for copy in loads:
        copy.wait()
    product = grad[...].astype(jnp.float32) * output[...].astype(jnp.float32)
    high = product.astype(jnp.bfloat16)
    low = (product - high.astype(jnp.float32)).astype(jnp.bfloat16)
    head_of = lax.broadcasted_iota(jnp.int32, (Q_HEADS, width), 1) // HEAD_DIM
    ones = (head_of == lax.broadcasted_iota(jnp.int32, (Q_HEADS, width), 0)).astype(jnp.bfloat16)
    delta = matmul(ones, high, NT) + matmul(ones, low, NT)
    for g in range(KV_HEADS):
        part = slice(g * GROUPS, (g + 1) * GROUPS)
        stat[g] = jnp.concatenate([lse[part, :], delta[part, :]], axis=0)
    zero = jnp.zeros((2 * GROUPS, rows), jnp.float32)
    for m in range(KV_HEADS):
        lines = [*split(stat[jnp.bitwise_xor(head, m)]), zero]
        for i, one in enumerate(lines):
            full = jnp.concatenate([one, zero], axis=0).astype(jnp.bfloat16)
            out_refs[m][rows:, i * rows:(i + 1) * rows] = full
    for copy in moves:
        copy.wait()


def hidden_moves(hid_ref, near_refs, far_ref, sems):
    mine = lax.axis_index("fsdp")
    near = len(near_refs)
    span = far_ref.shape[2]
    copies = []
    for m in range(near + far_ref.shape[0]):
        columns = pl.ds(pl.multiple_of(jnp.bitwise_xor(mine, m) * span, span), span)
        to = near_refs[m] if m < near else far_ref.at[m - near]
        copies.append(pltpu.make_async_copy(hid_ref.at[:, columns], to, sems.at[m]))
    for copy in copies:
        copy.start()
    return copies


def hidden_kernel(hid_ref, *rest):
    for copy in hidden_moves(hid_ref, rest[:-2], *rest[-2:]):
        copy.wait()


def project_kernel(fsdp, hid_ref, *rest):
    w_refs, out_refs, (parts,) = rest[:fsdp], rest[fsdp:fsdp + KV_HEADS], rest[fsdp + KV_HEADS:]
    mine = lax.axis_index("fsdp")
    head, _ = head_side()
    span = w_refs[0].shape[0]
    total = None
    for m in range(fsdp):
        start = pl.multiple_of(jnp.bitwise_xor(mine, m) * span, span)
        term = matmul(hid_ref[:, pl.ds(start, span)], w_refs[m][...])
        total = term if total is None else total + term
    low = total.astype(jnp.bfloat16)
    for g in range(KV_HEADS):
        key = low[:, g * HEAD_DIM:(g + 1) * HEAD_DIM]
        value = low[:, KEY_WIDTH + g * HEAD_DIM:KEY_WIDTH + (g + 1) * HEAD_DIM]
        parts[g] = jnp.concatenate([key, value], axis=1)
    for m in range(KV_HEADS):
        out_refs[m][...] = parts[jnp.bitwise_xor(head, m)]


def lower_half(shape):
    return lax.broadcasted_iota(jnp.int32, shape, len(shape) - 1) < LOWER


def stacked(key_value):
    wide = key_value.astype(jnp.float32)
    turned = pltpu.roll(wide, LOWER, 1)
    lower = lower_half(wide.shape)
    zero = jnp.zeros_like(wide)
    keys = jnp.concatenate([jnp.where(lower, wide, zero), jnp.where(lower, zero, turned)], axis=0) * SCALE
    values = jnp.concatenate([jnp.where(lower, turned, zero), jnp.where(lower, zero, wide)], axis=0)
    return keys.astype(jnp.bfloat16), values.astype(jnp.bfloat16)


def tile(keys, values, query, grad, stats, mask):
    size, edge = keys.shape[0] // 2, mask.shape[1]
    pairs = len(stats)
    width = query.shape[0] // pairs
    scores = matmul(keys, query, NT)
    prob_grad = matmul(values, grad, NT)
    lows, grads = [], []
    for head in range(2):
        part = slice(head * size, (head + 1) * size)
        lse = jnp.concatenate([lines[head] for lines in stats], axis=1)
        delta = jnp.concatenate([lines[2 + head] for lines in stats], axis=1)
        probs = jnp.exp(scores[part] - lse)
        pieces = []
        for first in range(0, pairs * width, width):
            pieces.append(jnp.where(mask, probs[:, first:first + edge], 0.0))
            if edge < width:
                pieces.append(probs[:, first + edge:first + width])
        probs = jnp.concatenate(pieces, axis=1)
        lows.append(probs.astype(jnp.bfloat16))
        grads.append((probs * (prob_grad[part] - delta)).astype(jnp.bfloat16))
    low, score_grad = jnp.concatenate(lows, axis=0), jnp.concatenate(grads, axis=0)
    return matmul(score_grad, query), matmul(low, grad), matmul(score_grad, keys, TN)


def folded(key_sum, value_sum):
    size = key_sum.shape[0] // 2
    lower = lower_half((size, PAIR))
    straight = jnp.where(lower, key_sum[:size], value_sum[size:])
    crossed = jnp.where(lower, value_sum[:size], key_sum[size:])
    return (straight + pltpu.roll(crossed, LOWER, 1)) * jnp.where(lower, SCALE, 1.0)


def unpacked(part, rows):
    exact = part[rows:, 0:3 * rows].astype(jnp.float32)[0:2 * GROUPS]
    return exact[:, 0:rows] + exact[:, rows:2 * rows] + exact[:, 2 * rows:]


def pair_stats(stat, pair):
    first = 2 * pair
    return [stat[first:first + 1], stat[first + 1:first + 2],
            stat[GROUPS + first:GROUPS + first + 1], stat[GROUPS + first + 1:GROUPS + first + 2]]


def sequence_kernel(near_parts, order_ref, hid_ref, *rest):
    qd_refs, kv_refs, rest = rest[:TEAM], rest[TEAM:TEAM + KV_HEADS], rest[TEAM + KV_HEADS:]
    dkv_refs, keep_ref, send_ref, rest = rest[:KV_HEADS], rest[KV_HEADS], rest[KV_HEADS + 1], rest[KV_HEADS + 2:]
    near_refs, far_ref, rest = rest[:near_parts], rest[near_parts], rest[near_parts + 1:]
    q_all, go_all, stat_all, key_all, value_all, dq_all, dkv_all, sems = rest
    moves = hidden_moves(hid_ref, near_refs, far_ref, sems)
    rows = kv_refs[0].shape[0]
    head, side = head_side()
    near = [order_ref[0, 2 * jnp.bitwise_xor(head, m) + side] for m in range(KV_HEADS)]
    far = [order_ref[0, 2 * jnp.bitwise_xor(head, m) + 1 - side] for m in range(KV_HEADS)]
    for place, ref in zip(near + far, by_head(qd_refs[:KV_HEADS]) + list(qd_refs[KV_HEADS:])):
        for pair in range(PAIRS):
            q_all[pair, place] = ref[0:rows, pair * PAIR:(pair + 1) * PAIR]
            go_all[pair, place] = ref[0:rows, GROUP + pair * PAIR:GROUP + (pair + 1) * PAIR]
        stat_all[place] = unpacked(ref, rows)
    for place, ref in zip(near, by_head(kv_refs)):
        key_all[place], value_all[place] = stacked(ref[...])
    dq_all[...] = jnp.zeros_like(dq_all)
    for block in range(TEAM):
        mine = functools.reduce(jnp.logical_or, [place == block for place in near])

        @pl.when(mine)
        def _():
            count = TEAM - block
            shape = (rows, rows)
            mask = lax.broadcasted_iota(jnp.int32, shape, 0) <= lax.broadcasted_iota(jnp.int32, shape, 1)
            stats = jnp.concatenate([stat_all[i] for i in range(block, TEAM)], axis=1)
            query = q_all[:, block:].reshape(PAIRS * count * rows, PAIR)
            grad = go_all[:, block:].reshape(PAIRS * count * rows, PAIR)
            key_sum, value_sum, query_part = tile(
                key_all[block], value_all[block], query, grad, [pair_stats(stats, pair) for pair in range(PAIRS)], mask)
            dq_all[:, block:] += query_part.reshape(PAIRS, count, rows, PAIR)
            dkv_all[block] = folded(key_sum, value_sum)

    for m in range(KV_HEADS):
        dkv_refs[m][...] = dkv_all[near[m]].astype(jnp.bfloat16)
        for pair in range(PAIRS):
            columns = slice(pair * PAIR, (pair + 1) * PAIR)
            keep_ref[m, :, columns] = dq_all[pair, near[m]]
            send_ref[m, :, columns] = dq_all[pair, far[m]].astype(jnp.bfloat16)
    for copy in moves:
        copy.wait()


def teams_kernel(order_ref, qd_ref, kv_ref, dkv_ref, keep_ref, send_ref, dq_all):
    rows = kv_ref.shape[1]
    head, side = head_side()
    base = lax.axis_index("ctx") // TEAM * TEAM
    dq_all[...] = jnp.zeros_like(dq_all)

    @pl.loop(0, kv_ref.shape[0])
    def _(block):
        keys, values = stacked(kv_ref[block])
        dkv_ref[block] = jnp.zeros((rows, PAIR), jnp.float32)
        stored = block // KV_HEADS * TEAM + 2 * jnp.bitwise_xor(head, lax.rem(block, KV_HEADS)) + side
        place = order_ref[0, stored]

        @pl.loop(0, TEAM)
        def _(at):
            turned = jnp.where(at < KV_HEADS, side, 1 - side)
            own = order_ref[0, base + 2 * jnp.bitwise_xor(head, lax.rem(at, KV_HEADS)) + turned]

            @pl.when(place <= own)
            def _():
                shape = (rows, rows)
                mask = (place * rows + lax.broadcasted_iota(jnp.int32, shape, 0)
                        <= own * rows + lax.broadcasted_iota(jnp.int32, shape, 1))
                one = qd_ref.at[at]
                stats = unpacked(one, rows)
                for pair in range(PAIRS):
                    first = pair * PAIR
                    key_part, value_part, query_part = tile(
                        keys, values, one[0:rows, first:first + PAIR], one[0:rows, GROUP + first:GROUP + first + PAIR],
                        [pair_stats(stats, pair)], mask)
                    dq_all[at, :, first:first + PAIR] += query_part
                    dkv_ref[block] += folded(key_part, value_part)

    keep_ref[...] = dq_all[0:KV_HEADS]
    send_ref[...] = dq_all[KV_HEADS:].astype(jnp.bfloat16)


def owner_kernel(*rest):
    dkv_refs, out_ref, parts = rest[:KV_HEADS], rest[KV_HEADS], rest[KV_HEADS + 1]
    head, _ = head_side()
    for m, ref in enumerate(by_head(dkv_refs)):
        parts[jnp.bitwise_xor(head, m)] = ref[...]
    keys = [parts[g, :, :HEAD_DIM] for g in range(KV_HEADS)]
    values = [parts[g, :, HEAD_DIM:] for g in range(KV_HEADS)]
    out_ref[...] = jnp.concatenate(keys + values, axis=1)


def pair_kernel(keep_ref, got_ref, *out_refs):
    for m, ref in enumerate(out_refs):
        ref[...] = (keep_ref[m] + got_ref[m].astype(jnp.float32)).astype(ref.dtype)


def query_kernel(*rest):
    dq_refs, out_ref = rest[:KV_HEADS], rest[KV_HEADS]
    head, _ = head_side()
    for m, ref in enumerate(by_head(dq_refs)):
        columns = pl.ds(pl.multiple_of(jnp.bitwise_xor(head, m) * GROUP, GROUP), GROUP)
        out_ref[:, columns] = ref[...]


def input_kernel(fsdp, grad_ref, *rest):
    w_refs, out_ref = rest[:fsdp], rest[fsdp]
    mine = lax.axis_index("fsdp")
    span = w_refs[0].shape[0]
    for m in range(fsdp):
        start = pl.multiple_of(jnp.bitwise_xor(mine, m) * span, span)
        out_ref[:, pl.ds(start, span)] = matmul(grad_ref[...], w_refs[m][...], NT).astype(jnp.bfloat16)


def weight_sums(fsdp, refs):
    hid = jnp.concatenate([ref[...] for ref in refs[:fsdp]], axis=0)
    grad = jnp.concatenate([ref[...] for ref in refs[fsdp:2 * fsdp]], axis=0)
    return matmul(hid, grad, TN)


def weight_kernel(fsdp, *rest):
    rest[2 * fsdp][...] = weight_sums(fsdp, rest).astype(jnp.bfloat16)


def sides_kernel(fsdp, *rest):
    keep_refs, send_refs, parts = rest[2 * fsdp:2 * fsdp + 2], rest[2 * fsdp + 2:2 * fsdp + 4], rest[-1]
    head, side = head_side()
    parts[...] = weight_sums(fsdp, rest).reshape(parts.shape)
    for m in range(KV_HEADS):
        to = 2 * jnp.bitwise_xor(head, m)
        keep_refs[m // 2][m % 2] = parts[to + side]
        send_refs[m // 2][m % 2] = parts[to + 1 - side].astype(jnp.bfloat16)


def own_total_kernel(*rest):
    part_refs, own_ref, out_ref = rest[:-2], rest[-2], rest[-1]
    total = own_ref[...]
    for ref in part_refs:
        total = total + ref[...].astype(jnp.float32)
    out_ref[...] = total


def total_kernel(part_ref, out_ref):
    total = part_ref[0].astype(jnp.float32)
    for i in range(1, part_ref.shape[0]):
        total = total + part_ref[i].astype(jnp.float32)
    out_ref[...] = total


def over_fsdp(own, bits):
    got = list(own)
    while bits:
        for m in range(len(own)):
            if m & bits:
                got[m] = swapped(got[m], "fsdp", bits)
        bits //= 2
    return got


def shards(hidden, queries, attn_out, grad_out, log_sums, block_order, w_kv):
    rows, model = hidden.shape[1:]
    fsdp, devices = lax.axis_size("fsdp"), lax.axis_size("ctx")
    teams = devices // TEAM
    f32 = jnp.float32
    span = model // fsdp
    inputs = hidden[0]
    columns = 2 * KEY_WIDTH
    block, wide = (rows, PAIR), (rows, GROUP)

    def along_heads(arrays):
        return [arrays[0]] + [swapped(arrays[m], "ctx", 2 * m) for m in range(1, KV_HEADS)]

    far = fsdp // 2
    qd = call(
        pieces_kernel, [sds((rows + 16, 2 * GROUP))] * KV_HEADS,
        [pltpu.VMEM((rows, Q_HEADS * HEAD_DIM), jnp.bfloat16)] * 2
        + [pltpu.VMEM((Q_HEADS, rows), f32), pltpu.VMEM((KV_HEADS, 2 * GROUPS, rows), f32),
           pltpu.SemaphoreType.DMA((3 + 2 * KV_HEADS,))],
        (queries[0], grad_out[0], attn_out[0], log_sums[0]), hbm=4)
    qd = along_heads(qd)
    turned = [swapped(one, "ctx", 1) for one in qd[:2]]
    w_far = held(swapped(w_kv, "fsdp", far), (*far_first(qd[:KV_HEADS])[1:], *turned))
    w_parts = over_fsdp([w_kv] * far + [w_far] * (fsdp - far), far // 2)

    kv = call(
        functools.partial(project_kernel, fsdp), [sds(block)] * KV_HEADS,
        [pltpu.VMEM((KV_HEADS,) + block, jnp.bfloat16)], (inputs, *w_parts))
    kv = along_heads(kv)
    qd = qd + turned + [swapped(one, "ctx", 1) for one in qd[2:]]

    half = (KV_HEADS,) + wide
    cut = [sds((rows, span))] * far + [sds((fsdp - far, rows, span))]
    cut_sems = pltpu.SemaphoreType.DMA((fsdp,))
    if teams == 1:
        outs = call(
            functools.partial(sequence_kernel, far), [sds(block)] * KV_HEADS + [sds(half, f32), sds(half)] + cut,
            [pltpu.VMEM((PAIRS, TEAM) + block, jnp.bfloat16)] * 2 + [pltpu.VMEM((TEAM, 2 * GROUPS, rows), f32)]
            + [pltpu.VMEM((TEAM, 2 * rows, PAIR), jnp.bfloat16)] * 2
            + [pltpu.VMEM((PAIRS, TEAM) + block, f32), pltpu.VMEM((TEAM,) + block, f32), cut_sems],
            (block_order, inputs, *far_first(qd[:KV_HEADS]), *qd[KV_HEADS:], *far_first(kv)), smem=1, hbm=1)
        dkv, (keep, give, *hid, hid_far) = outs[:KV_HEADS], outs[KV_HEADS:]
    else:
        alike = [[t * TEAM + i for t in range(teams)] for i in range(TEAM)]
        kv = lax.all_gather(jnp.stack(kv), "ctx", axis_index_groups=alike, axis=0, tiled=True)
        dkv, keep, give = call(
            teams_kernel, [sds((teams * KV_HEADS,) + block, f32), sds(half, f32), sds(half)],
            [pltpu.VMEM((TEAM,) + wide, f32)], (block_order, jnp.stack(qd), kv), smem=1)
        dkv = lax.psum_scatter(dkv, "ctx", axis_index_groups=alike, scatter_dimension=0, tiled=True)
        dkv = [dkv[m].astype(jnp.bfloat16) for m in range(KV_HEADS)]
        *hid, hid_far = call(hidden_kernel, cut, [cut_sems], (inputs,), hbm=1)

    hid_far = swapped(hid_far, "fsdp", far)
    hid = over_fsdp(hid + [hid_far[m] for m in range(fsdp - far)], far // 2)
    dkv = along_heads(dkv)
    give = swapped(give, "ctx", 1)
    (kv_grad,) = call(
        owner_kernel, [sds((rows, columns))], [pltpu.VMEM((KV_HEADS,) + block, jnp.bfloat16)],
        far_first(dkv), after=(give,))
    grads = over_fsdp([kv_grad] * fsdp, far)
    if teams == 1:
        share = (span // devices, columns)
        two = (2,) + share
        near_sums, far_sums, near_send, far_send = call(
            functools.partial(sides_kernel, fsdp), [sds(two, f32)] * 2 + [sds(two)] * 2,
            [pltpu.VMEM((devices,) + share, f32)], (*hid, *grads))
        formed = (near_sums,)
        dq = along_heads(call(pair_kernel, [sds(wide)] * KV_HEADS, [], (keep, give), after=formed))
        far_sums = call(pair_kernel, [sds(share)] * 2, [], (far_sums, swapped(far_send, "ctx", 1)))
        near_sums = call(
            pair_kernel, [sds(share, f32), sds(share)], [], (near_sums, swapped(near_send, "ctx", 1)), after=dq[1:2])
        own_sums, *sums = far_first(along_heads([*near_sums, *far_sums]))
        (weight_grads,) = call(own_total_kernel, [sds(share, f32)], [], (*sums, own_sums))
    else:
        formed = call(functools.partial(weight_kernel, fsdp), [sds((span, columns))], [], (*hid, *grads))
        dq = along_heads(call(pair_kernel, [sds(wide)] * KV_HEADS, [], (keep, give), after=formed))
        sums = lax.all_to_all(formed[0].reshape(devices, span // devices, columns), "ctx", 0, 0, tiled=True)
        (weight_grads,) = call(total_kernel, [sds((span // devices, columns), f32)], [], (sums,))
    (query_grads,) = call(query_kernel, [sds((rows, Q_HEADS * HEAD_DIM))], [], far_first(dq), after=formed)
    (input_grads,) = call(
        functools.partial(input_kernel, fsdp), [sds((rows, model))], [], (kv_grad, *w_parts), after=formed)
    return query_grads[None], input_grads[None], weight_grads


def solution(mesh):
    return jax.shard_map(
        shards,
        mesh=mesh,
        in_specs=(
            P("fsdp", "ctx", None),
            P("fsdp", "ctx", None),
            P("fsdp", "ctx", None),
            P("fsdp", "ctx", None),
            P("fsdp", None, "ctx"),
            P("fsdp", None),
            P("fsdp", None),
        ),
        out_specs=(P("fsdp", "ctx", None), P("fsdp", "ctx", None), P(("fsdp", "ctx"), None)),
        check_vma=False,
    )
```

```python
import functools

import jax
import jax.numpy as jnp
from jax import lax
from jax.experimental import pallas as pl
from jax.experimental.pallas import tpu as pltpu
from jax.sharding import PartitionSpec as P

Q_HEADS = 16
KV_HEADS = 4
HEAD_DIM = 64
GROUPS = Q_HEADS // KV_HEADS
KEY_WIDTH = KV_HEADS * HEAD_DIM
PAIR = 2 * HEAD_DIM
TEAM = 2 * KV_HEADS
PAIRS = GROUPS // 2
GROUP = GROUPS * HEAD_DIM
SCALE = HEAD_DIM ** -0.5
LOWER = HEAD_DIM

NT = (((1,), (1,)), ((), ()))
TN = (((0,), (0,)), ((), ()))
VMEM = pl.BlockSpec(memory_space=pltpu.VMEM)
SMEM = pl.BlockSpec(memory_space=pltpu.SMEM)
ANY = pl.BlockSpec(memory_space=pl.ANY)
HBM = pl.BlockSpec(memory_space=pltpu.HBM)
PARAMS = pltpu.CompilerParams(vmem_limit_bytes=40 * 1024 * 1024)
WHOLE = pltpu.CompilerParams(vmem_limit_bytes=60 * 1024 * 1024)


def matmul(left, right, dims=(((1,), (0,)), ((), ()))):
    return lax.dot_general(left, right, dims, preferred_element_type=jnp.float32)


def swapped(array, axis, bits):
    size = lax.axis_size(axis)
    return lax.ppermute(array, axis, [(i, i ^ bits) for i in range(size)])


def call(kernel, out_shape, scratch, args, smem=0, hbm=0, after=()):
    given = len(args)
    params = WHOLE if hbm == given else PARAMS

    def body(*refs):
        kernel(*refs[:given], *refs[given + len(after):])

    specs = [SMEM] * smem + [HBM] * hbm + [VMEM] * (given - smem - hbm) + [ANY] * len(after)
    return pl.pallas_call(
        body,
        out_shape=out_shape,
        in_specs=specs,
        out_specs=[VMEM] * len(out_shape),
        scratch_shapes=scratch,
        compiler_params=params,
    )(*args, *after)


def held(array, after):
    def body(*refs):
        pass

    return pl.pallas_call(
        body,
        out_shape=sds(array.shape, array.dtype),
        in_specs=[ANY] * (1 + len(after)),
        out_specs=ANY,
        input_output_aliases={0: 0},
        compiler_params=PARAMS,
    )(array, *after)


def sds(shape, dtype=jnp.bfloat16):
    return jax.ShapeDtypeStruct(shape, dtype)


def head_side():
    me = lax.rem(lax.axis_index("ctx"), TEAM)
    return me // 2, lax.rem(me, 2)


def far_first(arrays):
    return [arrays[m] for m in (0, 3, 2, 1)]


def by_head(refs):
    return [refs[i] for i in (0, 3, 2, 1)]


def split(exact):
    first = exact.astype(jnp.bfloat16).astype(jnp.float32)
    second = (exact - first).astype(jnp.bfloat16).astype(jnp.float32)
    return first, second, exact - first - second


def pieces_kernel(q_ref, go_ref, ao_ref, lse_ref, *rest):
    out_refs, (grad, output, lse, stat, sems) = rest[:KV_HEADS], rest[KV_HEADS:]
    rows, width = q_ref.shape
    head, _ = head_side()
    loads = [pltpu.make_async_copy(ref, to, sems.at[i])
             for i, (ref, to) in enumerate(((go_ref, grad), (ao_ref, output), (lse_ref, lse)))]
    moves = []
    for m in range(KV_HEADS):
        columns = pl.ds(pl.multiple_of(jnp.bitwise_xor(head, m) * GROUP, GROUP), GROUP)
        for i, ref in enumerate((q_ref, go_ref)):
            moves.append(pltpu.make_async_copy(
                ref.at[:, columns], out_refs[m].at[0:rows, i * GROUP:(i + 1) * GROUP], sems.at[3 + 2 * m + i]))
    for copy in loads + moves:
        copy.start()
    for copy in loads:
        copy.wait()
    product = grad[...].astype(jnp.float32) * output[...].astype(jnp.float32)
    high = product.astype(jnp.bfloat16)
    low = (product - high.astype(jnp.float32)).astype(jnp.bfloat16)
    head_of = lax.broadcasted_iota(jnp.int32, (Q_HEADS, width), 1) // HEAD_DIM
    ones = (head_of == lax.broadcasted_iota(jnp.int32, (Q_HEADS, width), 0)).astype(jnp.bfloat16)
    delta = matmul(ones, high, NT) + matmul(ones, low, NT)
    for g in range(KV_HEADS):
        part = slice(g * GROUPS, (g + 1) * GROUPS)
        stat[g] = jnp.concatenate([lse[part, :], delta[part, :]], axis=0)
    zero = jnp.zeros((2 * GROUPS, rows), jnp.float32)
    for m in range(KV_HEADS):
        lines = [*split(stat[jnp.bitwise_xor(head, m)]), zero]
        for i, one in enumerate(lines):
            full = jnp.concatenate([one, zero], axis=0).astype(jnp.bfloat16)
            out_refs[m][rows:, i * rows:(i + 1) * rows] = full
    for copy in moves:
        copy.wait()


def hidden_moves(hid_ref, near_refs, far_ref, sems):
    mine = lax.axis_index("fsdp")
    near = len(near_refs)
    span = far_ref.shape[2]
    copies = []
    for m in range(near + far_ref.shape[0]):
        columns = pl.ds(pl.multiple_of(jnp.bitwise_xor(mine, m) * span, span), span)
        to = near_refs[m] if m < near else far_ref.at[m - near]
        copies.append(pltpu.make_async_copy(hid_ref.at[:, columns], to, sems.at[m]))
    for copy in copies:
        copy.start()
    return copies


def hidden_kernel(hid_ref, *rest):
    for copy in hidden_moves(hid_ref, rest[:-2], *rest[-2:]):
        copy.wait()


def project_kernel(fsdp, hid_ref, *rest):
    w_refs, out_refs, (parts,) = rest[:fsdp], rest[fsdp:fsdp + KV_HEADS], rest[fsdp + KV_HEADS:]
    mine = lax.axis_index("fsdp")
    head, _ = head_side()
    span = w_refs[0].shape[0]
    total = None
    for m in range(fsdp):
        start = pl.multiple_of(jnp.bitwise_xor(mine, m) * span, span)
        term = matmul(hid_ref[:, pl.ds(start, span)], w_refs[m][...])
        total = term if total is None else total + term
    low = total.astype(jnp.bfloat16)
    for g in range(KV_HEADS):
        key = low[:, g * HEAD_DIM:(g + 1) * HEAD_DIM]
        value = low[:, KEY_WIDTH + g * HEAD_DIM:KEY_WIDTH + (g + 1) * HEAD_DIM]
        parts[g] = jnp.concatenate([key, value], axis=1)
    for m in range(KV_HEADS):
        out_refs[m][...] = parts[jnp.bitwise_xor(head, m)]


def lower_half(shape):
    return lax.broadcasted_iota(jnp.int32, shape, len(shape) - 1) < LOWER


def stacked(key_value):
    wide = key_value.astype(jnp.float32)
    turned = pltpu.roll(wide, LOWER, 1)
    lower = lower_half(wide.shape)
    zero = jnp.zeros_like(wide)
    keys = jnp.concatenate([jnp.where(lower, wide, zero), jnp.where(lower, zero, turned)], axis=0) * SCALE
    values = jnp.concatenate([jnp.where(lower, turned, zero), jnp.where(lower, zero, wide)], axis=0)
    return keys.astype(jnp.bfloat16), values.astype(jnp.bfloat16)


def tile(keys, values, query, grad, stats, mask):
    size, edge = keys.shape[0] // 2, mask.shape[1]
    pairs = len(stats)
    width = query.shape[0] // pairs
    scores = matmul(keys, query, NT)
    prob_grad = matmul(values, grad, NT)
    lows, grads = [], []
    for head in range(2):
        part = slice(head * size, (head + 1) * size)
        lse = jnp.concatenate([lines[head] for lines in stats], axis=1)
        delta = jnp.concatenate([lines[2 + head] for lines in stats], axis=1)
        probs = jnp.exp(scores[part] - lse)
        pieces = []
        for first in range(0, pairs * width, width):
            pieces.append(jnp.where(mask, probs[:, first:first + edge], 0.0))
            if edge < width:
                pieces.append(probs[:, first + edge:first + width])
        probs = jnp.concatenate(pieces, axis=1)
        lows.append(probs.astype(jnp.bfloat16))
        grads.append((probs * (prob_grad[part] - delta)).astype(jnp.bfloat16))
    low, score_grad = jnp.concatenate(lows, axis=0), jnp.concatenate(grads, axis=0)
    return matmul(score_grad, query), matmul(low, grad), matmul(score_grad, keys, TN)


def folded(key_sum, value_sum):
    size = key_sum.shape[0] // 2
    lower = lower_half((size, PAIR))
    straight = jnp.where(lower, key_sum[:size], value_sum[size:])
    crossed = jnp.where(lower, value_sum[:size], key_sum[size:])
    return (straight + pltpu.roll(crossed, LOWER, 1)) * jnp.where(lower, SCALE, 1.0)


def unpacked(part, rows):
    exact = part[rows:, 0:3 * rows].astype(jnp.float32)[0:2 * GROUPS]
    return exact[:, 0:rows] + exact[:, rows:2 * rows] + exact[:, 2 * rows:]


def pair_stats(stat, pair):
    first = 2 * pair
    return [stat[first:first + 1], stat[first + 1:first + 2],
            stat[GROUPS + first:GROUPS + first + 1], stat[GROUPS + first + 1:GROUPS + first + 2]]


def sequence_kernel(near_parts, order_ref, hid_ref, *rest):
    qd_refs, kv_refs, rest = rest[:TEAM], rest[TEAM:TEAM + KV_HEADS], rest[TEAM + KV_HEADS:]
    dkv_refs, keep_ref, send_ref, rest = rest[:KV_HEADS], rest[KV_HEADS], rest[KV_HEADS + 1], rest[KV_HEADS + 2:]
    near_refs, far_ref, rest = rest[:near_parts], rest[near_parts], rest[near_parts + 1:]
    q_all, go_all, stat_all, key_all, value_all, dq_all, dkv_all, sems = rest
    moves = hidden_moves(hid_ref, near_refs, far_ref, sems)
    rows = kv_refs[0].shape[0]
    head, side = head_side()
    near = [order_ref[0, 2 * jnp.bitwise_xor(head, m) + side] for m in range(KV_HEADS)]
    far = [order_ref[0, 2 * jnp.bitwise_xor(head, m) + 1 - side] for m in range(KV_HEADS)]
    for place, ref in zip(near + far, by_head(qd_refs[:KV_HEADS]) + list(qd_refs[KV_HEADS:])):
        for pair in range(PAIRS):
            q_all[pair, place] = ref[0:rows, pair * PAIR:(pair + 1) * PAIR]
            go_all[pair, place] = ref[0:rows, GROUP + pair * PAIR:GROUP + (pair + 1) * PAIR]
        stat_all[place] = unpacked(ref, rows)
    for place, ref in zip(near, by_head(kv_refs)):
        key_all[place], value_all[place] = stacked(ref[...])
    dq_all[...] = jnp.zeros_like(dq_all)
    for block in range(TEAM):
        mine = functools.reduce(jnp.logical_or, [place == block for place in near])

        @pl.when(mine)
        def _():
            count = TEAM - block
            shape = (rows, rows)
            mask = lax.broadcasted_iota(jnp.int32, shape, 0) <= lax.broadcasted_iota(jnp.int32, shape, 1)
            stats = jnp.concatenate([stat_all[i] for i in range(block, TEAM)], axis=1)
            query = q_all[:, block:].reshape(PAIRS * count * rows, PAIR)
            grad = go_all[:, block:].reshape(PAIRS * count * rows, PAIR)
            key_sum, value_sum, query_part = tile(
                key_all[block], value_all[block], query, grad, [pair_stats(stats, pair) for pair in range(PAIRS)], mask)
            dq_all[:, block:] += query_part.reshape(PAIRS, count, rows, PAIR)
            dkv_all[block] = folded(key_sum, value_sum)

    for m in range(KV_HEADS):
        dkv_refs[m][...] = dkv_all[near[m]].astype(jnp.bfloat16)
        for pair in range(PAIRS):
            columns = slice(pair * PAIR, (pair + 1) * PAIR)
            keep_ref[m, :, columns] = dq_all[pair, near[m]]
            send_ref[m, :, columns] = dq_all[pair, far[m]].astype(jnp.bfloat16)
    for copy in moves:
        copy.wait()


def teams_kernel(order_ref, qd_ref, kv_ref, dkv_ref, keep_ref, send_ref, dq_all):
    rows = kv_ref.shape[1]
    head, side = head_side()
    base = lax.axis_index("ctx") // TEAM * TEAM
    dq_all[...] = jnp.zeros_like(dq_all)

    @pl.loop(0, kv_ref.shape[0])
    def _(block):
        keys, values = stacked(kv_ref[block])
        dkv_ref[block] = jnp.zeros((rows, PAIR), jnp.float32)
        stored = block // KV_HEADS * TEAM + 2 * jnp.bitwise_xor(head, lax.rem(block, KV_HEADS)) + side
        place = order_ref[0, stored]

        @pl.loop(0, TEAM)
        def _(at):
            turned = jnp.where(at < KV_HEADS, side, 1 - side)
            own = order_ref[0, base + 2 * jnp.bitwise_xor(head, lax.rem(at, KV_HEADS)) + turned]

            @pl.when(place <= own)
            def _():
                shape = (rows, rows)
                mask = (place * rows + lax.broadcasted_iota(jnp.int32, shape, 0)
                        <= own * rows + lax.broadcasted_iota(jnp.int32, shape, 1))
                one = qd_ref.at[at]
                stats = unpacked(one, rows)
                for pair in range(PAIRS):
                    first = pair * PAIR
                    key_part, value_part, query_part = tile(
                        keys, values, one[0:rows, first:first + PAIR], one[0:rows, GROUP + first:GROUP + first + PAIR],
                        [pair_stats(stats, pair)], mask)
                    dq_all[at, :, first:first + PAIR] += query_part
                    dkv_ref[block] += folded(key_part, value_part)

    keep_ref[...] = dq_all[0:KV_HEADS]
    send_ref[...] = dq_all[KV_HEADS:].astype(jnp.bfloat16)


def owner_kernel(*rest):
    dkv_refs, out_ref, parts = rest[:KV_HEADS], rest[KV_HEADS], rest[KV_HEADS + 1]
    head, _ = head_side()
    for m, ref in enumerate(by_head(dkv_refs)):
        parts[jnp.bitwise_xor(head, m)] = ref[...]
    keys = [parts[g, :, :HEAD_DIM] for g in range(KV_HEADS)]
    values = [parts[g, :, HEAD_DIM:] for g in range(KV_HEADS)]
    out_ref[...] = jnp.concatenate(keys + values, axis=1)


def pair_kernel(keep_ref, got_ref, *out_refs):
    for m, ref in enumerate(out_refs):
        ref[...] = (keep_ref[m] + got_ref[m].astype(jnp.float32)).astype(ref.dtype)


def query_kernel(*rest):
    dq_refs, out_ref = rest[:KV_HEADS], rest[KV_HEADS]
    head, _ = head_side()
    for m, ref in enumerate(by_head(dq_refs)):
        columns = pl.ds(pl.multiple_of(jnp.bitwise_xor(head, m) * GROUP, GROUP), GROUP)
        out_ref[:, columns] = ref[...]


def input_kernel(fsdp, grad_ref, *rest):
    w_refs, out_ref = rest[:fsdp], rest[fsdp]
    mine = lax.axis_index("fsdp")
    span = w_refs[0].shape[0]
    for m in range(fsdp):
        start = pl.multiple_of(jnp.bitwise_xor(mine, m) * span, span)
        out_ref[:, pl.ds(start, span)] = matmul(grad_ref[...], w_refs[m][...], NT).astype(jnp.bfloat16)


def weight_sums(fsdp, refs):
    hid = jnp.concatenate([ref[...] for ref in refs[:fsdp]], axis=0)
    grad = jnp.concatenate([ref[...] for ref in refs[fsdp:2 * fsdp]], axis=0)
    return matmul(hid, grad, TN)


def weight_kernel(fsdp, *rest):
    rest[2 * fsdp][...] = weight_sums(fsdp, rest).astype(jnp.bfloat16)


def sides_kernel(fsdp, *rest):
    keep_refs, send_refs, parts = rest[2 * fsdp:2 * fsdp + 2], rest[2 * fsdp + 2:2 * fsdp + 4], rest[-1]
    head, side = head_side()
    parts[...] = weight_sums(fsdp, rest).reshape(parts.shape)
    for m in range(KV_HEADS):
        to = 2 * jnp.bitwise_xor(head, m)
        keep_refs[m // 2][m % 2] = parts[to + side]
        send_refs[m // 2][m % 2] = parts[to + 1 - side].astype(jnp.bfloat16)


def own_total_kernel(*rest):
    part_refs, own_ref, out_ref = rest[:-2], rest[-2], rest[-1]
    total = own_ref[...]
    for ref in part_refs:
        total = total + ref[...].astype(jnp.float32)
    out_ref[...] = total


def total_kernel(part_ref, out_ref):
    total = part_ref[0].astype(jnp.float32)
    for i in range(1, part_ref.shape[0]):
        total = total + part_ref[i].astype(jnp.float32)
    out_ref[...] = total


def over_fsdp(own, bits):
    got = list(own)
    while bits:
        for m in range(len(own)):
            if m & bits:
                got[m] = swapped(got[m], "fsdp", bits)
        bits //= 2
    return got


def shards(hidden, queries, attn_out, grad_out, log_sums, block_order, w_kv):
    rows, model = hidden.shape[1:]
    fsdp, devices = lax.axis_size("fsdp"), lax.axis_size("ctx")
    teams = devices // TEAM
    f32 = jnp.float32
    span = model // fsdp
    inputs = hidden[0]
    columns = 2 * KEY_WIDTH
    block, wide = (rows, PAIR), (rows, GROUP)

    def along_heads(arrays):
        return [arrays[0]] + [swapped(arrays[m], "ctx", 2 * m) for m in range(1, KV_HEADS)]

    far = fsdp // 2
    qd = call(
        pieces_kernel, [sds((rows + 16, 2 * GROUP))] * KV_HEADS,
        [pltpu.VMEM((rows, Q_HEADS * HEAD_DIM), jnp.bfloat16)] * 2
        + [pltpu.VMEM((Q_HEADS, rows), f32), pltpu.VMEM((KV_HEADS, 2 * GROUPS, rows), f32),
           pltpu.SemaphoreType.DMA((3 + 2 * KV_HEADS,))],
        (queries[0], grad_out[0], attn_out[0], log_sums[0]), hbm=4)
    qd = along_heads(qd)
    turned = [swapped(one, "ctx", 1) for one in qd[:2]]
    w_far = held(swapped(w_kv, "fsdp", far), (*far_first(qd[:KV_HEADS])[1:], *turned))
    w_parts = over_fsdp([w_kv] * far + [w_far] * (fsdp - far), far // 2)

    kv = call(
        functools.partial(project_kernel, fsdp), [sds(block)] * KV_HEADS,
        [pltpu.VMEM((KV_HEADS,) + block, jnp.bfloat16)], (inputs, *w_parts))
    kv = along_heads(kv)
    qd = qd + turned + [swapped(one, "ctx", 1) for one in qd[2:]]

    half = (KV_HEADS,) + wide
    cut = [sds((rows, span))] * far + [sds((fsdp - far, rows, span))]
    cut_sems = pltpu.SemaphoreType.DMA((fsdp,))
    if teams == 1:
        outs = call(
            functools.partial(sequence_kernel, far), [sds(block)] * KV_HEADS + [sds(half, f32), sds(half)] + cut,
            [pltpu.VMEM((PAIRS, TEAM) + block, jnp.bfloat16)] * 2 + [pltpu.VMEM((TEAM, 2 * GROUPS, rows), f32)]
            + [pltpu.VMEM((TEAM, 2 * rows, PAIR), jnp.bfloat16)] * 2
            + [pltpu.VMEM((PAIRS, TEAM) + block, f32), pltpu.VMEM((TEAM,) + block, f32), cut_sems],
            (block_order, inputs, *far_first(qd[:KV_HEADS]), *qd[KV_HEADS:], *far_first(kv)), smem=1, hbm=1)
        dkv, (keep, give, *hid, hid_far) = outs[:KV_HEADS], outs[KV_HEADS:]
    else:
        alike = [[t * TEAM + i for t in range(teams)] for i in range(TEAM)]
        kv = lax.all_gather(jnp.stack(kv), "ctx", axis_index_groups=alike, axis=0, tiled=True)
        dkv, keep, give = call(
            teams_kernel, [sds((teams * KV_HEADS,) + block, f32), sds(half, f32), sds(half)],
            [pltpu.VMEM((TEAM,) + wide, f32)], (block_order, jnp.stack(qd), kv), smem=1)
        dkv = lax.psum_scatter(dkv, "ctx", axis_index_groups=alike, scatter_dimension=0, tiled=True)
        dkv = [dkv[m].astype(jnp.bfloat16) for m in range(KV_HEADS)]
        *hid, hid_far = call(hidden_kernel, cut, [cut_sems], (inputs,), hbm=1)

    hid_far = swapped(hid_far, "fsdp", far)
    hid = over_fsdp(hid + [hid_far[m] for m in range(fsdp - far)], far // 2)
    dkv = along_heads(dkv)
    give = swapped(give, "ctx", 1)
    (kv_grad,) = call(
        owner_kernel, [sds((rows, columns))], [pltpu.VMEM((KV_HEADS,) + block, jnp.bfloat16)],
        far_first(dkv), after=(give,))
    grads = over_fsdp([kv_grad] * fsdp, far)
    if teams == 1:
        share = (span // devices, columns)
        two = (2,) + share
        near_sums, far_sums, near_send, far_send = call(
            functools.partial(sides_kernel, fsdp), [sds(two, f32)] * 2 + [sds(two)] * 2,
            [pltpu.VMEM((devices,) + share, f32)], (*hid, *grads))
        formed = (near_sums,)
        dq = along_heads(call(pair_kernel, [sds(wide)] * KV_HEADS, [], (keep, give), after=formed))
        far_sums = call(pair_kernel, [sds(share)] * 2, [], (far_sums, swapped(far_send, "ctx", 1)))
        near_sums = call(
            pair_kernel, [sds(share, f32), sds(share)], [], (near_sums, swapped(near_send, "ctx", 1)), after=dq[1:2])
        own_sums, *sums = far_first(along_heads([*near_sums, *far_sums]))
        (weight_grads,) = call(own_total_kernel, [sds(share, f32)], [], (*sums, own_sums))
    else:
        formed = call(functools.partial(weight_kernel, fsdp), [sds((span, columns))], [], (*hid, *grads))
        dq = along_heads(call(pair_kernel, [sds(wide)] * KV_HEADS, [], (keep, give), after=formed))
        sums = lax.all_to_all(formed[0].reshape(devices, span // devices, columns), "ctx", 0, 0, tiled=True)
        (weight_grads,) = call(total_kernel, [sds((span // devices, columns), f32)], [], (sums,))
    (query_grads,) = call(query_kernel, [sds((rows, Q_HEADS * HEAD_DIM))], [], far_first(dq), after=formed)
    (input_grads,) = call(
        functools.partial(input_kernel, fsdp), [sds((rows, model))], [], (kv_grad, *w_parts), after=formed)
    return query_grads[None], input_grads[None], weight_grads


def solution(mesh):
    return jax.shard_map(
        shards,
        mesh=mesh,
        in_specs=(
            P("fsdp", "ctx", None),
            P("fsdp", "ctx", None),
            P("fsdp", "ctx", None),
            P("fsdp", "ctx", None),
            P("fsdp", None, "ctx"),
            P("fsdp", None),
            P("fsdp", None),
        ),
        out_specs=(P("fsdp", "ctx", None), P("fsdp", "ctx", None), P(("fsdp", "ctx"), None)),
        check_vma=False,
    )
```

```python
import functools

import jax
import jax.numpy as jnp
from jax import lax
from jax.experimental import pallas as pl
from jax.experimental.pallas import tpu as pltpu
from jax.sharding import PartitionSpec as P

Q_HEADS = 16
KV_HEADS = 4
HEAD_DIM = 64
GROUPS = Q_HEADS // KV_HEADS
KEY_WIDTH = KV_HEADS * HEAD_DIM
PAIR = 2 * HEAD_DIM
TEAM = 2 * KV_HEADS
PAIRS = GROUPS // 2
GROUP = GROUPS * HEAD_DIM
SCALE = HEAD_DIM ** -0.5
LOWER = HEAD_DIM

NT = (((1,), (1,)), ((), ()))
TN = (((0,), (0,)), ((), ()))
VMEM = pl.BlockSpec(memory_space=pltpu.VMEM)
SMEM = pl.BlockSpec(memory_space=pltpu.SMEM)
ANY = pl.BlockSpec(memory_space=pl.ANY)
HBM = pl.BlockSpec(memory_space=pltpu.HBM)
PARAMS = pltpu.CompilerParams(vmem_limit_bytes=40 * 1024 * 1024)
WHOLE = pltpu.CompilerParams(vmem_limit_bytes=60 * 1024 * 1024)


def matmul(left, right, dims=(((1,), (0,)), ((), ()))):
    return lax.dot_general(left, right, dims, preferred_element_type=jnp.float32)


def swapped(array, axis, bits):
    size = lax.axis_size(axis)
    return lax.ppermute(array, axis, [(i, i ^ bits) for i in range(size)])


def call(kernel, out_shape, scratch, args, smem=0, hbm=0, after=()):
    given = len(args)
    params = WHOLE if hbm == given else PARAMS

    def body(*refs):
        kernel(*refs[:given], *refs[given + len(after):])

    specs = [SMEM] * smem + [HBM] * hbm + [VMEM] * (given - smem - hbm) + [ANY] * len(after)
    return pl.pallas_call(
        body,
        out_shape=out_shape,
        in_specs=specs,
        out_specs=[VMEM] * len(out_shape),
        scratch_shapes=scratch,
        compiler_params=params,
    )(*args, *after)


def held(array, after):
    def body(*refs):
        pass

    return pl.pallas_call(
        body,
        out_shape=sds(array.shape, array.dtype),
        in_specs=[ANY] * (1 + len(after)),
        out_specs=ANY,
        input_output_aliases={0: 0},
        compiler_params=PARAMS,
    )(array, *after)


def sds(shape, dtype=jnp.bfloat16):
    return jax.ShapeDtypeStruct(shape, dtype)


def head_side():
    me = lax.rem(lax.axis_index("ctx"), TEAM)
    return me // 2, lax.rem(me, 2)


def far_first(arrays):
    return [arrays[m] for m in (0, 2, 3, 1)]


def by_head(refs):
    return [refs[i] for i in (0, 3, 1, 2)]


def split(exact):
    first = exact.astype(jnp.bfloat16).astype(jnp.float32)
    second = (exact - first).astype(jnp.bfloat16).astype(jnp.float32)
    return first, second, exact - first - second


def pieces_kernel(q_ref, go_ref, ao_ref, lse_ref, *rest):
    out_refs, (grad, output, lse, stat, sems) = rest[:KV_HEADS], rest[KV_HEADS:]
    rows, width = q_ref.shape
    head, _ = head_side()
    loads = [pltpu.make_async_copy(ref, to, sems.at[i])
             for i, (ref, to) in enumerate(((go_ref, grad), (ao_ref, output), (lse_ref, lse)))]
    moves = []
    for m in range(KV_HEADS):
        columns = pl.ds(pl.multiple_of(jnp.bitwise_xor(head, m) * GROUP, GROUP), GROUP)
        for i, ref in enumerate((q_ref, go_ref)):
            moves.append(pltpu.make_async_copy(
                ref.at[:, columns], out_refs[m].at[0:rows, i * GROUP:(i + 1) * GROUP], sems.at[3 + 2 * m + i]))
    for copy in loads + moves:
        copy.start()
    for copy in loads:
        copy.wait()
    product = grad[...].astype(jnp.float32) * output[...].astype(jnp.float32)
    high = product.astype(jnp.bfloat16)
    low = (product - high.astype(jnp.float32)).astype(jnp.bfloat16)
    head_of = lax.broadcasted_iota(jnp.int32, (Q_HEADS, width), 1) // HEAD_DIM
    ones = (head_of == lax.broadcasted_iota(jnp.int32, (Q_HEADS, width), 0)).astype(jnp.bfloat16)
    delta = matmul(ones, high, NT) + matmul(ones, low, NT)
    for g in range(KV_HEADS):
        part = slice(g * GROUPS, (g + 1) * GROUPS)
        stat[g] = jnp.concatenate([lse[part, :], delta[part, :]], axis=0)
    zero = jnp.zeros((2 * GROUPS, rows), jnp.float32)
    for m in range(KV_HEADS):
        lines = [*split(stat[jnp.bitwise_xor(head, m)]), zero]
        for i, one in enumerate(lines):
            full = jnp.concatenate([one, zero], axis=0).astype(jnp.bfloat16)
            out_refs[m][rows:, i * rows:(i + 1) * rows] = full
    for copy in moves:
        copy.wait()


def hidden_moves(hid_ref, near_refs, far_ref, sems):
    mine = lax.axis_index("fsdp")
    near = len(near_refs)
    span = far_ref.shape[2]
    copies = []
    for m in range(near + far_ref.shape[0]):
        columns = pl.ds(pl.multiple_of(jnp.bitwise_xor(mine, m) * span, span), span)
        to = near_refs[m] if m < near else far_ref.at[m - near]
        copies.append(pltpu.make_async_copy(hid_ref.at[:, columns], to, sems.at[m]))
    for copy in copies:
        copy.start()
    return copies


def hidden_kernel(hid_ref, *rest):
    for copy in hidden_moves(hid_ref, rest[:-2], *rest[-2:]):
        copy.wait()


def project_kernel(fsdp, hid_ref, *rest):
    w_refs, out_refs, (parts,) = rest[:fsdp], rest[fsdp:fsdp + KV_HEADS], rest[fsdp + KV_HEADS:]
    mine = lax.axis_index("fsdp")
    head, _ = head_side()
    span = w_refs[0].shape[0]
    total = None
    for m in range(fsdp):
        start = pl.multiple_of(jnp.bitwise_xor(mine, m) * span, span)
        term = matmul(hid_ref[:, pl.ds(start, span)], w_refs[m][...])
        total = term if total is None else total + term
    low = total.astype(jnp.bfloat16)
    for g in range(KV_HEADS):
        key = low[:, g * HEAD_DIM:(g + 1) * HEAD_DIM]
        value = low[:, KEY_WIDTH + g * HEAD_DIM:KEY_WIDTH + (g + 1) * HEAD_DIM]
        parts[g] = jnp.concatenate([key, value], axis=1)
    for m in range(KV_HEADS):
        out_refs[m][...] = parts[jnp.bitwise_xor(head, m)]


def lower_half(shape):
    return lax.broadcasted_iota(jnp.int32, shape, len(shape) - 1) < LOWER


def stacked(key_value):
    wide = key_value.astype(jnp.float32)
    turned = pltpu.roll(wide, LOWER, 1)
    lower = lower_half(wide.shape)
    zero = jnp.zeros_like(wide)
    keys = jnp.concatenate([jnp.where(lower, wide, zero), jnp.where(lower, zero, turned)], axis=0) * SCALE
    values = jnp.concatenate([jnp.where(lower, turned, zero), jnp.where(lower, zero, wide)], axis=0)
    return keys.astype(jnp.bfloat16), values.astype(jnp.bfloat16)


def tile(keys, values, query, grad, stats, mask):
    size, edge = keys.shape[0] // 2, mask.shape[1]
    pairs = len(stats)
    width = query.shape[0] // pairs
    scores = matmul(keys, query, NT)
    prob_grad = matmul(values, grad, NT)
    lows, grads = [], []
    for head in range(2):
        part = slice(head * size, (head + 1) * size)
        lse = jnp.concatenate([lines[head] for lines in stats], axis=1)
        delta = jnp.concatenate([lines[2 + head] for lines in stats], axis=1)
        probs = jnp.exp(scores[part] - lse)
        pieces = []
        for first in range(0, pairs * width, width):
            pieces.append(jnp.where(mask, probs[:, first:first + edge], 0.0))
            if edge < width:
                pieces.append(probs[:, first + edge:first + width])
        probs = jnp.concatenate(pieces, axis=1)
        lows.append(probs.astype(jnp.bfloat16))
        grads.append((probs * (prob_grad[part] - delta)).astype(jnp.bfloat16))
    low, score_grad = jnp.concatenate(lows, axis=0), jnp.concatenate(grads, axis=0)
    return matmul(score_grad, query), matmul(low, grad), matmul(score_grad, keys, TN)


def folded(key_sum, value_sum):
    size = key_sum.shape[0] // 2
    lower = lower_half((size, PAIR))
    straight = jnp.where(lower, key_sum[:size], value_sum[size:])
    crossed = jnp.where(lower, value_sum[:size], key_sum[size:])
    return (straight + pltpu.roll(crossed, LOWER, 1)) * jnp.where(lower, SCALE, 1.0)


def unpacked(part, rows):
    exact = part[rows:, 0:3 * rows].astype(jnp.float32)[0:2 * GROUPS]
    return exact[:, 0:rows] + exact[:, rows:2 * rows] + exact[:, 2 * rows:]


def pair_stats(stat, pair):
    first = 2 * pair
    return [stat[first:first + 1], stat[first + 1:first + 2],
            stat[GROUPS + first:GROUPS + first + 1], stat[GROUPS + first + 1:GROUPS + first + 2]]


def sequence_kernel(near_parts, order_ref, hid_ref, *rest):
    qd_refs, kv_refs, rest = rest[:TEAM], rest[TEAM:TEAM + KV_HEADS], rest[TEAM + KV_HEADS:]
    dkv_refs, keep_ref, send_ref, rest = rest[:KV_HEADS], rest[KV_HEADS], rest[KV_HEADS + 1], rest[KV_HEADS + 2:]
    near_refs, far_ref, rest = rest[:near_parts], rest[near_parts], rest[near_parts + 1:]
    q_all, go_all, stat_all, key_all, value_all, dq_all, dkv_all, sems = rest
    moves = hidden_moves(hid_ref, near_refs, far_ref, sems)
    rows = kv_refs[0].shape[0]
    head, side = head_side()
    near = [order_ref[0, 2 * jnp.bitwise_xor(head, m) + side] for m in range(KV_HEADS)]
    far = [order_ref[0, 2 * jnp.bitwise_xor(head, m) + 1 - side] for m in range(KV_HEADS)]
    for place, ref in zip(near + far, by_head(qd_refs[:KV_HEADS]) + list(qd_refs[KV_HEADS:])):
        for pair in range(PAIRS):
            q_all[pair, place] = ref[0:rows, pair * PAIR:(pair + 1) * PAIR]
            go_all[pair, place] = ref[0:rows, GROUP + pair * PAIR:GROUP + (pair + 1) * PAIR]
        stat_all[place] = unpacked(ref, rows)
    for place, ref in zip(near, by_head(kv_refs)):
        key_all[place], value_all[place] = stacked(ref[...])
    dq_all[...] = jnp.zeros_like(dq_all)
    for block in range(TEAM):
        mine = functools.reduce(jnp.logical_or, [place == block for place in near])

        @pl.when(mine)
        def _():
            count = TEAM - block
            shape = (rows, rows)
            mask = lax.broadcasted_iota(jnp.int32, shape, 0) <= lax.broadcasted_iota(jnp.int32, shape, 1)
            stats = jnp.concatenate([stat_all[i] for i in range(block, TEAM)], axis=1)
            query = q_all[:, block:].reshape(PAIRS * count * rows, PAIR)
            grad = go_all[:, block:].reshape(PAIRS * count * rows, PAIR)
            key_sum, value_sum, query_part = tile(
                key_all[block], value_all[block], query, grad, [pair_stats(stats, pair) for pair in range(PAIRS)], mask)
            dq_all[:, block:] += query_part.reshape(PAIRS, count, rows, PAIR)
            dkv_all[block] = folded(key_sum, value_sum)

    for m in range(KV_HEADS):
        dkv_refs[m][...] = dkv_all[near[m]].astype(jnp.bfloat16)
        for pair in range(PAIRS):
            columns = slice(pair * PAIR, (pair + 1) * PAIR)
            keep_ref[m, :, columns] = dq_all[pair, near[m]]
            send_ref[m, :, columns] = dq_all[pair, far[m]].astype(jnp.bfloat16)
    for copy in moves:
        copy.wait()


def teams_kernel(order_ref, qd_ref, kv_ref, dkv_ref, keep_ref, send_ref, dq_all):
    rows = kv_ref.shape[1]
    head, side = head_side()
    base = lax.axis_index("ctx") // TEAM * TEAM
    dq_all[...] = jnp.zeros_like(dq_all)

    @pl.loop(0, kv_ref.shape[0])
    def _(block):
        keys, values = stacked(kv_ref[block])
        dkv_ref[block] = jnp.zeros((rows, PAIR), jnp.float32)
        stored = block // KV_HEADS * TEAM + 2 * jnp.bitwise_xor(head, lax.rem(block, KV_HEADS)) + side
        place = order_ref[0, stored]

        @pl.loop(0, TEAM)
        def _(at):
            turned = jnp.where(at < KV_HEADS, side, 1 - side)
            own = order_ref[0, base + 2 * jnp.bitwise_xor(head, lax.rem(at, KV_HEADS)) + turned]

            @pl.when(place <= own)
            def _():
                shape = (rows, rows)
                mask = (place * rows + lax.broadcasted_iota(jnp.int32, shape, 0)
                        <= own * rows + lax.broadcasted_iota(jnp.int32, shape, 1))
                one = qd_ref.at[at]
                stats = unpacked(one, rows)
                for pair in range(PAIRS):
                    first = pair * PAIR
                    key_part, value_part, query_part = tile(
                        keys, values, one[0:rows, first:first + PAIR], one[0:rows, GROUP + first:GROUP + first + PAIR],
                        [pair_stats(stats, pair)], mask)
                    dq_all[at, :, first:first + PAIR] += query_part
                    dkv_ref[block] += folded(key_part, value_part)

    keep_ref[...] = dq_all[0:KV_HEADS]
    send_ref[...] = dq_all[KV_HEADS:].astype(jnp.bfloat16)


def owner_kernel(keep_ref, got_ref, *rest):
    dkv_refs, out_ref, dq_refs, parts = rest[:KV_HEADS], rest[KV_HEADS], rest[KV_HEADS + 1:-1], rest[-1]
    head, _ = head_side()
    for m, ref in enumerate(by_head(dkv_refs)):
        parts[jnp.bitwise_xor(head, m)] = ref[...]
    keys = [parts[g, :, :HEAD_DIM] for g in range(KV_HEADS)]
    values = [parts[g, :, HEAD_DIM:] for g in range(KV_HEADS)]
    out_ref[...] = jnp.concatenate(keys + values, axis=1)
    pair_kernel(keep_ref, got_ref, *dq_refs)


def pair_kernel(keep_ref, got_ref, *out_refs):
    for m, ref in enumerate(out_refs):
        ref[...] = (keep_ref[m] + got_ref[m].astype(jnp.float32)).astype(ref.dtype)


def query_kernel(*rest):
    dq_refs, out_ref = rest[:KV_HEADS], rest[KV_HEADS]
    head, _ = head_side()
    for m, ref in enumerate(by_head(dq_refs)):
        columns = pl.ds(pl.multiple_of(jnp.bitwise_xor(head, m) * GROUP, GROUP), GROUP)
        out_ref[:, columns] = ref[...]


def input_kernel(fsdp, grad_ref, *rest):
    w_refs, out_ref = rest[:fsdp], rest[fsdp]
    mine = lax.axis_index("fsdp")
    span = w_refs[0].shape[0]
    for m in range(fsdp):
        start = pl.multiple_of(jnp.bitwise_xor(mine, m) * span, span)
        out_ref[:, pl.ds(start, span)] = matmul(grad_ref[...], w_refs[m][...], NT).astype(jnp.bfloat16)


def weight_sums(fsdp, refs):
    hid = jnp.concatenate([ref[...] for ref in refs[:fsdp]], axis=0)
    grad = jnp.concatenate([ref[...] for ref in refs[fsdp:2 * fsdp]], axis=0)
    return matmul(hid, grad, TN)


def weight_kernel(fsdp, *rest):
    rest[2 * fsdp][...] = weight_sums(fsdp, rest).astype(jnp.bfloat16)


def sides_kernel(fsdp, *rest):
    keep_refs, send_refs, parts = rest[2 * fsdp:2 * fsdp + 2], rest[2 * fsdp + 2:2 * fsdp + 4], rest[-1]
    head, side = head_side()
    parts[...] = weight_sums(fsdp, rest).reshape(parts.shape)
    for m in range(KV_HEADS):
        to = 2 * jnp.bitwise_xor(head, m)
        keep_refs[m // 2][m % 2] = parts[to + side]
        send_refs[m // 2][m % 2] = parts[to + 1 - side].astype(jnp.bfloat16)


def own_total_kernel(*rest):
    part_refs, own_ref, out_ref = rest[:-2], rest[-2], rest[-1]
    total = own_ref[...]
    for ref in part_refs:
        total = total + ref[...].astype(jnp.float32)
    out_ref[...] = total


def total_kernel(part_ref, out_ref):
    total = part_ref[0].astype(jnp.float32)
    for i in range(1, part_ref.shape[0]):
        total = total + part_ref[i].astype(jnp.float32)
    out_ref[...] = total


def over_fsdp(own, bits):
    got = list(own)
    while bits:
        for m in range(len(own)):
            if m & bits:
                got[m] = swapped(got[m], "fsdp", bits)
        bits //= 2
    return got


def shards(hidden, queries, attn_out, grad_out, log_sums, block_order, w_kv):
    rows, model = hidden.shape[1:]
    fsdp, devices = lax.axis_size("fsdp"), lax.axis_size("ctx")
    teams = devices // TEAM
    f32 = jnp.float32
    span = model // fsdp
    inputs = hidden[0]
    columns = 2 * KEY_WIDTH
    block, wide = (rows, PAIR), (rows, GROUP)

    def along_heads(arrays):
        return [arrays[0]] + [swapped(arrays[m], "ctx", 2 * m) for m in range(1, KV_HEADS)]

    far = fsdp // 2
    qd = call(
        pieces_kernel, [sds((rows + 16, 2 * GROUP))] * KV_HEADS,
        [pltpu.VMEM((rows, Q_HEADS * HEAD_DIM), jnp.bfloat16)] * 2
        + [pltpu.VMEM((Q_HEADS, rows), f32), pltpu.VMEM((KV_HEADS, 2 * GROUPS, rows), f32),
           pltpu.SemaphoreType.DMA((3 + 2 * KV_HEADS,))],
        (queries[0], grad_out[0], attn_out[0], log_sums[0]), hbm=4)
    qd = along_heads(qd)
    turned = [swapped(one, "ctx", 1) for one in qd[:2]]
    w_far = held(swapped(w_kv, "fsdp", far), (*far_first(qd[:KV_HEADS])[1:], *turned))
    w_parts = over_fsdp([w_kv] * far + [w_far] * (fsdp - far), far // 2)

    kv = call(
        functools.partial(project_kernel, fsdp), [sds(block)] * KV_HEADS,
        [pltpu.VMEM((KV_HEADS,) + block, jnp.bfloat16)], (inputs, *w_parts))
    kv = along_heads(kv)
    qd = qd + turned + [swapped(one, "ctx", 1) for one in qd[2:]]

    half = (KV_HEADS,) + wide
    cut = [sds((rows, span))] * far + [sds((fsdp - far, rows, span))]
    cut_sems = pltpu.SemaphoreType.DMA((fsdp,))
    if teams == 1:
        outs = call(
            functools.partial(sequence_kernel, far), [sds(block)] * KV_HEADS + [sds(half, f32), sds(half)] + cut,
            [pltpu.VMEM((PAIRS, TEAM) + block, jnp.bfloat16)] * 2 + [pltpu.VMEM((TEAM, 2 * GROUPS, rows), f32)]
            + [pltpu.VMEM((TEAM, 2 * rows, PAIR), jnp.bfloat16)] * 2
            + [pltpu.VMEM((PAIRS, TEAM) + block, f32), pltpu.VMEM((TEAM,) + block, f32), cut_sems],
            (block_order, inputs, *far_first(qd[:KV_HEADS]), *qd[KV_HEADS:], *far_first(kv)), smem=1, hbm=1)
        dkv, (keep, give, *hid, hid_far) = outs[:KV_HEADS], outs[KV_HEADS:]
    else:
        alike = [[t * TEAM + i for t in range(teams)] for i in range(TEAM)]
        kv = lax.all_gather(jnp.stack(kv), "ctx", axis_index_groups=alike, axis=0, tiled=True)
        dkv, keep, give = call(
            teams_kernel, [sds((teams * KV_HEADS,) + block, f32), sds(half, f32), sds(half)],
            [pltpu.VMEM((TEAM,) + wide, f32)], (block_order, jnp.stack(qd), kv), smem=1)
        dkv = lax.psum_scatter(dkv, "ctx", axis_index_groups=alike, scatter_dimension=0, tiled=True)
        dkv = [dkv[m].astype(jnp.bfloat16) for m in range(KV_HEADS)]
        *hid, hid_far = call(hidden_kernel, cut, [cut_sems], (inputs,), hbm=1)

    hid_far = swapped(hid_far, "fsdp", far)
    hid = over_fsdp(hid + [hid_far[m] for m in range(fsdp - far)], far // 2)
    dkv = along_heads(dkv)
    give = swapped(give, "ctx", 1)
    kv_grad, *dq = call(
        owner_kernel, [sds((rows, columns))] + [sds(wide)] * KV_HEADS,
        [pltpu.VMEM((KV_HEADS,) + block, jnp.bfloat16)], (keep, give, *far_first(dkv)))
    dq = along_heads(dq)
    grad_far = held(swapped(kv_grad, "fsdp", far), dq[2:3])
    grads = over_fsdp([kv_grad] * far + [grad_far] * (fsdp - far), far // 2)
    if teams == 1:
        share = (span // devices, columns)
        two = (2,) + share
        near_sums, far_sums, near_send, far_send = call(
            functools.partial(sides_kernel, fsdp), [sds(two, f32)] * 2 + [sds(two)] * 2,
            [pltpu.VMEM((devices,) + share, f32)], (*hid, *grads))
        formed = (near_sums,)
        far_sums = call(pair_kernel, [sds(share)] * 2, [], (far_sums, swapped(far_send, "ctx", 1)))
        near_sums = call(
            pair_kernel, [sds(share, f32), sds(share)], [], (near_sums, swapped(near_send, "ctx", 1)))
        own_sums, *sums = far_first(along_heads([*near_sums, *far_sums]))
        (weight_grads,) = call(own_total_kernel, [sds(share, f32)], [], (*sums, own_sums))
    else:
        formed = call(functools.partial(weight_kernel, fsdp), [sds((span, columns))], [], (*hid, *grads))
        sums = lax.all_to_all(formed[0].reshape(devices, span // devices, columns), "ctx", 0, 0, tiled=True)
        (weight_grads,) = call(total_kernel, [sds((span // devices, columns), f32)], [], (sums,))
    (query_grads,) = call(query_kernel, [sds((rows, Q_HEADS * HEAD_DIM))], [], far_first(dq), after=formed)
    (input_grads,) = call(
        functools.partial(input_kernel, fsdp), [sds((rows, model))], [], (kv_grad, *w_parts), after=formed)
    return query_grads[None], input_grads[None], weight_grads


def solution(mesh):
    return jax.shard_map(
        shards,
        mesh=mesh,
        in_specs=(
            P("fsdp", "ctx", None),
            P("fsdp", "ctx", None),
            P("fsdp", "ctx", None),
            P("fsdp", "ctx", None),
            P("fsdp", None, "ctx"),
            P("fsdp", None),
            P("fsdp", None),
        ),
        out_specs=(P("fsdp", "ctx", None), P("fsdp", "ctx", None), P(("fsdp", "ctx"), None)),
        check_vma=False,
    )
```

```python
import functools

import jax
import jax.numpy as jnp
from jax import lax
from jax.experimental import pallas as pl
from jax.experimental.pallas import tpu as pltpu
from jax.sharding import PartitionSpec as P

Q_HEADS = 16
KV_HEADS = 4
HEAD_DIM = 64
GROUPS = Q_HEADS // KV_HEADS
KEY_WIDTH = KV_HEADS * HEAD_DIM
PAIR = 2 * HEAD_DIM
TEAM = 2 * KV_HEADS
PAIRS = GROUPS // 2
GROUP = GROUPS * HEAD_DIM
SCALE = HEAD_DIM ** -0.5
LOWER = HEAD_DIM

NT = (((1,), (1,)), ((), ()))
TN = (((0,), (0,)), ((), ()))
VMEM = pl.BlockSpec(memory_space=pltpu.VMEM)
SMEM = pl.BlockSpec(memory_space=pltpu.SMEM)
ANY = pl.BlockSpec(memory_space=pl.ANY)
HBM = pl.BlockSpec(memory_space=pltpu.HBM)
PARAMS = pltpu.CompilerParams(vmem_limit_bytes=40 * 1024 * 1024)
WHOLE = pltpu.CompilerParams(vmem_limit_bytes=60 * 1024 * 1024)


def matmul(left, right, dims=(((1,), (0,)), ((), ()))):
    return lax.dot_general(left, right, dims, preferred_element_type=jnp.float32)


def swapped(array, axis, bits):
    size = lax.axis_size(axis)
    return lax.ppermute(array, axis, [(i, i ^ bits) for i in range(size)])


def call(kernel, out_shape, scratch, args, smem=0, hbm=0, after=()):
    given = len(args)
    params = WHOLE if hbm == given else PARAMS

    def body(*refs):
        kernel(*refs[:given], *refs[given + len(after):])

    specs = [SMEM] * smem + [HBM] * hbm + [VMEM] * (given - smem - hbm) + [ANY] * len(after)
    return pl.pallas_call(
        body,
        out_shape=out_shape,
        in_specs=specs,
        out_specs=[VMEM] * len(out_shape),
        scratch_shapes=scratch,
        compiler_params=params,
    )(*args, *after)


def held(array, after):
    def body(*refs):
        pass

    return pl.pallas_call(
        body,
        out_shape=sds(array.shape, array.dtype),
        in_specs=[ANY] * (1 + len(after)),
        out_specs=ANY,
        input_output_aliases={0: 0},
        compiler_params=PARAMS,
    )(array, *after)


def sds(shape, dtype=jnp.bfloat16):
    return jax.ShapeDtypeStruct(shape, dtype)


def head_side():
    me = lax.rem(lax.axis_index("ctx"), TEAM)
    return me // 2, lax.rem(me, 2)


def far_first(arrays):
    return [arrays[m] for m in (0, 2, 3, 1)]


def by_head(refs):
    return [refs[i] for i in (0, 3, 1, 2)]


def split(exact):
    first = exact.astype(jnp.bfloat16).astype(jnp.float32)
    second = (exact - first).astype(jnp.bfloat16).astype(jnp.float32)
    return first, second, exact - first - second


def pieces_kernel(q_ref, go_ref, ao_ref, lse_ref, *rest):
    out_refs, (grad, output, lse, stat, sems) = rest[:KV_HEADS], rest[KV_HEADS:]
    rows, width = q_ref.shape
    head, _ = head_side()
    loads = [pltpu.make_async_copy(ref, to, sems.at[i])
             for i, (ref, to) in enumerate(((go_ref, grad), (ao_ref, output), (lse_ref, lse)))]
    moves = []
    for m in range(KV_HEADS):
        columns = pl.ds(pl.multiple_of(jnp.bitwise_xor(head, m) * GROUP, GROUP), GROUP)
        for i, ref in enumerate((q_ref, go_ref)):
            moves.append(pltpu.make_async_copy(
                ref.at[:, columns], out_refs[m].at[0:rows, i * GROUP:(i + 1) * GROUP], sems.at[3 + 2 * m + i]))
    for copy in loads + moves:
        copy.start()
    for copy in loads:
        copy.wait()
    product = grad[...].astype(jnp.float32) * output[...].astype(jnp.float32)
    high = product.astype(jnp.bfloat16)
    low = (product - high.astype(jnp.float32)).astype(jnp.bfloat16)
    head_of = lax.broadcasted_iota(jnp.int32, (Q_HEADS, width), 1) // HEAD_DIM
    ones = (head_of == lax.broadcasted_iota(jnp.int32, (Q_HEADS, width), 0)).astype(jnp.bfloat16)
    delta = matmul(ones, high, NT) + matmul(ones, low, NT)
    for g in range(KV_HEADS):
        part = slice(g * GROUPS, (g + 1) * GROUPS)
        stat[g] = jnp.concatenate([lse[part, :], delta[part, :]], axis=0)
    zero = jnp.zeros((2 * GROUPS, rows), jnp.float32)
    for m in range(KV_HEADS):
        lines = [*split(stat[jnp.bitwise_xor(head, m)]), zero]
        for i, one in enumerate(lines):
            full = jnp.concatenate([one, zero], axis=0).astype(jnp.bfloat16)
            out_refs[m][rows:, i * rows:(i + 1) * rows] = full
    for copy in moves:
        copy.wait()


def hidden_moves(hid_ref, near_refs, far_ref, sems):
    mine = lax.axis_index("fsdp")
    near = len(near_refs)
    span = far_ref.shape[2]
    copies = []
    for m in range(near + far_ref.shape[0]):
        columns = pl.ds(pl.multiple_of(jnp.bitwise_xor(mine, m) * span, span), span)
        to = near_refs[m] if m < near else far_ref.at[m - near]
        copies.append(pltpu.make_async_copy(hid_ref.at[:, columns], to, sems.at[m]))
    for copy in copies:
        copy.start()
    return copies


def hidden_kernel(hid_ref, *rest):
    for copy in hidden_moves(hid_ref, rest[:-2], *rest[-2:]):
        copy.wait()


def project_kernel(fsdp, hid_ref, *rest):
    w_refs, out_refs, (parts,) = rest[:fsdp], rest[fsdp:fsdp + KV_HEADS], rest[fsdp + KV_HEADS:]
    mine = lax.axis_index("fsdp")
    head, _ = head_side()
    span = w_refs[0].shape[0]
    total = None
    for m in range(fsdp):
        start = pl.multiple_of(jnp.bitwise_xor(mine, m) * span, span)
        term = matmul(hid_ref[:, pl.ds(start, span)], w_refs[m][...])
        total = term if total is None else total + term
    low = total.astype(jnp.bfloat16)
    for g in range(KV_HEADS):
        key = low[:, g * HEAD_DIM:(g + 1) * HEAD_DIM]
        value = low[:, KEY_WIDTH + g * HEAD_DIM:KEY_WIDTH + (g + 1) * HEAD_DIM]
        parts[g] = jnp.concatenate([key, value], axis=1)
    for m in range(KV_HEADS):
        out_refs[m][...] = parts[jnp.bitwise_xor(head, m)]


def lower_half(shape):
    return lax.broadcasted_iota(jnp.int32, shape, len(shape) - 1) < LOWER


def stacked(key_value):
    wide = key_value.astype(jnp.float32)
    turned = pltpu.roll(wide, LOWER, 1)
    lower = lower_half(wide.shape)
    zero = jnp.zeros_like(wide)
    keys = jnp.concatenate([jnp.where(lower, wide, zero), jnp.where(lower, zero, turned)], axis=0) * SCALE
    values = jnp.concatenate([jnp.where(lower, turned, zero), jnp.where(lower, zero, wide)], axis=0)
    return keys.astype(jnp.bfloat16), values.astype(jnp.bfloat16)


def tile(keys, values, query, grad, stats, mask, rooms):
    size = mask.shape[0]
    width = query.shape[0]
    of_pair = width // len(stats)
    scores, prob_grad, low, score_grad = (room.at[:, 0:width] for room in rooms)
    scores[...] = matmul(keys, query, NT)
    prob_grad[...] = matmul(values, grad, NT)
    for first in range(0, width, size):
        pair, start = first // of_pair, first % of_pair
        for head in range(2):
            part = (slice(head * size, (head + 1) * size), slice(first, first + size))
            lse, delta = (stats[pair][i][:, start:start + size] for i in (head, 2 + head))
            probs = jnp.exp(scores[part] - lse)
            if start == 0:
                probs = jnp.where(mask, probs, 0.0)
            low[part] = probs.astype(jnp.bfloat16)
            score_grad[part] = (probs * (prob_grad[part] - delta)).astype(jnp.bfloat16)
    left = score_grad[...]
    return matmul(left, query), matmul(low[...], grad), matmul(left, keys, TN)


def rooms_for(rows, width):
    return [pltpu.VMEM((2 * rows, width), kind) for kind in (jnp.float32, jnp.float32, jnp.bfloat16, jnp.bfloat16)]


def folded(key_sum, value_sum):
    size = key_sum.shape[0] // 2
    lower = lower_half((size, PAIR))
    straight = jnp.where(lower, key_sum[:size], value_sum[size:])
    crossed = jnp.where(lower, value_sum[:size], key_sum[size:])
    return (straight + pltpu.roll(crossed, LOWER, 1)) * jnp.where(lower, SCALE, 1.0)


def unpacked(part, rows):
    exact = part[rows:, 0:3 * rows].astype(jnp.float32)[0:2 * GROUPS]
    return exact[:, 0:rows] + exact[:, rows:2 * rows] + exact[:, 2 * rows:]


def pair_stats(stat, pair):
    first = 2 * pair
    return [stat[first:first + 1], stat[first + 1:first + 2],
            stat[GROUPS + first:GROUPS + first + 1], stat[GROUPS + first + 1:GROUPS + first + 2]]


def sequence_kernel(near_parts, order_ref, hid_ref, *rest):
    qd_refs, kv_refs, rest = rest[:TEAM], rest[TEAM:TEAM + KV_HEADS], rest[TEAM + KV_HEADS:]
    dkv_refs, keep_ref, send_ref, rest = rest[:KV_HEADS], rest[KV_HEADS], rest[KV_HEADS + 1], rest[KV_HEADS + 2:]
    near_refs, far_ref, rest = rest[:near_parts], rest[near_parts], rest[near_parts + 1:]
    q_all, go_all, stat_all, key_all, value_all, dq_all, dkv_all, sems, *rooms = rest
    moves = hidden_moves(hid_ref, near_refs, far_ref, sems)
    rows = kv_refs[0].shape[0]
    head, side = head_side()
    near = [order_ref[0, 2 * jnp.bitwise_xor(head, m) + side] for m in range(KV_HEADS)]
    far = [order_ref[0, 2 * jnp.bitwise_xor(head, m) + 1 - side] for m in range(KV_HEADS)]
    for place, ref in zip(near + far, by_head(qd_refs[:KV_HEADS]) + list(qd_refs[KV_HEADS:])):
        for pair in range(PAIRS):
            q_all[pair, place] = ref[0:rows, pair * PAIR:(pair + 1) * PAIR]
            go_all[pair, place] = ref[0:rows, GROUP + pair * PAIR:GROUP + (pair + 1) * PAIR]
        stat_all[place] = unpacked(ref, rows)
    for place, ref in zip(near, by_head(kv_refs)):
        key_all[place], value_all[place] = stacked(ref[...])
    dq_all[...] = jnp.zeros_like(dq_all)
    for block in range(TEAM):
        mine = functools.reduce(jnp.logical_or, [place == block for place in near])

        @pl.when(mine)
        def _():
            count = TEAM - block
            shape = (rows, rows)
            mask = lax.broadcasted_iota(jnp.int32, shape, 0) <= lax.broadcasted_iota(jnp.int32, shape, 1)
            stats = jnp.concatenate([stat_all[i] for i in range(block, TEAM)], axis=1)
            query = q_all[:, block:].reshape(PAIRS * count * rows, PAIR)
            grad = go_all[:, block:].reshape(PAIRS * count * rows, PAIR)
            key_sum, value_sum, query_part = tile(
                key_all[block], value_all[block], query, grad, [pair_stats(stats, pair) for pair in range(PAIRS)], mask,
                rooms)
            dq_all[:, block:] += query_part.reshape(PAIRS, count, rows, PAIR)
            dkv_all[block] = folded(key_sum, value_sum)

    for m in range(KV_HEADS):
        dkv_refs[m][...] = dkv_all[near[m]].astype(jnp.bfloat16)
        for pair in range(PAIRS):
            columns = slice(pair * PAIR, (pair + 1) * PAIR)
            keep_ref[m, :, columns] = dq_all[pair, near[m]]
            send_ref[m, :, columns] = dq_all[pair, far[m]].astype(jnp.bfloat16)
    for copy in moves:
        copy.wait()


def teams_kernel(order_ref, qd_ref, kv_ref, dkv_ref, keep_ref, send_ref, dq_all, *rooms):
    rows = kv_ref.shape[1]
    head, side = head_side()
    base = lax.axis_index("ctx") // TEAM * TEAM
    dq_all[...] = jnp.zeros_like(dq_all)

    @pl.loop(0, kv_ref.shape[0])
    def _(block):
        keys, values = stacked(kv_ref[block])
        dkv_ref[block] = jnp.zeros((rows, PAIR), jnp.float32)
        stored = block // KV_HEADS * TEAM + 2 * jnp.bitwise_xor(head, lax.rem(block, KV_HEADS)) + side
        place = order_ref[0, stored]

        @pl.loop(0, TEAM)
        def _(at):
            turned = jnp.where(at < KV_HEADS, side, 1 - side)
            own = order_ref[0, base + 2 * jnp.bitwise_xor(head, lax.rem(at, KV_HEADS)) + turned]

            @pl.when(place <= own)
            def _():
                shape = (rows, rows)
                mask = (place * rows + lax.broadcasted_iota(jnp.int32, shape, 0)
                        <= own * rows + lax.broadcasted_iota(jnp.int32, shape, 1))
                one = qd_ref.at[at]
                stats = unpacked(one, rows)
                for pair in range(PAIRS):
                    first = pair * PAIR
                    key_part, value_part, query_part = tile(
                        keys, values, one[0:rows, first:first + PAIR], one[0:rows, GROUP + first:GROUP + first + PAIR],
                        [pair_stats(stats, pair)], mask, rooms)
                    dq_all[at, :, first:first + PAIR] += query_part
                    dkv_ref[block] += folded(key_part, value_part)

    keep_ref[...] = dq_all[0:KV_HEADS]
    send_ref[...] = dq_all[KV_HEADS:].astype(jnp.bfloat16)


def owner_kernel(*rest):
    dkv_refs, out_ref, parts = rest[:KV_HEADS], rest[KV_HEADS], rest[KV_HEADS + 1]
    head, _ = head_side()
    for m, ref in enumerate(by_head(dkv_refs)):
        parts[jnp.bitwise_xor(head, m)] = ref[...]
    keys = [parts[g, :, :HEAD_DIM] for g in range(KV_HEADS)]
    values = [parts[g, :, HEAD_DIM:] for g in range(KV_HEADS)]
    out_ref[...] = jnp.concatenate(keys + values, axis=1)


def pair_kernel(keep_ref, got_ref, *out_refs):
    for m, ref in enumerate(out_refs):
        ref[...] = (keep_ref[m] + got_ref[m].astype(jnp.float32)).astype(ref.dtype)


def query_kernel(*rest):
    dq_refs, out_ref = rest[:KV_HEADS], rest[KV_HEADS]
    head, _ = head_side()
    for m, ref in enumerate(by_head(dq_refs)):
        columns = pl.ds(pl.multiple_of(jnp.bitwise_xor(head, m) * GROUP, GROUP), GROUP)
        out_ref[:, columns] = ref[...]


def input_kernel(fsdp, grad_ref, *rest):
    w_refs, out_ref = rest[:fsdp], rest[fsdp]
    mine = lax.axis_index("fsdp")
    span = w_refs[0].shape[0]
    for m in range(fsdp):
        start = pl.multiple_of(jnp.bitwise_xor(mine, m) * span, span)
        out_ref[:, pl.ds(start, span)] = matmul(grad_ref[...], w_refs[m][...], NT).astype(jnp.bfloat16)


def weight_sums(fsdp, refs):
    hid = jnp.concatenate([ref[...] for ref in refs[:fsdp]], axis=0)
    grad = jnp.concatenate([ref[...] for ref in refs[fsdp:2 * fsdp]], axis=0)
    return matmul(hid, grad, TN)


def weight_kernel(fsdp, *rest):
    rest[2 * fsdp][...] = weight_sums(fsdp, rest).astype(jnp.bfloat16)


def sides_kernel(fsdp, *rest):
    keep_refs, send_refs, parts = rest[2 * fsdp:2 * fsdp + 2], rest[2 * fsdp + 2:2 * fsdp + 4], rest[-1]
    head, side = head_side()
    parts[...] = weight_sums(fsdp, rest).reshape(parts.shape)
    for m in range(KV_HEADS):
        to = 2 * jnp.bitwise_xor(head, m)
        keep_refs[m // 2][m % 2] = parts[to + side]
        send_refs[m // 2][m % 2] = parts[to + 1 - side].astype(jnp.bfloat16)


def own_total_kernel(*rest):
    part_refs, own_ref, out_ref = rest[:-2], rest[-2], rest[-1]
    total = own_ref[...]
    for ref in part_refs:
        total = total + ref[...].astype(jnp.float32)
    out_ref[...] = total


def total_kernel(part_ref, out_ref):
    total = part_ref[0].astype(jnp.float32)
    for i in range(1, part_ref.shape[0]):
        total = total + part_ref[i].astype(jnp.float32)
    out_ref[...] = total


def over_fsdp(own, bits):
    got = list(own)
    while bits:
        for m in range(len(own)):
            if m & bits:
                got[m] = swapped(got[m], "fsdp", bits)
        bits //= 2
    return got


def shards(hidden, queries, attn_out, grad_out, log_sums, block_order, w_kv):
    rows, model = hidden.shape[1:]
    fsdp, devices = lax.axis_size("fsdp"), lax.axis_size("ctx")
    teams = devices // TEAM
    f32 = jnp.float32
    span = model // fsdp
    inputs = hidden[0]
    columns = 2 * KEY_WIDTH
    block, wide = (rows, PAIR), (rows, GROUP)

    def along_heads(arrays):
        return [arrays[0]] + [swapped(arrays[m], "ctx", 2 * m) for m in range(1, KV_HEADS)]

    far = fsdp // 2
    qd = call(
        pieces_kernel, [sds((rows + 16, 2 * GROUP))] * KV_HEADS,
        [pltpu.VMEM((rows, Q_HEADS * HEAD_DIM), jnp.bfloat16)] * 2
        + [pltpu.VMEM((Q_HEADS, rows), f32), pltpu.VMEM((KV_HEADS, 2 * GROUPS, rows), f32),
           pltpu.SemaphoreType.DMA((3 + 2 * KV_HEADS,))],
        (queries[0], grad_out[0], attn_out[0], log_sums[0]), hbm=4)
    qd = along_heads(qd)
    turned = [swapped(one, "ctx", 1) for one in qd[:2]]
    w_far = held(swapped(w_kv, "fsdp", far), (*far_first(qd[:KV_HEADS])[1:], *turned))
    w_parts = over_fsdp([w_kv] * far + [w_far] * (fsdp - far), far // 2)

    kv = call(
        functools.partial(project_kernel, fsdp), [sds(block)] * KV_HEADS,
        [pltpu.VMEM((KV_HEADS,) + block, jnp.bfloat16)], (inputs, *w_parts))
    kv = along_heads(kv)
    qd = qd + turned + [swapped(one, "ctx", 1) for one in qd[2:]]

    half = (KV_HEADS,) + wide
    cut = [sds((rows, span))] * far + [sds((fsdp - far, rows, span))]
    cut_sems = pltpu.SemaphoreType.DMA((fsdp,))
    if teams == 1:
        outs = call(
            functools.partial(sequence_kernel, far), [sds(block)] * KV_HEADS + [sds(half, f32), sds(half)] + cut,
            [pltpu.VMEM((PAIRS, TEAM) + block, jnp.bfloat16)] * 2 + [pltpu.VMEM((TEAM, 2 * GROUPS, rows), f32)]
            + [pltpu.VMEM((TEAM, 2 * rows, PAIR), jnp.bfloat16)] * 2
            + [pltpu.VMEM((PAIRS, TEAM) + block, f32), pltpu.VMEM((TEAM,) + block, f32), cut_sems]
            + rooms_for(rows, PAIRS * TEAM * rows),
            (block_order, inputs, *far_first(qd[:KV_HEADS]), *qd[KV_HEADS:], *far_first(kv)), smem=1, hbm=1)
        dkv, (keep, give, *hid, hid_far) = outs[:KV_HEADS], outs[KV_HEADS:]
    else:
        alike = [[t * TEAM + i for t in range(teams)] for i in range(TEAM)]
        kv = lax.all_gather(jnp.stack(kv), "ctx", axis_index_groups=alike, axis=0, tiled=True)
        dkv, keep, give = call(
            teams_kernel, [sds((teams * KV_HEADS,) + block, f32), sds(half, f32), sds(half)],
            [pltpu.VMEM((TEAM,) + wide, f32)] + rooms_for(rows, rows), (block_order, jnp.stack(qd), kv), smem=1)
        dkv = lax.psum_scatter(dkv, "ctx", axis_index_groups=alike, scatter_dimension=0, tiled=True)
        dkv = [dkv[m].astype(jnp.bfloat16) for m in range(KV_HEADS)]
        *hid, hid_far = call(hidden_kernel, cut, [cut_sems], (inputs,), hbm=1)

    hid_far = swapped(hid_far, "fsdp", far)
    hid = over_fsdp(hid + [hid_far[m] for m in range(fsdp - far)], far // 2)
    dkv = along_heads(dkv)
    give = swapped(give, "ctx", 1)
    (kv_grad,) = call(
        owner_kernel, [sds((rows, columns))], [pltpu.VMEM((KV_HEADS,) + block, jnp.bfloat16)],
        far_first(dkv), after=(give,))
    grads = over_fsdp([kv_grad] * fsdp, far)
    if teams == 1:
        share = (span // devices, columns)
        two = (2,) + share
        near_sums, far_sums, near_send, far_send = call(
            functools.partial(sides_kernel, fsdp), [sds(two, f32)] * 2 + [sds(two)] * 2,
            [pltpu.VMEM((devices,) + share, f32)], (*hid, *grads))
        formed = (near_sums,)
        dq = along_heads(call(pair_kernel, [sds(wide)] * KV_HEADS, [], (keep, give), after=formed))
        far_sums = call(pair_kernel, [sds(share)] * 2, [], (far_sums, swapped(far_send, "ctx", 1)))
        near_sums = call(
            pair_kernel, [sds(share, f32), sds(share)], [], (near_sums, swapped(near_send, "ctx", 1)), after=dq[1:2])
        own_sums, *sums = far_first(along_heads([*near_sums, *far_sums]))
        (weight_grads,) = call(own_total_kernel, [sds(share, f32)], [], (*sums, own_sums))
    else:
        formed = call(functools.partial(weight_kernel, fsdp), [sds((span, columns))], [], (*hid, *grads))
        dq = along_heads(call(pair_kernel, [sds(wide)] * KV_HEADS, [], (keep, give), after=formed))
        sums = lax.all_to_all(formed[0].reshape(devices, span // devices, columns), "ctx", 0, 0, tiled=True)
        (weight_grads,) = call(total_kernel, [sds((span // devices, columns), f32)], [], (sums,))
    (query_grads,) = call(query_kernel, [sds((rows, Q_HEADS * HEAD_DIM))], [], far_first(dq), after=formed)
    (input_grads,) = call(
        functools.partial(input_kernel, fsdp), [sds((rows, model))], [], (kv_grad, *w_parts), after=formed)
    return query_grads[None], input_grads[None], weight_grads


def solution(mesh):
    return jax.shard_map(
        shards,
        mesh=mesh,
        in_specs=(
            P("fsdp", "ctx", None),
            P("fsdp", "ctx", None),
            P("fsdp", "ctx", None),
            P("fsdp", "ctx", None),
            P("fsdp", None, "ctx"),
            P("fsdp", None),
            P("fsdp", None),
        ),
        out_specs=(P("fsdp", "ctx", None), P("fsdp", "ctx", None), P(("fsdp", "ctx"), None)),
        check_vma=False,
    )
```

```python
import functools

import jax
import jax.numpy as jnp
from jax import lax
from jax.experimental import pallas as pl
from jax.experimental.pallas import tpu as pltpu
from jax.sharding import PartitionSpec as P

Q_HEADS = 16
KV_HEADS = 4
HEAD_DIM = 64
GROUPS = Q_HEADS // KV_HEADS
KEY_WIDTH = KV_HEADS * HEAD_DIM
PAIR = 2 * HEAD_DIM
TEAM = 2 * KV_HEADS
PAIRS = GROUPS // 2
GROUP = GROUPS * HEAD_DIM
SCALE = HEAD_DIM ** -0.5
LOWER = HEAD_DIM

NT = (((1,), (1,)), ((), ()))
TN = (((0,), (0,)), ((), ()))
VMEM = pl.BlockSpec(memory_space=pltpu.VMEM)
SMEM = pl.BlockSpec(memory_space=pltpu.SMEM)
ANY = pl.BlockSpec(memory_space=pl.ANY)
HBM = pl.BlockSpec(memory_space=pltpu.HBM)
PARAMS = pltpu.CompilerParams(vmem_limit_bytes=40 * 1024 * 1024)
WHOLE = pltpu.CompilerParams(vmem_limit_bytes=60 * 1024 * 1024)


def matmul(left, right, dims=(((1,), (0,)), ((), ()))):
    return lax.dot_general(left, right, dims, preferred_element_type=jnp.float32)


def swapped(array, axis, bits):
    size = lax.axis_size(axis)
    return lax.ppermute(array, axis, [(i, i ^ bits) for i in range(size)])


def call(kernel, out_shape, scratch, args, smem=0, hbm=0, after=()):
    given = len(args)
    params = WHOLE if hbm == given else PARAMS

    def body(*refs):
        kernel(*refs[:given], *refs[given + len(after):])

    specs = [SMEM] * smem + [HBM] * hbm + [VMEM] * (given - smem - hbm) + [ANY] * len(after)
    return pl.pallas_call(
        body,
        out_shape=out_shape,
        in_specs=specs,
        out_specs=[VMEM] * len(out_shape),
        scratch_shapes=scratch,
        compiler_params=params,
    )(*args, *after)


def held(array, after):
    def body(*refs):
        pass

    return pl.pallas_call(
        body,
        out_shape=sds(array.shape, array.dtype),
        in_specs=[ANY] * (1 + len(after)),
        out_specs=ANY,
        input_output_aliases={0: 0},
        compiler_params=PARAMS,
    )(array, *after)


def sds(shape, dtype=jnp.bfloat16):
    return jax.ShapeDtypeStruct(shape, dtype)


def head_side():
    me = lax.rem(lax.axis_index("ctx"), TEAM)
    return me // 2, lax.rem(me, 2)


def far_first(arrays):
    return [arrays[m] for m in (0, 2, 3, 1)]


def by_head(refs):
    return [refs[i] for i in (0, 3, 1, 2)]


def split(exact):
    first = exact.astype(jnp.bfloat16).astype(jnp.float32)
    second = (exact - first).astype(jnp.bfloat16).astype(jnp.float32)
    return first, second, exact - first - second


def pieces_kernel(q_ref, go_ref, ao_ref, lse_ref, *rest):
    out_refs, (grad, output, lse, stat, sems) = rest[:KV_HEADS], rest[KV_HEADS:]
    rows, width = q_ref.shape
    head, _ = head_side()
    loads = [pltpu.make_async_copy(ref, to, sems.at[i])
             for i, (ref, to) in enumerate(((go_ref, grad), (ao_ref, output), (lse_ref, lse)))]
    columns = [pl.ds(pl.multiple_of(jnp.bitwise_xor(head, m) * GROUP, GROUP), GROUP) for m in range(KV_HEADS)]
    moves = [pltpu.make_async_copy(q_ref.at[:, columns[m]], out_refs[m].at[0:rows, 0:GROUP], sems.at[3 + m])
             for m in range(KV_HEADS)]
    for copy in loads + moves:
        copy.start()
    for copy in loads:
        copy.wait()
    product = grad[...].astype(jnp.float32) * output[...].astype(jnp.float32)
    high = product.astype(jnp.bfloat16)
    low = (product - high.astype(jnp.float32)).astype(jnp.bfloat16)
    head_of = lax.broadcasted_iota(jnp.int32, (Q_HEADS, width), 1) // HEAD_DIM
    ones = (head_of == lax.broadcasted_iota(jnp.int32, (Q_HEADS, width), 0)).astype(jnp.bfloat16)
    delta = matmul(ones, high, NT) + matmul(ones, low, NT)
    for g in range(KV_HEADS):
        part = slice(g * GROUPS, (g + 1) * GROUPS)
        stat[g] = jnp.concatenate([lse[part, :], delta[part, :]], axis=0)
    zero = jnp.zeros((2 * GROUPS, rows), jnp.float32)
    for m in range(KV_HEADS):
        out_refs[m][0:rows, GROUP:] = grad[:, columns[m]]
        lines = [*split(stat[jnp.bitwise_xor(head, m)]), zero]
        for i, one in enumerate(lines):
            full = jnp.concatenate([one, zero], axis=0).astype(jnp.bfloat16)
            out_refs[m][rows:, i * rows:(i + 1) * rows] = full
    for copy in moves:
        copy.wait()


def hidden_moves(hid_ref, near_refs, far_ref, sems):
    mine = lax.axis_index("fsdp")
    near = len(near_refs)
    span = far_ref.shape[2]
    copies = []
    for m in range(near + far_ref.shape[0]):
        columns = pl.ds(pl.multiple_of(jnp.bitwise_xor(mine, m) * span, span), span)
        to = near_refs[m] if m < near else far_ref.at[m - near]
        copies.append(pltpu.make_async_copy(hid_ref.at[:, columns], to, sems.at[m]))
    for copy in copies:
        copy.start()
    return copies


def hidden_kernel(hid_ref, *rest):
    for copy in hidden_moves(hid_ref, rest[:-2], *rest[-2:]):
        copy.wait()


def project_kernel(fsdp, hid_ref, *rest):
    w_refs, out_refs, (parts,) = rest[:fsdp], rest[fsdp:fsdp + KV_HEADS], rest[fsdp + KV_HEADS:]
    mine = lax.axis_index("fsdp")
    head, _ = head_side()
    span = w_refs[0].shape[0]
    total = None
    for m in range(fsdp):
        start = pl.multiple_of(jnp.bitwise_xor(mine, m) * span, span)
        term = matmul(hid_ref[:, pl.ds(start, span)], w_refs[m][...])
        total = term if total is None else total + term
    low = total.astype(jnp.bfloat16)
    for g in range(KV_HEADS):
        key = low[:, g * HEAD_DIM:(g + 1) * HEAD_DIM]
        value = low[:, KEY_WIDTH + g * HEAD_DIM:KEY_WIDTH + (g + 1) * HEAD_DIM]
        parts[g] = jnp.concatenate([key, value], axis=1)
    for m in range(KV_HEADS):
        out_refs[m][...] = parts[jnp.bitwise_xor(head, m)]


def lower_half(shape):
    return lax.broadcasted_iota(jnp.int32, shape, len(shape) - 1) < LOWER


def stacked(key_value):
    wide = key_value.astype(jnp.float32)
    turned = pltpu.roll(wide, LOWER, 1)
    lower = lower_half(wide.shape)
    zero = jnp.zeros_like(wide)
    keys = jnp.concatenate([jnp.where(lower, wide, zero), jnp.where(lower, zero, turned)], axis=0) * SCALE
    values = jnp.concatenate([jnp.where(lower, turned, zero), jnp.where(lower, zero, wide)], axis=0)
    return keys.astype(jnp.bfloat16), values.astype(jnp.bfloat16)


def tile(keys, values, query, grad, stats, mask):
    size, edge = keys.shape[0] // 2, mask.shape[1]
    pairs = len(stats)
    width = query.shape[0] // pairs
    scores = matmul(keys, query, NT)
    prob_grad = matmul(values, grad, NT)
    lows, grads = [], []
    for head in range(2):
        part = slice(head * size, (head + 1) * size)
        lse = jnp.concatenate([lines[head] for lines in stats], axis=1)
        delta = jnp.concatenate([lines[2 + head] for lines in stats], axis=1)
        probs = jnp.exp(scores[part] - lse)
        pieces = []
        for first in range(0, pairs * width, width):
            pieces.append(jnp.where(mask, probs[:, first:first + edge], 0.0))
            if edge < width:
                pieces.append(probs[:, first + edge:first + width])
        probs = jnp.concatenate(pieces, axis=1)
        lows.append(probs.astype(jnp.bfloat16))
        grads.append((probs * (prob_grad[part] - delta)).astype(jnp.bfloat16))
    low, score_grad = jnp.concatenate(lows, axis=0), jnp.concatenate(grads, axis=0)
    return matmul(score_grad, query), matmul(low, grad), matmul(score_grad, keys, TN)


def folded(key_sum, value_sum):
    size = key_sum.shape[0] // 2
    lower = lower_half((size, PAIR))
    straight = jnp.where(lower, key_sum[:size], value_sum[size:])
    crossed = jnp.where(lower, value_sum[:size], key_sum[size:])
    return (straight + pltpu.roll(crossed, LOWER, 1)) * jnp.where(lower, SCALE, 1.0)


def unpacked(part, rows):
    exact = part[rows:, 0:3 * rows].astype(jnp.float32)[0:2 * GROUPS]
    return exact[:, 0:rows] + exact[:, rows:2 * rows] + exact[:, 2 * rows:]


def pair_stats(stat, pair):
    first = 2 * pair
    return [stat[first:first + 1], stat[first + 1:first + 2],
            stat[GROUPS + first:GROUPS + first + 1], stat[GROUPS + first + 1:GROUPS + first + 2]]


def sequence_kernel(near_parts, order_ref, hid_ref, *rest):
    qd_refs, kv_refs, rest = rest[:TEAM], rest[TEAM:TEAM + KV_HEADS], rest[TEAM + KV_HEADS:]
    dkv_refs, keep_ref, send_ref, rest = rest[:KV_HEADS], rest[KV_HEADS], rest[KV_HEADS + 1], rest[KV_HEADS + 2:]
    near_refs, far_ref, rest = rest[:near_parts], rest[near_parts], rest[near_parts + 1:]
    q_all, go_all, stat_all, key_all, value_all, dq_all, dkv_all, sems = rest
    moves = hidden_moves(hid_ref, near_refs, far_ref, sems)
    rows = kv_refs[0].shape[0]
    head, side = head_side()
    near = [order_ref[0, 2 * jnp.bitwise_xor(head, m) + side] for m in range(KV_HEADS)]
    far = [order_ref[0, 2 * jnp.bitwise_xor(head, m) + 1 - side] for m in range(KV_HEADS)]
    for place, ref in zip(near + far, by_head(qd_refs[:KV_HEADS]) + list(qd_refs[KV_HEADS:])):
        for pair in range(PAIRS):
            q_all[pair, place] = ref[0:rows, pair * PAIR:(pair + 1) * PAIR]
            go_all[pair, place] = ref[0:rows, GROUP + pair * PAIR:GROUP + (pair + 1) * PAIR]
        stat_all[place] = unpacked(ref, rows)
    for place, ref in zip(near, by_head(kv_refs)):
        key_all[place], value_all[place] = stacked(ref[...])
    dq_all[...] = jnp.zeros_like(dq_all)
    for block in range(TEAM):
        mine = functools.reduce(jnp.logical_or, [place == block for place in near])

        @pl.when(mine)
        def _():
            count = TEAM - block
            shape = (rows, rows)
            mask = lax.broadcasted_iota(jnp.int32, shape, 0) <= lax.broadcasted_iota(jnp.int32, shape, 1)
            stats = jnp.concatenate([stat_all[i] for i in range(block, TEAM)], axis=1)
            query = q_all[:, block:].reshape(PAIRS * count * rows, PAIR)
            grad = go_all[:, block:].reshape(PAIRS * count * rows, PAIR)
            key_sum, value_sum, query_part = tile(
                key_all[block], value_all[block], query, grad, [pair_stats(stats, pair) for pair in range(PAIRS)], mask)
            dq_all[:, block:] += query_part.reshape(PAIRS, count, rows, PAIR)
            dkv_all[block] = folded(key_sum, value_sum)

    for m in range(KV_HEADS):
        dkv_refs[m][...] = dkv_all[near[m]].astype(jnp.bfloat16)
        for pair in range(PAIRS):
            columns = slice(pair * PAIR, (pair + 1) * PAIR)
            keep_ref[m, :, columns] = dq_all[pair, near[m]]
            send_ref[m, :, columns] = dq_all[pair, far[m]].astype(jnp.bfloat16)
    for copy in moves:
        copy.wait()


def teams_kernel(order_ref, qd_ref, kv_ref, dkv_ref, keep_ref, send_ref, dq_all):
    rows = kv_ref.shape[1]
    head, side = head_side()
    base = lax.axis_index("ctx") // TEAM * TEAM
    dq_all[...] = jnp.zeros_like(dq_all)

    @pl.loop(0, kv_ref.shape[0])
    def _(block):
        keys, values = stacked(kv_ref[block])
        dkv_ref[block] = jnp.zeros((rows, PAIR), jnp.float32)
        stored = block // KV_HEADS * TEAM + 2 * jnp.bitwise_xor(head, lax.rem(block, KV_HEADS)) + side
        place = order_ref[0, stored]

        @pl.loop(0, TEAM)
        def _(at):
            turned = jnp.where(at < KV_HEADS, side, 1 - side)
            own = order_ref[0, base + 2 * jnp.bitwise_xor(head, lax.rem(at, KV_HEADS)) + turned]

            @pl.when(place <= own)
            def _():
                shape = (rows, rows)
                mask = (place * rows + lax.broadcasted_iota(jnp.int32, shape, 0)
                        <= own * rows + lax.broadcasted_iota(jnp.int32, shape, 1))
                one = qd_ref.at[at]
                stats = unpacked(one, rows)
                for pair in range(PAIRS):
                    first = pair * PAIR
                    key_part, value_part, query_part = tile(
                        keys, values, one[0:rows, first:first + PAIR], one[0:rows, GROUP + first:GROUP + first + PAIR],
                        [pair_stats(stats, pair)], mask)
                    dq_all[at, :, first:first + PAIR] += query_part
                    dkv_ref[block] += folded(key_part, value_part)

    keep_ref[...] = dq_all[0:KV_HEADS]
    send_ref[...] = dq_all[KV_HEADS:].astype(jnp.bfloat16)


def owner_kernel(*rest):
    dkv_refs, out_ref, parts = rest[:KV_HEADS], rest[KV_HEADS], rest[KV_HEADS + 1]
    head, _ = head_side()
    for m, ref in enumerate(by_head(dkv_refs)):
        parts[jnp.bitwise_xor(head, m)] = ref[...]
    keys = [parts[g, :, :HEAD_DIM] for g in range(KV_HEADS)]
    values = [parts[g, :, HEAD_DIM:] for g in range(KV_HEADS)]
    out_ref[...] = jnp.concatenate(keys + values, axis=1)


def pair_kernel(keep_ref, got_ref, *out_refs):
    for m, ref in enumerate(out_refs):
        ref[...] = (keep_ref[m] + got_ref[m].astype(jnp.float32)).astype(ref.dtype)


def query_kernel(*rest):
    dq_refs, out_ref = rest[:KV_HEADS], rest[KV_HEADS]
    head, _ = head_side()
    for m, ref in enumerate(by_head(dq_refs)):
        columns = pl.ds(pl.multiple_of(jnp.bitwise_xor(head, m) * GROUP, GROUP), GROUP)
        out_ref[:, columns] = ref[...]


def input_kernel(fsdp, grad_ref, *rest):
    w_refs, out_ref = rest[:fsdp], rest[fsdp]
    mine = lax.axis_index("fsdp")
    span = w_refs[0].shape[0]
    for m in range(fsdp):
        start = pl.multiple_of(jnp.bitwise_xor(mine, m) * span, span)
        out_ref[:, pl.ds(start, span)] = matmul(grad_ref[...], w_refs[m][...], NT).astype(jnp.bfloat16)


def weight_sums(fsdp, refs):
    hid = jnp.concatenate([ref[...] for ref in refs[:fsdp]], axis=0)
    grad = jnp.concatenate([ref[...] for ref in refs[fsdp:2 * fsdp]], axis=0)
    return matmul(hid, grad, TN)


def weight_kernel(fsdp, *rest):
    rest[2 * fsdp][...] = weight_sums(fsdp, rest).astype(jnp.bfloat16)


def sides_kernel(fsdp, *rest):
    keep_refs, send_refs, parts = rest[2 * fsdp:2 * fsdp + 2], rest[2 * fsdp + 2:2 * fsdp + 4], rest[-1]
    head, side = head_side()
    parts[...] = weight_sums(fsdp, rest).reshape(parts.shape)
    for m in range(KV_HEADS):
        to = 2 * jnp.bitwise_xor(head, m)
        keep_refs[m // 2][m % 2] = parts[to + side]
        send_refs[m // 2][m % 2] = parts[to + 1 - side].astype(jnp.bfloat16)


def own_total_kernel(*rest):
    part_refs, own_ref, out_ref = rest[:-2], rest[-2], rest[-1]
    total = own_ref[...]
    for ref in part_refs:
        total = total + ref[...].astype(jnp.float32)
    out_ref[...] = total


def total_kernel(part_ref, out_ref):
    total = part_ref[0].astype(jnp.float32)
    for i in range(1, part_ref.shape[0]):
        total = total + part_ref[i].astype(jnp.float32)
    out_ref[...] = total


def over_fsdp(own, bits):
    got = list(own)
    while bits:
        for m in range(len(own)):
            if m & bits:
                got[m] = swapped(got[m], "fsdp", bits)
        bits //= 2
    return got


def shards(hidden, queries, attn_out, grad_out, log_sums, block_order, w_kv):
    rows, model = hidden.shape[1:]
    fsdp, devices = lax.axis_size("fsdp"), lax.axis_size("ctx")
    teams = devices // TEAM
    f32 = jnp.float32
    span = model // fsdp
    inputs = hidden[0]
    columns = 2 * KEY_WIDTH
    block, wide = (rows, PAIR), (rows, GROUP)

    def along_heads(arrays):
        return [arrays[0]] + [swapped(arrays[m], "ctx", 2 * m) for m in range(1, KV_HEADS)]

    far = fsdp // 2
    qd = call(
        pieces_kernel, [sds((rows + 16, 2 * GROUP))] * KV_HEADS,
        [pltpu.VMEM((rows, Q_HEADS * HEAD_DIM), jnp.bfloat16)] * 2
        + [pltpu.VMEM((Q_HEADS, rows), f32), pltpu.VMEM((KV_HEADS, 2 * GROUPS, rows), f32),
           pltpu.SemaphoreType.DMA((3 + KV_HEADS,))],
        (queries[0], grad_out[0], attn_out[0], log_sums[0]), hbm=4)
    qd = along_heads(qd)
    turned = [swapped(one, "ctx", 1) for one in qd[:2]]
    w_far = held(swapped(w_kv, "fsdp", far), (*far_first(qd[:KV_HEADS])[1:], *turned))
    w_parts = over_fsdp([w_kv] * far + [w_far] * (fsdp - far), far // 2)

    kv = call(
        functools.partial(project_kernel, fsdp), [sds(block)] * KV_HEADS,
        [pltpu.VMEM((KV_HEADS,) + block, jnp.bfloat16)], (inputs, *w_parts))
    kv = along_heads(kv)
    qd = qd + turned + [swapped(one, "ctx", 1) for one in qd[2:]]

    half = (KV_HEADS,) + wide
    cut = [sds((rows, span))] * far + [sds((fsdp - far, rows, span))]
    cut_sems = pltpu.SemaphoreType.DMA((fsdp,))
    if teams == 1:
        outs = call(
            functools.partial(sequence_kernel, far), [sds(block)] * KV_HEADS + [sds(half, f32), sds(half)] + cut,
            [pltpu.VMEM((PAIRS, TEAM) + block, jnp.bfloat16)] * 2 + [pltpu.VMEM((TEAM, 2 * GROUPS, rows), f32)]
            + [pltpu.VMEM((TEAM, 2 * rows, PAIR), jnp.bfloat16)] * 2
            + [pltpu.VMEM((PAIRS, TEAM) + block, f32), pltpu.VMEM((TEAM,) + block, f32), cut_sems],
            (block_order, inputs, *far_first(qd[:KV_HEADS]), *qd[KV_HEADS:], *far_first(kv)), smem=1, hbm=1)
        dkv, (keep, give, *hid, hid_far) = outs[:KV_HEADS], outs[KV_HEADS:]
    else:
        alike = [[t * TEAM + i for t in range(teams)] for i in range(TEAM)]
        kv = lax.all_gather(jnp.stack(kv), "ctx", axis_index_groups=alike, axis=0, tiled=True)
        dkv, keep, give = call(
            teams_kernel, [sds((teams * KV_HEADS,) + block, f32), sds(half, f32), sds(half)],
            [pltpu.VMEM((TEAM,) + wide, f32)], (block_order, jnp.stack(qd), kv), smem=1)
        dkv = lax.psum_scatter(dkv, "ctx", axis_index_groups=alike, scatter_dimension=0, tiled=True)
        dkv = [dkv[m].astype(jnp.bfloat16) for m in range(KV_HEADS)]
        *hid, hid_far = call(hidden_kernel, cut, [cut_sems], (inputs,), hbm=1)

    hid_far = swapped(hid_far, "fsdp", far)
    hid = over_fsdp(hid + [hid_far[m] for m in range(fsdp - far)], far // 2)
    dkv = along_heads(dkv)
    give = swapped(give, "ctx", 1)
    (kv_grad,) = call(
        owner_kernel, [sds((rows, columns))], [pltpu.VMEM((KV_HEADS,) + block, jnp.bfloat16)],
        far_first(dkv), after=(give,))
    grads = over_fsdp([kv_grad] * fsdp, far)
    if teams == 1:
        share = (span // devices, columns)
        two = (2,) + share
        near_sums, far_sums, near_send, far_send = call(
            functools.partial(sides_kernel, fsdp), [sds(two, f32)] * 2 + [sds(two)] * 2,
            [pltpu.VMEM((devices,) + share, f32)], (*hid, *grads))
        formed = (near_sums,)
        dq = along_heads(call(pair_kernel, [sds(wide)] * KV_HEADS, [], (keep, give), after=formed))
        far_sums = call(pair_kernel, [sds(share)] * 2, [], (far_sums, swapped(far_send, "ctx", 1)))
        near_sums = call(
            pair_kernel, [sds(share, f32), sds(share)], [], (near_sums, swapped(near_send, "ctx", 1)), after=dq[1:2])
        own_sums, *sums = far_first(along_heads([*near_sums, *far_sums]))
        (weight_grads,) = call(own_total_kernel, [sds(share, f32)], [], (*sums, own_sums))
    else:
        formed = call(functools.partial(weight_kernel, fsdp), [sds((span, columns))], [], (*hid, *grads))
        dq = along_heads(call(pair_kernel, [sds(wide)] * KV_HEADS, [], (keep, give), after=formed))
        sums = lax.all_to_all(formed[0].reshape(devices, span // devices, columns), "ctx", 0, 0, tiled=True)
        (weight_grads,) = call(total_kernel, [sds((span // devices, columns), f32)], [], (sums,))
    (query_grads,) = call(query_kernel, [sds((rows, Q_HEADS * HEAD_DIM))], [], far_first(dq), after=formed)
    (input_grads,) = call(
        functools.partial(input_kernel, fsdp), [sds((rows, model))], [], (kv_grad, *w_parts), after=formed)
    return query_grads[None], input_grads[None], weight_grads


def solution(mesh):
    return jax.shard_map(
        shards,
        mesh=mesh,
        in_specs=(
            P("fsdp", "ctx", None),
            P("fsdp", "ctx", None),
            P("fsdp", "ctx", None),
            P("fsdp", "ctx", None),
            P("fsdp", None, "ctx"),
            P("fsdp", None),
            P("fsdp", None),
        ),
        out_specs=(P("fsdp", "ctx", None), P("fsdp", "ctx", None), P(("fsdp", "ctx"), None)),
        check_vma=False,
    )
```

```python
import functools

import jax
import jax.numpy as jnp
from jax import lax
from jax.experimental import pallas as pl
from jax.experimental.pallas import tpu as pltpu
from jax.sharding import PartitionSpec as P

Q_HEADS = 16
KV_HEADS = 4
HEAD_DIM = 64
GROUPS = Q_HEADS // KV_HEADS
KEY_WIDTH = KV_HEADS * HEAD_DIM
PAIR = 2 * HEAD_DIM
TEAM = 2 * KV_HEADS
PAIRS = GROUPS // 2
GROUP = GROUPS * HEAD_DIM
SCALE = HEAD_DIM ** -0.5
LOWER = HEAD_DIM

NT = (((1,), (1,)), ((), ()))
TN = (((0,), (0,)), ((), ()))
VMEM = pl.BlockSpec(memory_space=pltpu.VMEM)
SMEM = pl.BlockSpec(memory_space=pltpu.SMEM)
ANY = pl.BlockSpec(memory_space=pl.ANY)
HBM = pl.BlockSpec(memory_space=pltpu.HBM)
PARAMS = pltpu.CompilerParams(vmem_limit_bytes=40 * 1024 * 1024)
WHOLE = pltpu.CompilerParams(vmem_limit_bytes=60 * 1024 * 1024)


def matmul(left, right, dims=(((1,), (0,)), ((), ()))):
    return lax.dot_general(left, right, dims, preferred_element_type=jnp.float32)


def swapped(array, axis, bits):
    size = lax.axis_size(axis)
    return lax.ppermute(array, axis, [(i, i ^ bits) for i in range(size)])


def call(kernel, out_shape, scratch, args, smem=0, hbm=0, after=()):
    given = len(args)
    params = WHOLE if hbm == given else PARAMS

    def body(*refs):
        kernel(*refs[:given], *refs[given + len(after):])

    specs = [SMEM] * smem + [HBM] * hbm + [VMEM] * (given - smem - hbm) + [ANY] * len(after)
    return pl.pallas_call(
        body,
        out_shape=out_shape,
        in_specs=specs,
        out_specs=[VMEM] * len(out_shape),
        scratch_shapes=scratch,
        compiler_params=params,
    )(*args, *after)


def held(array, after):
    def body(*refs):
        pass

    return pl.pallas_call(
        body,
        out_shape=sds(array.shape, array.dtype),
        in_specs=[ANY] * (1 + len(after)),
        out_specs=ANY,
        input_output_aliases={0: 0},
        compiler_params=PARAMS,
    )(array, *after)


def sds(shape, dtype=jnp.bfloat16):
    return jax.ShapeDtypeStruct(shape, dtype)


def head_side():
    me = lax.rem(lax.axis_index("ctx"), TEAM)
    return me // 2, lax.rem(me, 2)


def far_first(arrays):
    return [arrays[m] for m in (0, 2, 3, 1)]


def by_head(refs):
    return [refs[i] for i in (0, 3, 1, 2)]


def split(exact):
    first = exact.astype(jnp.bfloat16).astype(jnp.float32)
    second = (exact - first).astype(jnp.bfloat16).astype(jnp.float32)
    return first, second, exact - first - second


def pieces_kernel(q_ref, go_ref, ao_ref, lse_ref, *rest):
    out_refs, (grad, output, lse, stat, sems) = rest[:KV_HEADS], rest[KV_HEADS:]
    rows, width = q_ref.shape
    head, _ = head_side()
    loads = [pltpu.make_async_copy(ref, to, sems.at[i])
             for i, (ref, to) in enumerate(((go_ref, grad), (ao_ref, output), (lse_ref, lse)))]
    columns = [pl.ds(pl.multiple_of(jnp.bitwise_xor(head, m) * GROUP, GROUP), GROUP) for m in range(KV_HEADS)]
    moves = [pltpu.make_async_copy(q_ref.at[:, columns[m]], out_refs[m].at[0:rows, 0:GROUP], sems.at[3 + m])
             for m in range(KV_HEADS)]
    for copy in loads + moves:
        copy.start()
    for copy in loads:
        copy.wait()
    product = grad[...].astype(jnp.float32) * output[...].astype(jnp.float32)
    high = product.astype(jnp.bfloat16)
    low = (product - high.astype(jnp.float32)).astype(jnp.bfloat16)
    head_of = lax.broadcasted_iota(jnp.int32, (Q_HEADS, width), 1) // HEAD_DIM
    ones = (head_of == lax.broadcasted_iota(jnp.int32, (Q_HEADS, width), 0)).astype(jnp.bfloat16)
    delta = matmul(ones, high, NT) + matmul(ones, low, NT)
    for g in range(KV_HEADS):
        part = slice(g * GROUPS, (g + 1) * GROUPS)
        stat[g] = jnp.concatenate([lse[part, :], delta[part, :]], axis=0)
    zero = jnp.zeros((2 * GROUPS, rows), jnp.float32)
    for m in range(KV_HEADS):
        out_refs[m][0:rows, GROUP:] = grad[:, columns[m]]
        lines = [*split(stat[jnp.bitwise_xor(head, m)]), zero]
        for i, one in enumerate(lines):
            full = jnp.concatenate([one, zero], axis=0).astype(jnp.bfloat16)
            out_refs[m][rows:, i * rows:(i + 1) * rows] = full
    for copy in moves:
        copy.wait()


def hidden_moves(hid_ref, near_refs, far_ref, sems):
    mine = lax.axis_index("fsdp")
    near = len(near_refs)
    span = far_ref.shape[2]
    copies = []
    for m in range(near + far_ref.shape[0]):
        columns = pl.ds(pl.multiple_of(jnp.bitwise_xor(mine, m) * span, span), span)
        to = near_refs[m] if m < near else far_ref.at[m - near]
        copies.append(pltpu.make_async_copy(hid_ref.at[:, columns], to, sems.at[m]))
    for copy in copies:
        copy.start()
    return copies


def hidden_kernel(hid_ref, *rest):
    for copy in hidden_moves(hid_ref, rest[:-2], *rest[-2:]):
        copy.wait()


def project_kernel(fsdp, hid_ref, *rest):
    w_refs, out_refs, (parts,) = rest[:fsdp], rest[fsdp:fsdp + KV_HEADS], rest[fsdp + KV_HEADS:]
    mine = lax.axis_index("fsdp")
    head, _ = head_side()
    span = w_refs[0].shape[0]
    total = None
    for m in range(fsdp):
        start = pl.multiple_of(jnp.bitwise_xor(mine, m) * span, span)
        term = matmul(hid_ref[:, pl.ds(start, span)], w_refs[m][...])
        total = term if total is None else total + term
    low = total.astype(jnp.bfloat16)
    for g in range(KV_HEADS):
        key = low[:, g * HEAD_DIM:(g + 1) * HEAD_DIM]
        value = low[:, KEY_WIDTH + g * HEAD_DIM:KEY_WIDTH + (g + 1) * HEAD_DIM]
        parts[g] = jnp.concatenate([key, value], axis=1)
    for m in range(KV_HEADS):
        out_refs[m][...] = parts[jnp.bitwise_xor(head, m)]


def lower_half(shape):
    return lax.broadcasted_iota(jnp.int32, shape, len(shape) - 1) < LOWER


def stacked(key_value):
    wide = key_value.astype(jnp.float32)
    turned = pltpu.roll(wide, LOWER, 1)
    lower = lower_half(wide.shape)
    zero = jnp.zeros_like(wide)
    keys = jnp.concatenate([jnp.where(lower, wide, zero), jnp.where(lower, zero, turned)], axis=0) * SCALE
    values = jnp.concatenate([jnp.where(lower, turned, zero), jnp.where(lower, zero, wide)], axis=0)
    return keys.astype(jnp.bfloat16), values.astype(jnp.bfloat16)


def tile(keys, values, query, grad, stats, mask):
    size, edge = keys.shape[0] // 2, mask.shape[1]
    pairs = len(stats)
    width = query.shape[0] // pairs
    scores = matmul(keys, query, NT)
    prob_grad = matmul(values, grad, NT)
    lows, grads = [], []
    for head in range(2):
        part = slice(head * size, (head + 1) * size)
        lse = jnp.concatenate([lines[head] for lines in stats], axis=1)
        delta = jnp.concatenate([lines[2 + head] for lines in stats], axis=1)
        probs = jnp.exp(scores[part] - lse)
        pieces = []
        for first in range(0, pairs * width, width):
            pieces.append(jnp.where(mask, probs[:, first:first + edge], 0.0))
            if edge < width:
                pieces.append(probs[:, first + edge:first + width])
        probs = jnp.concatenate(pieces, axis=1)
        lows.append(probs.astype(jnp.bfloat16))
        grads.append((probs * (prob_grad[part] - delta)).astype(jnp.bfloat16))
    low, score_grad = jnp.concatenate(lows, axis=0), jnp.concatenate(grads, axis=0)
    return matmul(score_grad, query), matmul(low, grad), matmul(score_grad, keys, TN)


def folded(key_sum, value_sum):
    size = key_sum.shape[0] // 2
    lower = lower_half((size, PAIR))
    straight = jnp.where(lower, key_sum[:size], value_sum[size:])
    crossed = jnp.where(lower, value_sum[:size], key_sum[size:])
    return (straight + pltpu.roll(crossed, LOWER, 1)) * jnp.where(lower, SCALE, 1.0)


def unpacked(part, rows):
    exact = part[rows:, 0:3 * rows].astype(jnp.float32)[0:2 * GROUPS]
    return exact[:, 0:rows] + exact[:, rows:2 * rows] + exact[:, 2 * rows:]


def pair_stats(stat, pair):
    first = 2 * pair
    return [stat[first:first + 1], stat[first + 1:first + 2],
            stat[GROUPS + first:GROUPS + first + 1], stat[GROUPS + first + 1:GROUPS + first + 2]]


def sequence_kernel(near_parts, order_ref, hid_ref, *rest):
    qd_refs, kv_refs, rest = rest[:TEAM], rest[TEAM:TEAM + KV_HEADS], rest[TEAM + KV_HEADS:]
    dkv_refs, keep_ref, send_ref, rest = rest[:KV_HEADS], rest[KV_HEADS], rest[KV_HEADS + 1], rest[KV_HEADS + 2:]
    near_refs, far_ref, rest = rest[:near_parts], rest[near_parts], rest[near_parts + 1:]
    q_all, go_all, stat_all, key_all, value_all, dq_all, dkv_all, sems = rest
    moves = hidden_moves(hid_ref, near_refs, far_ref, sems)
    rows = kv_refs[0].shape[0]
    head, side = head_side()
    near = [order_ref[0, 2 * jnp.bitwise_xor(head, m) + side] for m in range(KV_HEADS)]
    far = [order_ref[0, 2 * jnp.bitwise_xor(head, m) + 1 - side] for m in range(KV_HEADS)]
    for place, ref in zip(near + far, by_head(qd_refs[:KV_HEADS]) + list(qd_refs[KV_HEADS:])):
        for pair in range(PAIRS):
            q_all[pair, place] = ref[0:rows, pair * PAIR:(pair + 1) * PAIR]
            go_all[pair, place] = ref[0:rows, GROUP + pair * PAIR:GROUP + (pair + 1) * PAIR]
        stat_all[place] = unpacked(ref, rows)
    for place, ref in zip(near, by_head(kv_refs)):
        key_all[place], value_all[place] = stacked(ref[...])
    dq_all[...] = jnp.zeros_like(dq_all)
    for block in range(TEAM):
        mine = functools.reduce(jnp.logical_or, [place == block for place in near])

        @pl.when(mine)
        def _():
            count = TEAM - block
            shape = (rows, rows)
            mask = lax.broadcasted_iota(jnp.int32, shape, 0) <= lax.broadcasted_iota(jnp.int32, shape, 1)
            stats = jnp.concatenate([stat_all[i] for i in range(block, TEAM)], axis=1)
            query = q_all[:, block:].reshape(PAIRS * count * rows, PAIR)
            grad = go_all[:, block:].reshape(PAIRS * count * rows, PAIR)
            key_sum, value_sum, query_part = tile(
                key_all[block], value_all[block], query, grad, [pair_stats(stats, pair) for pair in range(PAIRS)], mask)
            dq_all[:, block:] += query_part.reshape(PAIRS, count, rows, PAIR)
            dkv_all[block] = folded(key_sum, value_sum)

    for m in range(KV_HEADS):
        dkv_refs[m][...] = dkv_all[near[m]].astype(jnp.bfloat16)
        for pair in range(PAIRS):
            columns = slice(pair * PAIR, (pair + 1) * PAIR)
            keep_ref[m, :, columns] = dq_all[pair, near[m]]
            send_ref[m, :, columns] = dq_all[pair, far[m]].astype(jnp.bfloat16)
    for copy in moves:
        copy.wait()


def teams_kernel(order_ref, qd_ref, kv_ref, dkv_ref, keep_ref, send_ref, dq_all):
    rows = kv_ref.shape[1]
    head, side = head_side()
    base = lax.axis_index("ctx") // TEAM * TEAM
    dq_all[...] = jnp.zeros_like(dq_all)

    @pl.loop(0, kv_ref.shape[0])
    def _(block):
        keys, values = stacked(kv_ref[block])
        dkv_ref[block] = jnp.zeros((rows, PAIR), jnp.float32)
        stored = block // KV_HEADS * TEAM + 2 * jnp.bitwise_xor(head, lax.rem(block, KV_HEADS)) + side
        place = order_ref[0, stored]

        @pl.loop(0, TEAM)
        def _(at):
            turned = jnp.where(at < KV_HEADS, side, 1 - side)
            own = order_ref[0, base + 2 * jnp.bitwise_xor(head, lax.rem(at, KV_HEADS)) + turned]

            @pl.when(place <= own)
            def _():
                shape = (rows, rows)
                mask = (place * rows + lax.broadcasted_iota(jnp.int32, shape, 0)
                        <= own * rows + lax.broadcasted_iota(jnp.int32, shape, 1))
                one = qd_ref.at[at]
                stats = unpacked(one, rows)
                for pair in range(PAIRS):
                    first = pair * PAIR
                    key_part, value_part, query_part = tile(
                        keys, values, one[0:rows, first:first + PAIR], one[0:rows, GROUP + first:GROUP + first + PAIR],
                        [pair_stats(stats, pair)], mask)
                    dq_all[at, :, first:first + PAIR] += query_part
                    dkv_ref[block] += folded(key_part, value_part)

    keep_ref[...] = dq_all[0:KV_HEADS]
    send_ref[...] = dq_all[KV_HEADS:].astype(jnp.bfloat16)


def owner_kernel(*rest):
    dkv_refs, out_ref, parts = rest[:KV_HEADS], rest[KV_HEADS], rest[KV_HEADS + 1]
    head, _ = head_side()
    for m, ref in enumerate(by_head(dkv_refs)):
        parts[jnp.bitwise_xor(head, m)] = ref[...]
    keys = [parts[g, :, :HEAD_DIM] for g in range(KV_HEADS)]
    values = [parts[g, :, HEAD_DIM:] for g in range(KV_HEADS)]
    out_ref[...] = jnp.concatenate(keys + values, axis=1)


def pair_kernel(keep_ref, got_ref, *out_refs):
    for m, ref in enumerate(out_refs):
        ref[...] = (keep_ref[m] + got_ref[m].astype(jnp.float32)).astype(ref.dtype)


def query_kernel(*rest):
    dq_refs, out_ref = rest[:KV_HEADS], rest[KV_HEADS]
    head, _ = head_side()
    for m, ref in enumerate(by_head(dq_refs)):
        columns = pl.ds(pl.multiple_of(jnp.bitwise_xor(head, m) * GROUP, GROUP), GROUP)
        out_ref[:, columns] = ref[...]


def input_kernel(fsdp, grad_ref, *rest):
    w_refs, out_ref = rest[:fsdp], rest[fsdp]
    mine = lax.axis_index("fsdp")
    span = w_refs[0].shape[0]
    for m in range(fsdp):
        start = pl.multiple_of(jnp.bitwise_xor(mine, m) * span, span)
        out_ref[:, pl.ds(start, span)] = matmul(grad_ref[...], w_refs[m][...], NT).astype(jnp.bfloat16)


def weight_sums(fsdp, refs):
    hid = jnp.concatenate([ref[...] for ref in refs[:fsdp]], axis=0)
    grad = jnp.concatenate([ref[...] for ref in refs[fsdp:2 * fsdp]], axis=0)
    return matmul(hid, grad, TN)


def weight_kernel(fsdp, *rest):
    rest[2 * fsdp][...] = weight_sums(fsdp, rest).astype(jnp.bfloat16)


def sides_kernel(fsdp, *rest):
    keep_refs, send_refs, parts = rest[2 * fsdp:2 * fsdp + 2], rest[2 * fsdp + 2:2 * fsdp + 4], rest[-1]
    head, side = head_side()
    parts[...] = weight_sums(fsdp, rest).reshape(parts.shape)
    for m in range(KV_HEADS):
        to = 2 * jnp.bitwise_xor(head, m)
        keep_refs[m // 2][m % 2] = parts[to + side]
        send_refs[m // 2][m % 2] = parts[to + 1 - side].astype(jnp.bfloat16)


def own_total_kernel(*rest):
    part_refs, own_ref, out_ref = rest[:-2], rest[-2], rest[-1]
    total = own_ref[...]
    for ref in part_refs:
        total = total + ref[...].astype(jnp.float32)
    out_ref[...] = total


def total_kernel(part_ref, out_ref):
    total = part_ref[0].astype(jnp.float32)
    for i in range(1, part_ref.shape[0]):
        total = total + part_ref[i].astype(jnp.float32)
    out_ref[...] = total


def over_fsdp(own, bits):
    got = list(own)
    while bits:
        for m in range(len(own)):
            if m & bits:
                got[m] = swapped(got[m], "fsdp", bits)
        bits //= 2
    return got


def shards(hidden, queries, attn_out, grad_out, log_sums, block_order, w_kv):
    rows, model = hidden.shape[1:]
    fsdp, devices = lax.axis_size("fsdp"), lax.axis_size("ctx")
    teams = devices // TEAM
    f32 = jnp.float32
    span = model // fsdp
    inputs = hidden[0]
    columns = 2 * KEY_WIDTH
    block, wide = (rows, PAIR), (rows, GROUP)

    def along_heads(arrays):
        return [arrays[0]] + [swapped(arrays[m], "ctx", 2 * m) for m in range(1, KV_HEADS)]

    far = fsdp // 2
    qd = call(
        pieces_kernel, [sds((rows + 16, 2 * GROUP))] * KV_HEADS,
        [pltpu.VMEM((rows, Q_HEADS * HEAD_DIM), jnp.bfloat16)] * 2
        + [pltpu.VMEM((Q_HEADS, rows), f32), pltpu.VMEM((KV_HEADS, 2 * GROUPS, rows), f32),
           pltpu.SemaphoreType.DMA((3 + KV_HEADS,))],
        (queries[0], grad_out[0], attn_out[0], log_sums[0]), hbm=4)
    qd = along_heads(qd)
    turned = [swapped(one, "ctx", 1) for one in qd[:2]]
    w_far = held(swapped(w_kv, "fsdp", far), (*far_first(qd[:KV_HEADS])[1:], *turned))
    w_parts = over_fsdp([w_kv] * far + [w_far] * (fsdp - far), far // 2)

    kv = call(
        functools.partial(project_kernel, fsdp), [sds(block)] * KV_HEADS,
        [pltpu.VMEM((KV_HEADS,) + block, jnp.bfloat16)], (inputs, *w_parts))
    kv = along_heads(kv)
    qd = qd + turned + [swapped(one, "ctx", 1) for one in qd[2:]]

    half = (KV_HEADS,) + wide
    cut = [sds((rows, span))] * far + [sds((fsdp - far, rows, span))]
    cut_sems = pltpu.SemaphoreType.DMA((fsdp,))
    if teams == 1:
        outs = call(
            functools.partial(sequence_kernel, far), [sds(block)] * KV_HEADS + [sds(half, f32), sds(half)] + cut,
            [pltpu.VMEM((PAIRS, TEAM) + block, jnp.bfloat16)] * 2 + [pltpu.VMEM((TEAM, 2 * GROUPS, rows), f32)]
            + [pltpu.VMEM((TEAM, 2 * rows, PAIR), jnp.bfloat16)] * 2
            + [pltpu.VMEM((PAIRS, TEAM) + block, f32), pltpu.VMEM((TEAM,) + block, f32), cut_sems],
            (block_order, inputs, *far_first(qd[:KV_HEADS]), *qd[KV_HEADS:], *far_first(kv)), smem=1, hbm=1)
        dkv, (keep, give, *hid, hid_far) = outs[:KV_HEADS], outs[KV_HEADS:]
    else:
        alike = [[t * TEAM + i for t in range(teams)] for i in range(TEAM)]
        kv = lax.all_gather(jnp.stack(kv), "ctx", axis_index_groups=alike, axis=0, tiled=True)
        dkv, keep, give = call(
            teams_kernel, [sds((teams * KV_HEADS,) + block, f32), sds(half, f32), sds(half)],
            [pltpu.VMEM((TEAM,) + wide, f32)], (block_order, jnp.stack(qd), kv), smem=1)
        dkv = lax.psum_scatter(dkv, "ctx", axis_index_groups=alike, scatter_dimension=0, tiled=True)
        dkv = [dkv[m].astype(jnp.bfloat16) for m in range(KV_HEADS)]
        *hid, hid_far = call(hidden_kernel, cut, [cut_sems], (inputs,), hbm=1)

    hid_far = swapped(hid_far, "fsdp", far)
    hid = over_fsdp(hid + [hid_far[m] for m in range(fsdp - far)], far // 2)
    dkv = along_heads(dkv)
    give = swapped(give, "ctx", 1)
    (kv_grad,) = call(
        owner_kernel, [sds((rows, columns))], [pltpu.VMEM((KV_HEADS,) + block, jnp.bfloat16)],
        far_first(dkv), after=(give,))
    grads = over_fsdp([kv_grad] * fsdp, far)
    if teams == 1:
        share = (span // devices, columns)
        two = (2,) + share
        near_sums, far_sums, near_send, far_send = call(
            functools.partial(sides_kernel, fsdp), [sds(two, f32)] * 2 + [sds(two)] * 2,
            [pltpu.VMEM((devices,) + share, f32)], (*hid, *grads))
        formed = (near_sums,)
        dq = along_heads(call(pair_kernel, [sds(wide)] * KV_HEADS, [], (keep, give), after=formed))
        far_sums = call(pair_kernel, [sds(share)] * 2, [], (far_sums, swapped(far_send, "ctx", 1)))
        near_sums = call(
            pair_kernel, [sds(share, f32), sds(share)], [], (near_sums, swapped(near_send, "ctx", 1)), after=dq[2:3])
        own_sums, *sums = far_first(along_heads([*near_sums, *far_sums]))
        (weight_grads,) = call(own_total_kernel, [sds(share, f32)], [], (*sums, own_sums))
    else:
        formed = call(functools.partial(weight_kernel, fsdp), [sds((span, columns))], [], (*hid, *grads))
        dq = along_heads(call(pair_kernel, [sds(wide)] * KV_HEADS, [], (keep, give), after=formed))
        sums = lax.all_to_all(formed[0].reshape(devices, span // devices, columns), "ctx", 0, 0, tiled=True)
        (weight_grads,) = call(total_kernel, [sds((span // devices, columns), f32)], [], (sums,))
    (query_grads,) = call(query_kernel, [sds((rows, Q_HEADS * HEAD_DIM))], [], far_first(dq), after=formed)
    (input_grads,) = call(
        functools.partial(input_kernel, fsdp), [sds((rows, model))], [], (kv_grad, *w_parts), after=formed)
    return query_grads[None], input_grads[None], weight_grads


def solution(mesh):
    return jax.shard_map(
        shards,
        mesh=mesh,
        in_specs=(
            P("fsdp", "ctx", None),
            P("fsdp", "ctx", None),
            P("fsdp", "ctx", None),
            P("fsdp", "ctx", None),
            P("fsdp", None, "ctx"),
            P("fsdp", None),
            P("fsdp", None),
        ),
        out_specs=(P("fsdp", "ctx", None), P("fsdp", "ctx", None), P(("fsdp", "ctx"), None)),
        check_vma=False,
    )
```
